256 devices in a mesh: dp: 8 (over y_lo, x), fsdp: 32 (over y_hi, z, core).
Axes of the slice: x: 4, y: 4 (y_hi: 2, y_lo: 2; y = y_hi * 2 + y_lo), z: 8, core: 2. Of those that a mesh axis runs over, the one named last changes fastest.
Arguments:
- patches: bfloat16 [32768, 1280], P(('dp', 'fsdp')), may hold values from -6 to 6
- cotangent: bfloat16 [32768, 1280], P(('dp', 'fsdp')), may hold values from -24 to 24
- tile_counts: int32 [256], P(('dp', 'fsdp')), may hold values from 0 to 4, as said below
- ln_gain: float32 [1280], replicated, may hold values from 0.25 to 4
- qkv_weight: bfloat16 [1280, 1920], P('fsdp'), may hold values from -2 to 2
- out_weight: bfloat16 [640, 1280], P('fsdp'), may hold values from -0.25 to 0.25
- text_states: bfloat16 [1024, 8192], P('dp'), may hold values from -6 to 6
- mask_ids: int32 [1024], P('dp'), may hold values from 0 to 32
- text_lengths: int32 [8], P('dp'), may hold values from 1 to 128
- gate_value: float32 [1], replicated, may hold values from -1.5 to 1.5
- query_weight: bfloat16 [8192, 8192], P(None, 'fsdp'), may hold values from -1 to 1
- kv_weight: bfloat16 [1280, 2048], P('fsdp'), may hold values from -2 to 2
- output_weight: bfloat16 [8192, 8192], P('fsdp'), may hold values from -0.25 to 0.25
Outputs:
- grad_qkv: float32 [1280, 1920], P('fsdp')
- grad_out: float32 [640, 1280], P('fsdp')
- cross_out: bfloat16 [1024, 8192], P('dp', 'fsdp')
The draws below stay inside these ranges and needn't reach their ends.
Inputs may be any that keep to these rules, and one draw needn't show every extreme that they name: `tile_counts`: some image has 4 live tiles and some has none.
All inputs are finite; a program needn't handle non-finite values.
Results may differ from the reference program's by a relative error of at most 0.024.
The reference program's roundings to bfloat16 on the way count: a program that leaves them out, or rounds other values in their place, can miss the bound.
Values may be sent and summed in bfloat16 or wider, within the bound.
A program may use at most 128 MiB of HBM per device.

```python
import math
import jax
import jax.numpy as jnp
from jax import lax

ENC = 1280
EH = 8
EHD = 80
TILES = 4
PATCH = 32
TEXT = 128
D = 8192
HEADS = 64
HD = 128
KVH = 8
PATCH_ROWS = 32768
TEXT_ROWS = 1024
N_DP = 8
N_FSDP = 32
DEVICES = 256


def draw_tile_counts(key, part):
    key = jax.random.fold_in(key, 11)
    key_counts, key_spread, key_order = jax.random.split(key, 3)
    counts = jax.random.randint(key_counts, (DEVICES,), 0, TILES + 1)
    spread = jax.random.randint(key_spread, (DEVICES,), 0, 2)
    counts = counts * spread
    order = jax.random.permutation(key_order, DEVICES)
    counts = counts.at[order[0]].set(TILES)
    counts = counts.at[order[1]].set(0)
    return counts.astype(jnp.int32)


def draw_patches(key, part):
    key = jax.random.fold_in(key, 1)
    values = jax.random.truncated_normal(key, -6.0, 6.0, (PATCH_ROWS, ENC), jnp.float32)
    return values.astype(jnp.bfloat16)


def draw_qkv_weight(key, part):
    key = jax.random.fold_in(key, 2)
    columns = 3 * EH * EHD
    values = jax.random.truncated_normal(key, -6.0, 6.0, (ENC, columns), jnp.float32) * ENC ** (-0.5)
    return values.astype(jnp.bfloat16)


def draw_text_states(key, part):
    key = jax.random.fold_in(key, 3)
    values = jax.random.truncated_normal(key, -6.0, 6.0, (TEXT_ROWS, D), jnp.float32)
    return values.astype(jnp.bfloat16)


def draw_query_weight(key, part):
    key = jax.random.fold_in(key, 4)
    columns = HEADS * HD
    values = jax.random.truncated_normal(key, -6.0, 6.0, (D, columns), jnp.float32) * D ** (-0.5)
    return values.astype(jnp.bfloat16)


def draw_kv_weight(key, part):
    key = jax.random.fold_in(key, 5)
    columns = KVH * 2 * HD
    values = jax.random.truncated_normal(key, -6.0, 6.0, (ENC, columns), jnp.float32) * ENC ** (-0.5)
    return values.astype(jnp.bfloat16)


def plant(array, rng, least, high):
    shape = array.shape
    spot = [jax.random.randint(jax.random.fold_in(rng, axis), (), 0, shape[axis]) for axis in range(len(shape))]
    array = array.at[tuple(spot)].set(least)
    longest = shape.index(max(shape))
    spot[longest] = (spot[longest] + 1) % shape[longest]
    return array.at[tuple(spot)].set(high)


def spiked(values, own_key, source, target, shards_of, factor):
    def block_of(dim):
        return (jnp.arange(values.shape[dim]) // (values.shape[dim] // shards_of)).reshape((-1,) + (1,) * (values.ndim - 1 - dim))

    one_side = jax.random.permutation(own_key, shards_of)[block_of(target)]
    other_side = (block_of(target) + shards_of // 2) % shards_of
    return jnp.where((block_of(source) == one_side) | (block_of(source) == other_side), factor * values, values)


def levels(own_key, dims, shards, smallest, largest):
    loudness = 1.0
    for dim, parts in shards:
        steps = jax.random.uniform(jax.random.fold_in(jax.random.fold_in(own_key, 6), dim), (parts,), jnp.float32, smallest / len(shards), largest / len(shards))
        loudness = loudness * jnp.repeat(jnp.exp(steps), dims[dim] // parts).reshape((-1,) + (1,) * (len(dims) - 1 - dim))
    return loudness


def gaussian(rng, extent, scale, most, pieces=(), held_as=jnp.bfloat16):
    level = levels(rng, extent, pieces, -0.22, 0.18) if pieces else 1.0
    values = jax.random.normal(rng, extent, jnp.float32) * scale * level
    return jnp.minimum(jnp.maximum(values, -most), most).astype(held_as)


def noise_with(own_key, shape, width, reach, cuts, heavy, dtype=jnp.bfloat16):
    values = width * jax.random.normal(own_key, shape, jnp.float32)
    if cuts:
        values = values * levels(own_key, shape, cuts, -0.22, 0.18)
    return jnp.clip(spiked(values, jax.random.fold_in(own_key, 3), *heavy), -reach, reach).astype(dtype)


def setup_inputs(seed: int = 0) -> dict:
    key_of = jax.random.split(jax.random.key(seed), 14)
    patches = draw_patches(jax.random.fold_in(key_of[13], 71), 0)
    cotangent = noise_with(key_of[1], (PATCH_ROWS, ENC), 1.0, 24.0, ((0, 256),), (0, 1, 256, 6.0))
    tile_counts = draw_tile_counts(jax.random.fold_in(key_of[13], 71), 0)
    ln_gain = jnp.clip(jnp.exp(jax.random.uniform(key_of[3], (ENC,), jnp.float32, math.log(0.25), math.log(4.0))), 0.25, 4.0)
    qkv_weight = draw_qkv_weight(jax.random.fold_in(key_of[13], 71), 0)
    out_weight = gaussian(key_of[5], (EH * EHD, ENC), (EH * EHD) ** -0.5, 0.25, ((0, 32),))
    text_states = draw_text_states(jax.random.fold_in(key_of[13], 71), 0)
    mask_ids = plant(jax.random.randint(key_of[7], (TEXT_ROWS,), 0, N_FSDP + 1), jax.random.fold_in(key_of[7], 1), 0, N_FSDP).astype(jnp.int32)
    text_lengths = plant(jax.random.randint(key_of[8], (N_DP,), 1, TEXT + 1), jax.random.fold_in(key_of[8], 1), 1, TEXT).astype(jnp.int32)
    gate_value = jnp.clip(jax.random.uniform(key_of[9], (1,), jnp.float32, -1.5, 1.5), -1.5, 1.5)
    query_weight = draw_query_weight(jax.random.fold_in(key_of[13], 71), 0)
    kv_weight = draw_kv_weight(jax.random.fold_in(key_of[13], 71), 0)
    output_weight = gaussian(key_of[12], (HEADS * HD, D), (HEADS * HD // 16) ** -0.5, 0.25, ((0, 32),))
    return dict(patches=patches, cotangent=cotangent, tile_counts=tile_counts, ln_gain=ln_gain, qkv_weight=qkv_weight, out_weight=out_weight, text_states=text_states, mask_ids=mask_ids, text_lengths=text_lengths, gate_value=gate_value, query_weight=query_weight, kv_weight=kv_weight, output_weight=output_weight)


EPS = 1e-05
NEG = -1e+30

def encode(patch_piece, ln_gain, qkv_weight, out_weight, tile_count):
    row_count = patch_piece.shape[0]
    head_width = out_weight.shape[0]
    head_size = head_width // EH
    inputs_f = patch_piece.astype(jnp.float32)
    row_mean = lax.optimization_barrier(jnp.mean(inputs_f, axis=-1, keepdims=True))
    centred = inputs_f - row_mean
    spread = lax.optimization_barrier(jnp.mean(centred * centred, axis=-1, keepdims=True))
    normed = (centred * lax.rsqrt(spread + EPS) * ln_gain).astype(jnp.bfloat16)
    joined_qkv = jnp.dot(normed, qkv_weight, preferred_element_type=jnp.float32).astype(jnp.bfloat16)
    joined_qkv = joined_qkv.reshape(row_count, 3, EH, head_size)
    queries = joined_qkv[:, 0]
    key_rows = joined_qkv[:, 1]
    value_rows = joined_qkv[:, 2]
    live_rows = jnp.arange(row_count) // PATCH < tile_count
    scores = jnp.einsum('qhd,khd->hqk', queries.astype(jnp.float32), key_rows.astype(jnp.float32)) * head_size ** (-0.5)
    scores = jnp.where(live_rows[None, None, :], scores, NEG)
    row_top = lax.optimization_barrier(jnp.max(scores, axis=-1, keepdims=True))
    weights = jnp.exp(scores - row_top)
    attn_probs = weights / lax.optimization_barrier(jnp.sum(weights, axis=-1, keepdims=True))
    attn_low = attn_probs.astype(jnp.bfloat16)
    context = jnp.einsum('hqk,khd->qhd', attn_low.astype(jnp.float32), value_rows.astype(jnp.float32))
    context = context.astype(jnp.bfloat16).reshape(row_count, head_width)
    branch = jnp.dot(context, out_weight, preferred_element_type=jnp.float32)
    vision = jnp.where(live_rows[:, None], inputs_f + branch, 0.0).astype(jnp.bfloat16)
    return (vision, (normed, queries, key_rows, value_rows, attn_probs, attn_low, context, live_rows))

def encode_grads(saved, out_weight, cotangent):
    normed, queries, key_rows, value_rows, attn_probs, attn_low, context, live_rows = saved
    row_count, head_count, head_size = queries.shape
    upstream = jnp.where(live_rows[:, None], cotangent, jnp.zeros_like(cotangent))
    grad_out = jnp.dot(context.T, upstream, preferred_element_type=jnp.float32)
    grad_context = jnp.dot(upstream, out_weight.T, preferred_element_type=jnp.float32)
    grad_context = grad_context.astype(jnp.bfloat16).reshape(row_count, head_count, head_size)
    grad_probs = jnp.einsum('qhd,khd->hqk', grad_context.astype(jnp.float32), value_rows.astype(jnp.float32))
    grad_values = jnp.einsum('hqk,qhd->khd', attn_low.astype(jnp.float32), grad_context.astype(jnp.float32))
    inner_sum = lax.optimization_barrier(jnp.sum(attn_probs * grad_probs, axis=-1, keepdims=True))
    grad_scores = (attn_probs * (grad_probs - inner_sum) * head_size ** (-0.5)).astype(jnp.bfloat16)
    grad_queries = jnp.einsum('hqk,khd->qhd', grad_scores.astype(jnp.float32), key_rows.astype(jnp.float32))
    grad_keys = jnp.einsum('hqk,qhd->khd', grad_scores.astype(jnp.float32), queries.astype(jnp.float32))
    grad_joined = jnp.stack([grad_queries, grad_keys, grad_values], axis=1).astype(jnp.bfloat16)
    grad_joined = grad_joined.reshape(row_count, 3 * head_count * head_size)
    grad_qkv = jnp.dot(normed.T, grad_joined, preferred_element_type=jnp.float32)
    return (grad_qkv, grad_out)

def rounded_f(value_f):
    return lax.optimization_barrier(value_f.astype(jnp.bfloat16)).astype(jnp.float32)

def reference(patches, cotangent, tile_counts, ln_gain, qkv_weight, out_weight, text_states, mask_ids, text_lengths, gate_value, query_weight, kv_weight, output_weight):
    row_count = TILES * PATCH

    def device_step(totals, inputs):
        patch_piece, upstream, tile_count = inputs
        vision, saved = encode(patch_piece, ln_gain, qkv_weight, out_weight, tile_count)
        grad_qkv, grad_out = encode_grads(saved, out_weight, upstream)
        return ((totals[0] + rounded_f(grad_qkv), totals[1] + rounded_f(grad_out)), vision)
    zero_sums = (jnp.zeros(qkv_weight.shape, jnp.float32), jnp.zeros(out_weight.shape, jnp.float32))
    (sum_qkv, sum_out), vision_all = lax.scan(device_step, zero_sums, (patches.reshape(DEVICES, row_count, ENC), cotangent.reshape(DEVICES, row_count, ENC), tile_counts))
    key_total = N_FSDP * row_count
    group_heads = HEADS // KVH
    block_width = HEADS * HD // N_FSDP
    gate_tanh = jnp.tanh(gate_value[0])

    def group_step(inputs):
        rows_text, mask_row, text_len, features, counts = inputs
        kv_rows = jnp.dot(features, kv_weight, preferred_element_type=jnp.float32).astype(jnp.bfloat16)
        kv_rows = kv_rows.reshape(key_total, KVH, 2, HD)
        queries = jnp.dot(rows_text, query_weight, preferred_element_type=jnp.float32).astype(jnp.bfloat16)
        queries = queries.reshape(TEXT, KVH, group_heads, HD)
        position = jnp.arange(key_total)
        image_of = position // row_count
        tile_of = position % row_count // PATCH
        key_live = tile_of < jnp.repeat(counts, row_count)
        allowed = key_live[None, :] & (image_of[None, :] < mask_row[:, None])

        def head_step(head_index):
            q_block = queries[:, head_index].astype(jnp.float32)
            key_block = kv_rows[:, head_index, 0].astype(jnp.float32)
            value_block = kv_rows[:, head_index, 1].astype(jnp.float32)
            scores = jnp.einsum('tgd,kd->gtk', q_block, key_block) * HD ** (-0.5)
            scores = jnp.where(allowed[None], scores, NEG)
            row_top = lax.optimization_barrier(jnp.max(scores, axis=-1, keepdims=True))
            weights = jnp.exp(scores - row_top)
            attn_low = (weights / lax.optimization_barrier(jnp.sum(weights, axis=-1, keepdims=True))).astype(jnp.bfloat16)
            return jnp.einsum('gtk,kd->tgd', attn_low.astype(jnp.float32), value_block).astype(jnp.bfloat16)
        context = lax.map(head_step, jnp.arange(KVH))
        context = jnp.transpose(context, (1, 0, 2, 3)).reshape(TEXT, N_FSDP, block_width)
        blocks_out = output_weight.reshape(N_FSDP, block_width, D)

        def block_step(total, block_index):
            term = jnp.dot(context[:, block_index], blocks_out[block_index], preferred_element_type=jnp.float32)
            return (total + rounded_f(term), None)
        attended, unused = lax.scan(block_step, jnp.zeros((TEXT, D), jnp.float32), jnp.arange(N_FSDP))
        row_live = jnp.any(allowed, axis=-1) & (jnp.arange(TEXT) < text_len)
        result = rows_text.astype(jnp.float32) + gate_tanh * jnp.where(row_live[:, None], attended, 0.0)
        return result.astype(jnp.bfloat16)
    cross_out = lax.map(group_step, (text_states.reshape(N_DP, TEXT, D), mask_ids.reshape(N_DP, TEXT), text_lengths, vision_all.reshape(N_DP, key_total, ENC), tile_counts.reshape(N_DP, N_FSDP)))
    return (sum_qkv, sum_out, cross_out.reshape(N_DP * TEXT, D))
```

```python
import jax
import jax.numpy as jnp
from jax import lax
from jax.sharding import PartitionSpec as P
from jax.experimental import pallas as pl
from jax.experimental.pallas import tpu as pltpu

EH = 8
PATCH = 32
HD = 128
KVH = 8


EPS = 1e-05
NEG = -1e30


MESH = pl.DeviceIdType.MESH


def place():
    dp = lax.axis_index("dp")
    f = lax.axis_index("fsdp")
    x = lax.rem(dp, 4)
    y = (f // 16) * 2 + dp // 4
    z = lax.rem(f // 2, 8)
    return x, y, z, lax.rem(f, 2)


def device(x, y, z, core):
    return (lax.rem(y, 2) * 4 + x, (y // 2) * 16 + z * 2 + core)


def meet(peers):
    barrier = pltpu.get_barrier_semaphore()
    for peer in peers:
        pl.semaphore_signal(barrier, inc=1, device_id=peer, device_id_type=MESH)
    pl.semaphore_wait(barrier, len(peers))


def remote(src, dst, send_sem, recv_sem, peer):
    return pltpu.make_async_remote_copy(
        src_ref=src, dst_ref=dst, send_sem=send_sem, recv_sem=recv_sem,
        device_id=peer, device_id_type=MESH,
    )


def gather_kernel(a_ref, b_ref, a_full, b_full, local_sem, init_send, init_recv, z_send, z_recv,
                  near_send, near_recv, far_send, far_recv, core_send, core_recv):
    x, y, z, core = place()
    y_hi = y // 2
    partner = device(x, y, z, 1 - core)
    y_mirror = 3 - y
    spots = (y, x)
    mirror_spots = (y_mirror, x)
    shards = (a_ref, b_ref)
    fulls = (a_full, b_full)

    def along(t, step):
        if t == 0:
            return device(x, lax.rem(y + step + 4, 4), z, core)
        return device(lax.rem(x + step + 4, 4), y, z, core)

    def along_z(step):
        return device(x, y, lax.rem(z + step + 8, 8), core)

    meet([partner, device(x, y_mirror, z, 0), device(x, y_mirror, z, 1),
          along_z(1), along_z(-1), along(0, 1), along(0, -1), along(1, 1), along(1, -1)])

    def own_copy(t):
        return pltpu.make_async_copy(
            shards[t].at[spots[t]], fulls[t].at[spots[t], y_hi, z, core], local_sem.at[t])

    def to_partner(t):
        return remote(shards[t].at[spots[t]], fulls[t].at[spots[t], y_hi, z, core],
                      init_send.at[t, 0], init_recv.at[t, core], partner)

    def to_mirror(t):
        return remote(shards[t].at[mirror_spots[t]], fulls[t].at[mirror_spots[t], y_hi, z, core],
                      init_send.at[t, 1], init_recv.at[t, core], device(x, y_mirror, z, y_hi))

    def from_core(t, other):
        return remote(shards[t].at[spots[t]], fulls[t].at[spots[t], core, z, other],
                      init_send.at[t, 0], init_recv.at[t, other], partner)

    mine = core == y_hi
    for t in range(2):
        to_mirror(t).start()

        @pl.when(mine)
        def _(t=t):
            own_copy(t).start()

        @pl.when(jnp.logical_not(mine))
        def _(t=t):
            to_partner(t).start()

    signs = (1, -1)

    def unit_z(t, u):
        d = (u + 1) // 2 if u % 2 else -(u // 2)
        return lax.rem(z - signs[t] * d + 8, 8)

    def unit(t, spot, u):
        return fulls[t].at[spot, core, unit_z(t, u)]

    def pass_on(t, spot, u):
        src = unit(t, spot, u)
        return remote(src, src, core_send.at[t], core_recv.at[t], partner)

    def z_copy(t, u, u_next):
        src = unit(t, spots[t], u)
        step = signs[t] if u_next % 2 else -signs[t]
        return remote(src, src, z_send.at[t], z_recv.at[t, u_next], along_z(step))

    def near_copy(t, side, u):
        src = unit(t, spots[t], u)
        return remote(src, src, near_send.at[t], near_recv.at[t, side, u], along(t, 1 - 2 * side))

    def far_copy(t, side, u):
        spot = lax.rem(spots[t] + (3 if side == 0 else 1), 4)
        src = fulls[t].at[spot, core, unit_z(t, u), side]
        return remote(src, src, far_send.at[t], far_recv.at[t, side, u], along(t, 1 - 2 * side))

    def near_arrival(t, side, u):
        spot = lax.rem(spots[t] + (3 if side == 0 else 1), 4)
        dst = unit(t, spot, u)
        return remote(dst, dst, near_send.at[t], near_recv.at[t, side, u], partner)

    def far_arrival(t, side, u):
        spot = lax.rem(spots[t] + 2, 4)
        dst = fulls[t].at[spot, core, unit_z(t, u), side]
        return remote(dst, dst, far_send.at[t], far_recv.at[t, side, u], partner)

    for u in range(10):
        for t in range(2):
            if u < 8:
                if u == 0:
                    @pl.when(mine)
                    def _(t=t):
                        own_copy(t).wait()
                        from_core(t, 1 - core).wait_recv()

                    @pl.when(jnp.logical_not(mine))
                    def _(t=t):
                        from_core(t, 0).wait_recv()
                        from_core(t, 1).wait_recv()
                    z_copy(t, 0, 1).start()
                    z_copy(t, 0, 2).start()
                else:
                    z_copy(t, u, u).wait_recv()
                    if u + 2 < 8:
                        z_copy(t, u, u + 2).start()
                near_copy(t, 0, u).start()
                near_copy(t, 1, u).start()
                pass_on(t, spots[t], u).start()
        for t in range(2):
            if 1 <= u < 9:
                for side in range(2):
                    near_arrival(t, side, u - 1).wait_recv()
                    far_copy(t, side, u - 1).start()
                for side in range(2):
                    spot = lax.rem(spots[t] + (3 if side == 0 else 1), 4)
                    pass_on(t, spot, u - 1).start()
        for t in range(2):
            if 2 <= u:
                far_arrival(t, 0, u - 2).wait_recv()
                far_arrival(t, 1, u - 2).wait_recv()
                pass_on(t, lax.rem(spots[t] + 2, 4), u - 2).start()

    for t in range(2):
        to_mirror(t).wait_send()

        @pl.when(jnp.logical_not(mine))
        def _(t=t):
            to_partner(t).wait_send()
        seven = fulls[t].at[0, core, pl.ds(0, 7)]
        two = fulls[t].at[pl.ds(0, 2), core]
        one = fulls[t].at[0, core]
        every = fulls[t].at[:, 1 - core]
        remote(seven, seven, z_send.at[t], z_recv.at[t, 0], partner).wait_send()
        remote(two, two, near_send.at[t], near_recv.at[t, 0, 0], partner).wait_send()
        remote(one, one, far_send.at[t], far_recv.at[t, 0, 0], partner).wait_send()
        remote(every, every, core_send.at[t], core_recv.at[t], partner).wait()


def gather_weights(a, b):
    dma = pltpu.SemaphoreType.DMA
    any_space = pl.BlockSpec(memory_space=pl.ANY)
    return pl.pallas_call(
        gather_kernel,
        out_shape=(jax.ShapeDtypeStruct((4, 2, 8, 2) + a.shape[1:], a.dtype),
                   jax.ShapeDtypeStruct((4, 2, 8, 2) + b.shape[1:], b.dtype)),
        in_specs=[any_space] * 2,
        out_specs=[any_space] * 2,
        scratch_shapes=[
            dma((2,)), dma((2, 2)), dma((2, 2)), dma((2,)), dma((2, 8)),
            dma((2,)), dma((2, 2, 8)), dma((2,)), dma((2, 2, 8)), dma((2,)), dma((2,)),
        ],
        compiler_params=pltpu.CompilerParams(collective_id=0, has_side_effects=True),
        name="gather_weights",
    )(a, b)


def encode(patch_piece, ln_gain, qkv_weight, out_weight, tile_count):
    row_count = patch_piece.shape[0]
    head_width = out_weight.shape[0]
    head_size = head_width // EH
    inputs_f = patch_piece.astype(jnp.float32)
    row_mean = jnp.mean(inputs_f, axis=-1, keepdims=True)
    centred = inputs_f - row_mean
    spread = jnp.mean(centred * centred, axis=-1, keepdims=True)
    normed = (centred * lax.rsqrt(spread + EPS) * ln_gain).astype(jnp.bfloat16)
    queries, key_rows, value_rows = (
        jnp.dot(normed, qkv_weight[part], preferred_element_type=jnp.float32)
        .astype(jnp.bfloat16)
        .reshape(row_count, EH, head_size)
        for part in range(3)
    )
    live_rows = jnp.arange(row_count) // PATCH < tile_count
    scores = jnp.einsum(
        "qhd,khd->hqk", queries, key_rows, preferred_element_type=jnp.float32
    ) * head_size ** (-0.5)
    scores = jnp.where(live_rows[None, None, :], scores, NEG)
    row_top = jnp.max(scores, axis=-1, keepdims=True)
    weights = jnp.exp(scores - row_top)
    attn_probs = weights / jnp.sum(weights, axis=-1, keepdims=True)
    attn_low = attn_probs.astype(jnp.bfloat16)
    context = jnp.einsum("hqk,khd->qhd", attn_low, value_rows, preferred_element_type=jnp.float32)
    context = context.astype(jnp.bfloat16).reshape(row_count, head_width)
    branch = jnp.dot(context, out_weight, preferred_element_type=jnp.float32)
    vision = jnp.where(live_rows[:, None], inputs_f + branch, 0.0).astype(jnp.bfloat16)
    return (
        vision,
        (normed, queries, key_rows, value_rows, attn_probs, attn_low, context, live_rows),
    )


def encode_grads(saved, out_weight, cotangent):
    normed, queries, key_rows, value_rows, attn_probs, attn_low, context, live_rows = saved
    row_count, head_count, head_size = queries.shape
    upstream = jnp.where(live_rows[:, None], cotangent, jnp.zeros_like(cotangent))
    grad_out = lax.dot_general(
        context, upstream, (((0,), (0,)), ((), ())), preferred_element_type=jnp.float32
    )
    grad_context = lax.dot_general(
        upstream, out_weight, (((1,), (1,)), ((), ())), preferred_element_type=jnp.float32
    )
    grad_context = grad_context.astype(jnp.bfloat16).reshape(row_count, head_count, head_size)
    grad_probs = jnp.einsum(
        "qhd,khd->hqk", grad_context, value_rows, preferred_element_type=jnp.float32
    )
    grad_values = jnp.einsum(
        "hqk,qhd->khd", attn_low, grad_context, preferred_element_type=jnp.float32
    )
    inner_sum = jnp.sum(attn_probs * grad_probs, axis=-1, keepdims=True)
    grad_scores = (attn_probs * (grad_probs - inner_sum) * head_size ** (-0.5)).astype(jnp.bfloat16)
    grad_queries = jnp.einsum(
        "hqk,khd->qhd", grad_scores, key_rows, preferred_element_type=jnp.float32
    )
    grad_keys = jnp.einsum("hqk,qhd->khd", grad_scores, queries, preferred_element_type=jnp.float32)
    grad_joined = jnp.stack([grad_queries, grad_keys, grad_values], axis=1).astype(jnp.bfloat16)
    grad_joined = grad_joined.reshape(row_count, 3 * head_count * head_size)
    grad_qkv = lax.dot_general(
        normed, grad_joined, (((0,), (0,)), ((), ())), preferred_element_type=jnp.float32
    )
    return (grad_qkv, grad_out)


def per_device(
    patches,
    cotangent,
    tile_counts,
    ln_gain,
    qkv_weight,
    out_weight,
    text_states,
    mask_ids,
    text_lengths,
    gate_value,
    query_weight,
    kv_weight,
    output_weight,
):
    groups = lax.axis_size("fsdp")
    fsdp_index = lax.axis_index("fsdp")
    row_count = patches.shape[0]
    out_halves = jnp.transpose(out_weight.reshape(-1, 2, 640), (1, 0, 2)).reshape(-1, 640)
    joint = jnp.concatenate([qkv_weight, out_halves], axis=1)
    joint = jnp.transpose(joint.reshape(-1, 4, 640), (1, 0, 2))
    kv_parts = jnp.transpose(kv_weight.reshape(-1, 4, 512), (1, 0, 2))
    joint_full, kv_full = gather_weights(joint, kv_parts)
    joint_full = joint_full.reshape(4, 1280, 640)
    kv_full = kv_full.reshape(4, 1280, 512)
    full_out = joint_full[3].reshape(32, 2, 20, 640)
    full_out = jnp.transpose(full_out, (0, 2, 1, 3)).reshape(640, 1280)
    vision, saved = encode(patches, ln_gain, joint_full, full_out, tile_counts[0])
    grad_qkv, grad_out = encode_grads(saved, full_out, cotangent)
    shard_qkv, shard_out = (
        lax.psum_scatter(
            grad_qkv.astype(jnp.bfloat16), "fsdp", scatter_dimension=0, tiled=True
        ).astype(jnp.float32),
        lax.psum_scatter(
            grad_out.astype(jnp.bfloat16), "fsdp", scatter_dimension=0, tiled=True
        ).astype(jnp.float32),
    )
    sum_qkv, sum_out = lax.psum((shard_qkv, shard_out), "dp")
    counts_all = lax.all_gather(tile_counts, "fsdp", axis=0, tiled=True)
    key_total = groups * row_count
    local_kv = jnp.concatenate(
        [
            jnp.dot(vision, kv_full[part], preferred_element_type=jnp.float32).astype(jnp.bfloat16)
            for part in range(4)
        ],
        axis=1,
    )
    local_kv = jnp.transpose(local_kv.reshape(row_count, KVH, 2 * HD), (1, 0, 2))
    outgoing = jnp.repeat(local_kv, groups // KVH, axis=0)
    arrived = lax.all_to_all(outgoing, "fsdp", split_axis=0, concat_axis=1, tiled=True)
    keys_values = arrived.reshape(key_total, 2 * HD)
    key_block = keys_values[:, :HD]
    value_block = keys_values[:, HD:]
    text_count = text_states.shape[0]
    queries = jnp.dot(text_states, query_weight, preferred_element_type=jnp.float32).astype(
        jnp.bfloat16
    )
    queries = queries.reshape(text_count, -1, HD)
    position = jnp.arange(key_total)
    image_of = position // row_count
    tile_of = position % row_count // PATCH
    key_live = tile_of < jnp.repeat(counts_all, row_count)
    allowed = key_live[None, :] & (image_of[None, :] < mask_ids[:, None])
    scores = jnp.einsum(
        "thd,kd->htk", queries, key_block, preferred_element_type=jnp.float32
    ) * HD ** (-0.5)
    scores = jnp.where(allowed[None], scores, NEG)
    row_top = jnp.max(scores, axis=-1, keepdims=True)
    weights = jnp.exp(scores - row_top)
    attn_low = (weights / jnp.sum(weights, axis=-1, keepdims=True)).astype(jnp.bfloat16)
    context = jnp.einsum("htk,kd->thd", attn_low, value_block, preferred_element_type=jnp.float32)
    context = context.astype(jnp.bfloat16).reshape(text_count, -1)
    partial_out = jnp.dot(context, output_weight, preferred_element_type=jnp.float32)
    attended = lax.psum_scatter(
        partial_out.astype(jnp.bfloat16), "fsdp", scatter_dimension=1, tiled=True
    ).astype(jnp.float32)
    col_width = attended.shape[1]
    text_cols = lax.dynamic_slice_in_dim(text_states, fsdp_index * col_width, col_width, 1)
    row_live = jnp.any(allowed, axis=-1) & (jnp.arange(text_count) < text_lengths[0])
    gate_tanh = jnp.tanh(gate_value[0])
    result = text_cols.astype(jnp.float32) + gate_tanh * jnp.where(row_live[:, None], attended, 0.0)
    return (sum_qkv, sum_out, result.astype(jnp.bfloat16))


def solution(mesh):
    placed = (
        P(("dp", "fsdp"), None),
        P(("dp", "fsdp"), None),
        P(("dp", "fsdp")),
        P(),
        P("fsdp", None),
        P("fsdp", None),
        P("dp", None),
        P("dp"),
        P("dp"),
        P(),
        P(None, "fsdp"),
        P("fsdp", None),
        P("fsdp", None),
    )
    return jax.shard_map(
        per_device,
        mesh=mesh,
        in_specs=placed,
        out_specs=(P("fsdp", None), P("fsdp", None), P("dp", "fsdp")),
        check_vma=False,
    )
```

```python
import jax
import jax.numpy as jnp
from jax import lax
from jax.sharding import PartitionSpec as P
from jax.experimental import pallas as pl
from jax.experimental.pallas import tpu as pltpu

EH = 8
PATCH = 32
HD = 128
KVH = 8


EPS = 1e-05
NEG = -1e30


MESH = pl.DeviceIdType.MESH


def place():
    dp = lax.axis_index("dp")
    f = lax.axis_index("fsdp")
    x = lax.rem(dp, 4)
    y = (f // 16) * 2 + dp // 4
    z = lax.rem(f // 2, 8)
    return x, y, z, lax.rem(f, 2)


def device(x, y, z, core):
    return (lax.rem(y, 2) * 4 + x, (y // 2) * 16 + z * 2 + core)


def meet(peers):
    barrier = pltpu.get_barrier_semaphore()
    for peer in peers:
        pl.semaphore_signal(barrier, inc=1, device_id=peer, device_id_type=MESH)
    pl.semaphore_wait(barrier, len(peers))


def remote(src, dst, send_sem, recv_sem, peer):
    return pltpu.make_async_remote_copy(
        src_ref=src, dst_ref=dst, send_sem=send_sem, recv_sem=recv_sem,
        device_id=peer, device_id_type=MESH,
    )


def gather_kernel(a_ref, b_ref, a_full, b_full, local_sem, init_send, init_recv, z_send, z_recv,
                  near_send, near_recv, far_send, far_recv, core_send, core_recv):
    x, y, z, core = place()
    y_hi = y // 2
    partner = device(x, y, z, 1 - core)
    y_mirror = 3 - y
    spots = (y, x)
    mirror_spots = (y_mirror, x)
    shards = (a_ref, b_ref)
    fulls = (a_full, b_full)

    def along(t, step):
        if t == 0:
            return device(x, lax.rem(y + step + 4, 4), z, core)
        return device(lax.rem(x + step + 4, 4), y, z, core)

    def along_z(step):
        return device(x, y, lax.rem(z + step + 8, 8), core)

    meet([partner, device(x, y_mirror, z, 0), device(x, y_mirror, z, 1),
          along_z(1), along_z(-1), along(0, 1), along(0, -1), along(1, 1), along(1, -1)])

    def own_copy(t):
        return pltpu.make_async_copy(
            shards[t].at[spots[t]], fulls[t].at[spots[t], y_hi, z, core], local_sem.at[t])

    def to_partner(t):
        return remote(shards[t].at[spots[t]], fulls[t].at[spots[t], y_hi, z, core],
                      init_send.at[t, 0], init_recv.at[t, core], partner)

    def to_mirror(t):
        return remote(shards[t].at[mirror_spots[t]], fulls[t].at[mirror_spots[t], y_hi, z, core],
                      init_send.at[t, 1], init_recv.at[t, core], device(x, y_mirror, z, y_hi))

    def from_core(t, other):
        return remote(shards[t].at[spots[t]], fulls[t].at[spots[t], core, z, other],
                      init_send.at[t, 0], init_recv.at[t, other], partner)

    mine = core == y_hi
    for t in range(2):
        to_mirror(t).start()

        @pl.when(mine)
        def _(t=t):
            own_copy(t).start()

        @pl.when(jnp.logical_not(mine))
        def _(t=t):
            to_partner(t).start()

    signs = (1, -1)

    def unit_z(t, u):
        d = (u + 1) // 2 if u % 2 else -(u // 2)
        return lax.rem(z - signs[t] * d + 8, 8)

    def unit(t, spot, u):
        return fulls[t].at[spot, core, unit_z(t, u)]

    def pass_on(t, spot, u):
        src = unit(t, spot, u)
        return remote(src, src, core_send.at[t], core_recv.at[t], partner)

    def z_copy(t, u, u_next):
        src = unit(t, spots[t], u)
        step = signs[t] if u_next % 2 else -signs[t]
        return remote(src, src, z_send.at[t], z_recv.at[t, u_next], along_z(step))

    def near_copy(t, side, u):
        src = unit(t, spots[t], u)
        return remote(src, src, near_send.at[t], near_recv.at[t, side, u], along(t, 1 - 2 * side))

    def far_copy(t, side, u):
        spot = lax.rem(spots[t] + (3 if side == 0 else 1), 4)
        src = fulls[t].at[spot, core, unit_z(t, u), side]
        return remote(src, src, far_send.at[t], far_recv.at[t, side, u], along(t, 1 - 2 * side))

    def near_arrival(t, side, u):
        spot = lax.rem(spots[t] + (3 if side == 0 else 1), 4)
        dst = unit(t, spot, u)
        return remote(dst, dst, near_send.at[t], near_recv.at[t, side, u], partner)

    def far_arrival(t, side, u):
        spot = lax.rem(spots[t] + 2, 4)
        dst = fulls[t].at[spot, core, unit_z(t, u), side]
        return remote(dst, dst, far_send.at[t], far_recv.at[t, side, u], partner)

    for u in range(10):
        for t in range(2):
            if u < 8:
                if u == 0:
                    @pl.when(mine)
                    def _(t=t):
                        own_copy(t).wait()
                        from_core(t, 1 - core).wait_recv()

                    @pl.when(jnp.logical_not(mine))
                    def _(t=t):
                        from_core(t, 0).wait_recv()
                        from_core(t, 1).wait_recv()
                    z_copy(t, 0, 1).start()
                    z_copy(t, 0, 2).start()
                else:
                    z_copy(t, u, u).wait_recv()
                    if u + 2 < 8:
                        z_copy(t, u, u + 2).start()
                near_copy(t, 0, u).start()
                near_copy(t, 1, u).start()
                pass_on(t, spots[t], u).start()
        for t in range(2):
            if 1 <= u < 9:
                for side in range(2):
                    near_arrival(t, side, u - 1).wait_recv()
                    far_copy(t, side, u - 1).start()
                for side in range(2):
                    spot = lax.rem(spots[t] + (3 if side == 0 else 1), 4)
                    pass_on(t, spot, u - 1).start()
        for t in range(2):
            if 2 <= u:
                far_arrival(t, 0, u - 2).wait_recv()
                far_arrival(t, 1, u - 2).wait_recv()
                pass_on(t, lax.rem(spots[t] + 2, 4), u - 2).start()

    for t in range(2):
        to_mirror(t).wait_send()

        @pl.when(jnp.logical_not(mine))
        def _(t=t):
            to_partner(t).wait_send()
        seven = fulls[t].at[0, core, pl.ds(0, 7)]
        two = fulls[t].at[pl.ds(0, 2), core]
        one = fulls[t].at[0, core]
        every = fulls[t].at[:, 1 - core]
        remote(seven, seven, z_send.at[t], z_recv.at[t, 0], partner).wait_send()
        remote(two, two, near_send.at[t], near_recv.at[t, 0, 0], partner).wait_send()
        remote(one, one, far_send.at[t], far_recv.at[t, 0, 0], partner).wait_send()
        remote(every, every, core_send.at[t], core_recv.at[t], partner).wait()


def gather_weights(a, b):
    dma = pltpu.SemaphoreType.DMA
    any_space = pl.BlockSpec(memory_space=pl.ANY)
    return pl.pallas_call(
        gather_kernel,
        out_shape=(jax.ShapeDtypeStruct((4, 2, 8, 2) + a.shape[1:], a.dtype),
                   jax.ShapeDtypeStruct((4, 2, 8, 2) + b.shape[1:], b.dtype)),
        in_specs=[any_space] * 2,
        out_specs=[any_space] * 2,
        scratch_shapes=[
            dma((2,)), dma((2, 2)), dma((2, 2)), dma((2,)), dma((2, 8)),
            dma((2,)), dma((2, 2, 8)), dma((2,)), dma((2, 2, 8)), dma((2,)), dma((2,)),
        ],
        compiler_params=pltpu.CompilerParams(collective_id=0, has_side_effects=True),
        name="gather_weights",
    )(a, b)


def reduce_peers():
    x, y, z, core = place()
    peers = [device(x, y, z, 1 - core)]
    for step in range(1, 4):
        for other in range(2):
            peers.append(device(x, lax.rem(y + step, 4), z, other))
            peers.append(device(lax.rem(x + step, 4), y, z, other))
    for step in range(1, 8):
        peers.append(device(x, y, lax.rem(z + step, 8), core))
    return peers


def reduce_steps(grads, out, from_core, chip_sum, from_near, plane_sum, from_z, from_cross, total,
                 core_send, core_recv, near_send, near_recv, z_send, z_recv, cross_send, cross_recv,
                 last_send, last_recv):
    x, y, z, core = place()
    y_hi = y // 2
    partner = device(x, y, z, 1 - core)
    spots = (y, x)
    rows, width = out.shape[1:]

    def along(axis, step):
        if axis == 0:
            return device(x, lax.rem(y + step, 4), z, core)
        return device(lax.rem(x + step, 4), y, z, core)

    def part(v, d):
        return lax.rem(spots[v] + d, 4)

    def core_copy(v, d):
        return remote(grads.at[1 - core, v, part(v, d)], from_core.at[v, d],
                      core_send.at[v, d], core_recv.at[v, d], partner)

    def near_copy(v, d):
        return remote(chip_sum.at[v, d - 1], from_near.at[v, d - 1],
                      near_send.at[v, d - 1], near_recv.at[v, d - 1], along(v, d))

    def z_copy(v, d):
        return remote(plane_sum.at[v, lax.rem(z + d, 8)], from_z.at[v, d - 1],
                      z_send.at[v, d - 1], z_recv.at[v, d - 1], device(x, y, lax.rem(z + d, 8), core))

    def cross_copy(v, d):
        slot = spots[1 - v]
        return remote(from_cross.at[v, slot], from_cross.at[v, slot],
                      cross_send.at[v, d - 1], cross_recv.at[v, d - 1], along(1 - v, d))

    def cross_arrival(v, d):
        slot = lax.rem(spots[1 - v] + 4 - d, 4)
        return remote(from_cross.at[v, slot], from_cross.at[v, slot],
                      cross_send.at[v, d - 1], cross_recv.at[v, d - 1], partner)

    def last_copy(v, i):
        peer = device(x, 2 * core + i, z, 0) if v == 0 else device(i, y, z, 1)
        slot = spots[v]
        return remote(total.at[v], out.at[slot], last_send.at[v, i], last_recv.at[slot], peer)

    def last_self(v, i):
        if v == 0:
            return jnp.logical_and(2 * core + i == y, core == 0)
        return jnp.logical_and(i == x, core == 1)

    for d in (2, 1, 3, 0):
        for v in range(2):
            core_copy(v, d).start()
    yield
    for d in (2, 1, 3):
        for v in range(2):
            core_copy(v, d).wait_recv()

            def add(k, carry, v=v, d=d):
                chip_sum[v, d - 1, k] = (
                    grads[core, v, part(v, d), k].astype(jnp.float32)
                    + from_core[v, d, k].astype(jnp.float32)
                ).astype(jnp.bfloat16)
                return carry
            lax.fori_loop(0, 8, add, 0)
            near_copy(v, d).start()
        yield
    for v in range(2):
        core_copy(v, 0).wait_recv()
        for d in range(1, 4):
            near_copy(v, d).wait_recv()

        def add(k, carry, v=v):
            sums = (grads[core, v, spots[v], k].astype(jnp.float32)
                    + from_core[v, 0, k].astype(jnp.float32))
            for d in range(3):
                sums = sums + from_near[v, d, k].astype(jnp.float32)
            plane_sum[v, k] = sums.astype(jnp.bfloat16)
            return carry
        lax.fori_loop(0, 8, add, 0)
        for d in (4, 3, 5, 2, 6, 1, 7):
            z_copy(v, d).start()
        yield
    for v in range(2):
        for d in range(1, 8):
            z_copy(v, d).wait_recv()
        sums = plane_sum[v, z].astype(jnp.float32)
        for d in range(7):
            sums = sums + from_z[v, d].astype(jnp.float32)
        from_cross[v, spots[1 - v]] = sums
        for d in (2, 1, 3):
            cross_copy(v, d).start()
    yield
    for v in range(2):
        for d in range(1, 4):
            cross_arrival(v, d).wait_recv()
        total[v] = (from_cross[v, 0] + from_cross[v, 1]) + (from_cross[v, 2] + from_cross[v, 3])
        for i in range(2 if v == 0 else 4):
            active = True if v == 0 else y_hi == core

            @pl.when(jnp.logical_and(active, jnp.logical_not(last_self(v, i))))
            def _(v=v, i=i):
                last_copy(v, i).start()

            @pl.when(jnp.logical_and(active, last_self(v, i)))
            def _(v=v):
                out[spots[v]] = total[v]
    yield
    for j in range(4):
        skip = jnp.where(core == 0, jnp.logical_and(j == y, y_hi == 0),
                         jnp.logical_and(j == x, y_hi == 1))

        @pl.when(jnp.logical_not(skip))
        def _(j=j):
            remote(out.at[j], out.at[j], last_send.at[0, 0], last_recv.at[j], partner).wait_recv()
    for v in range(2):
        for d in range(4):
            core_copy(v, d).wait_send()
        for d in range(1, 4):
            near_copy(v, d).wait_send()
            cross_copy(v, d).wait_send()
        for d in range(1, 8):
            z_copy(v, d).wait_send()
        for i in range(2 if v == 0 else 4):
            active = True if v == 0 else y_hi == core

            @pl.when(jnp.logical_and(active, jnp.logical_not(last_self(v, i))))
            def _(v=v, i=i):
                last_copy(v, i).wait_send()


def reduce_scratch():
    dma = pltpu.SemaphoreType.DMA
    block = (40, 640)
    return [
        pltpu.VMEM((2, 4, 8) + block, jnp.bfloat16),
        pltpu.VMEM((2, 3, 8) + block, jnp.bfloat16),
        pltpu.VMEM((2, 3, 8) + block, jnp.bfloat16),
        pltpu.VMEM((2, 8) + block, jnp.bfloat16),
        pltpu.VMEM((2, 7) + block, jnp.bfloat16),
        pltpu.VMEM((2, 4) + block, jnp.float32),
        pltpu.VMEM((2,) + block, jnp.float32),
        dma((2, 4)), dma((2, 4)), dma((2, 3)), dma((2, 3)), dma((2, 7)), dma((2, 7)),
        dma((2, 3)), dma((2, 3)), dma((2, 4)), dma((4,)),
    ]


def reduce_kernel(grads, out, *scratch):
    meet(reduce_peers())
    for _ in reduce_steps(grads, out, *scratch):
        pass


def reduce_grads(grads):
    vmem = pl.BlockSpec(memory_space=pltpu.VMEM)
    return pl.pallas_call(
        reduce_kernel,
        out_shape=jax.ShapeDtypeStruct((4, 40, 640), jnp.float32),
        in_specs=[vmem],
        out_specs=vmem,
        scratch_shapes=reduce_scratch(),
        compiler_params=pltpu.CompilerParams(
            collective_id=1, has_side_effects=True, vmem_limit_bytes=56 * 2**20),
        name="reduce_grads",
    )(grads)


def attended_peers():
    x, y, z, core = place()
    peers = [device(x, y, z, 1 - core), device(x, lax.rem(y + 2, 4), z, core)]
    for step in range(1, 8):
        peers.append(device(x, y, lax.rem(z + step, 8), core))
    return peers


def attended_steps(partial, out, from_core, chip_sum, from_y, group_sum, from_z,
                   core_send, core_recv, y_send, y_recv, z_send, z_recv):
    x, y, z, core = place()
    y_hi = y // 2
    partner = device(x, y, z, 1 - core)
    across = device(x, lax.rem(y + 2, 4), z, core)
    order = (4, 3, 5, 2, 6, 1, 7, 0)

    def spot(d):
        return lax.rem(z + d, 8)

    def core_copy(half, d):
        row = y_hi if half else 1 - y_hi
        return remote(partial.at[row, spot(d), 1 - core], from_core.at[half, d],
                      core_send.at[half, d], core_recv.at[half, d], partner)

    def y_copy(d):
        return remote(chip_sum.at[d], from_y.at[d], y_send.at[d], y_recv.at[d], across)

    def z_copy(d):
        return remote(group_sum.at[d], from_z.at[d], z_send.at[d], z_recv.at[d],
                      device(x, y, spot(d), core))

    for half in range(2):
        for d in order:
            core_copy(half, d).start()
    yield
    for d in order:
        core_copy(0, d).wait_recv()
        chip_sum[d] = (partial[1 - y_hi, spot(d), core].astype(jnp.float32)
                       + from_core[0, d].astype(jnp.float32)).astype(jnp.bfloat16)
        y_copy(d).start()
    yield
    for d in order:
        core_copy(1, d).wait_recv()
        y_copy(d).wait_recv()
        sums = (partial[y_hi, spot(d), core].astype(jnp.float32)
                + from_core[1, d].astype(jnp.float32) + from_y[d].astype(jnp.float32))
        if d:
            group_sum[d] = sums.astype(jnp.bfloat16)
            z_copy(d).start()
        else:
            out[...] = sums
    yield
    sums = out[...]
    for d in range(1, 8):
        z_copy(d).wait_recv()
        sums = sums + from_z[d].astype(jnp.float32)
    out[...] = sums
    for d in range(8):
        core_copy(0, d).wait_send()
        core_copy(1, d).wait_send()
        y_copy(d).wait_send()
        if d:
            z_copy(d).wait_send()


def attended_scratch():
    dma = pltpu.SemaphoreType.DMA
    block = (128, 256)
    return [
        pltpu.VMEM((2, 8) + block, jnp.bfloat16),
        pltpu.VMEM((8,) + block, jnp.bfloat16),
        pltpu.VMEM((8,) + block, jnp.bfloat16),
        pltpu.VMEM((8,) + block, jnp.bfloat16),
        pltpu.VMEM((8,) + block, jnp.bfloat16),
        dma((2, 8)), dma((2, 8)), dma((8,)), dma((8,)), dma((8,)), dma((8,)),
    ]


def attended_kernel(partial, out, *scratch):
    meet(attended_peers())
    for _ in attended_steps(partial, out, *scratch):
        pass


def reduce_attended(partial):
    vmem = pl.BlockSpec(memory_space=pltpu.VMEM)
    return pl.pallas_call(
        attended_kernel,
        out_shape=jax.ShapeDtypeStruct((128, 256), jnp.float32),
        in_specs=[vmem],
        out_specs=vmem,
        scratch_shapes=attended_scratch(),
        compiler_params=pltpu.CompilerParams(
            collective_id=2, has_side_effects=True, vmem_limit_bytes=56 * 2**20),
        name="reduce_attended",
    )(partial)


def exchange_peers():
    x, y, z, core = place()
    peers = [device(x, y, z, 1 - core)]
    for step in range(8):
        for turn in range(2):
            if step or turn:
                peers.append(device(x, lax.rem(y + 2 * turn, 4), lax.rem(z + step, 8), core))
    return peers


ORDER = ((4, 1), (4, 0), (3, 1), (5, 1), (3, 0), (5, 0), (2, 1), (6, 1), (2, 0), (6, 0),
         (1, 1), (7, 1), (1, 0), (7, 0), (0, 1), (0, 0))


def exchange_steps(kv, arrived, local_sem, far_send, far_recv, core_send, core_recv):
    x, y, z, core = place()
    y_hi = y // 2
    partner = device(x, y, z, 1 - core)

    def far_copy(step, turn):
        to_y = lax.rem(y + 2 * turn, 4)
        to_z = lax.rem(z + step, 8)
        head = (to_y // 2) * 4 + to_z // 2
        return remote(kv.at[head], arrived.at[y_hi, z, core], far_send.at[step, turn],
                      far_recv.at[step, turn], device(x, to_y, to_z, core))

    def source(step, turn):
        return arrived.at[lax.rem(y_hi + turn, 2), lax.rem(z + 8 - step, 8), core]

    def pass_on(step, turn):
        src = source(step, turn)
        return remote(src, src, core_send.at[step, turn], core_recv.at[step, turn], partner)

    own = pltpu.make_async_copy(kv.at[y_hi * 4 + z // 2], arrived.at[y_hi, z, core], local_sem)
    own.start()
    for step, turn in ORDER:
        if step or turn:
            far_copy(step, turn).start()
    yield
    for step, turn in reversed(ORDER):
        if step or turn:
            src = source(step, turn)
            remote(src, src, far_send.at[step, turn], far_recv.at[step, turn], partner).wait_recv()
        else:
            own.wait()
        pass_on(step, turn).start()
    yield
    for step, turn in reversed(ORDER):
        dst = arrived.at[lax.rem(y_hi + turn, 2), lax.rem(z + 8 - step, 8), 1 - core]
        remote(dst, dst, core_send.at[step, turn], core_recv.at[step, turn], partner).wait_recv()
    for step, turn in ORDER:
        pass_on(step, turn).wait_send()
        if step or turn:
            far_copy(step, turn).wait_send()


def exchange_scratch():
    dma = pltpu.SemaphoreType.DMA
    return [dma(()), dma((8, 2)), dma((8, 2)), dma((8, 2)), dma((8, 2))]


def exchange_kernel(kv, arrived, *scratch):
    meet(exchange_peers())
    for _ in exchange_steps(kv, arrived, *scratch):
        pass


def exchange_kv(kv):
    vmem = pl.BlockSpec(memory_space=pltpu.VMEM)
    return pl.pallas_call(
        exchange_kernel,
        out_shape=jax.ShapeDtypeStruct((2, 8, 2) + kv.shape[1:], kv.dtype),
        in_specs=[vmem],
        out_specs=vmem,
        scratch_shapes=exchange_scratch(),
        compiler_params=pltpu.CompilerParams(
            collective_id=3, has_side_effects=True, vmem_limit_bytes=56 * 2**20),
        name="exchange_kv",
    )(kv)


def encode(patch_piece, ln_gain, qkv_weight, out_weight, tile_count):
    row_count = patch_piece.shape[0]
    head_width = out_weight.shape[0]
    head_size = head_width // EH
    inputs_f = patch_piece.astype(jnp.float32)
    row_mean = jnp.mean(inputs_f, axis=-1, keepdims=True)
    centred = inputs_f - row_mean
    spread = jnp.mean(centred * centred, axis=-1, keepdims=True)
    normed = (centred * lax.rsqrt(spread + EPS) * ln_gain).astype(jnp.bfloat16)
    queries, key_rows, value_rows = (
        jnp.dot(normed, qkv_weight[part], preferred_element_type=jnp.float32)
        .astype(jnp.bfloat16)
        .reshape(row_count, EH, head_size)
        for part in range(3)
    )
    live_rows = jnp.arange(row_count) // PATCH < tile_count
    scores = jnp.einsum(
        "qhd,khd->hqk", queries, key_rows, preferred_element_type=jnp.float32
    ) * head_size ** (-0.5)
    scores = jnp.where(live_rows[None, None, :], scores, NEG)
    row_top = jnp.max(scores, axis=-1, keepdims=True)
    weights = jnp.exp(scores - row_top)
    attn_probs = weights / jnp.sum(weights, axis=-1, keepdims=True)
    attn_low = attn_probs.astype(jnp.bfloat16)
    context = jnp.einsum("hqk,khd->qhd", attn_low, value_rows, preferred_element_type=jnp.float32)
    context = context.astype(jnp.bfloat16).reshape(row_count, head_width)
    branch = jnp.dot(context, out_weight, preferred_element_type=jnp.float32)
    vision = jnp.where(live_rows[:, None], inputs_f + branch, 0.0).astype(jnp.bfloat16)
    return (
        vision,
        (normed, queries, key_rows, value_rows, attn_probs, attn_low, context, live_rows),
    )


def encode_grads(saved, out_weight, cotangent):
    normed, queries, key_rows, value_rows, attn_probs, attn_low, context, live_rows = saved
    row_count, head_count, head_size = queries.shape
    upstream = jnp.where(live_rows[:, None], cotangent, jnp.zeros_like(cotangent))
    grad_out = lax.dot_general(
        context, upstream, (((0,), (0,)), ((), ())), preferred_element_type=jnp.float32
    )
    grad_context = lax.dot_general(
        upstream, out_weight, (((1,), (1,)), ((), ())), preferred_element_type=jnp.float32
    )
    grad_context = grad_context.astype(jnp.bfloat16).reshape(row_count, head_count, head_size)
    grad_probs = jnp.einsum(
        "qhd,khd->hqk", grad_context, value_rows, preferred_element_type=jnp.float32
    )
    grad_values = jnp.einsum(
        "hqk,qhd->khd", attn_low, grad_context, preferred_element_type=jnp.float32
    )
    inner_sum = jnp.sum(attn_probs * grad_probs, axis=-1, keepdims=True)
    grad_scores = (attn_probs * (grad_probs - inner_sum) * head_size ** (-0.5)).astype(jnp.bfloat16)
    grad_queries = jnp.einsum(
        "hqk,khd->qhd", grad_scores, key_rows, preferred_element_type=jnp.float32
    )
    grad_keys = jnp.einsum("hqk,qhd->khd", grad_scores, queries, preferred_element_type=jnp.float32)
    grad_joined = jnp.stack([grad_queries, grad_keys, grad_values], axis=1).astype(jnp.bfloat16)
    grad_joined = grad_joined.reshape(row_count, 3 * head_count * head_size)
    grad_qkv = lax.dot_general(
        normed, grad_joined, (((0,), (0,)), ((), ())), preferred_element_type=jnp.float32
    )
    return (grad_qkv, grad_out)


def per_device(
    patches,
    cotangent,
    tile_counts,
    ln_gain,
    qkv_weight,
    out_weight,
    text_states,
    mask_ids,
    text_lengths,
    gate_value,
    query_weight,
    kv_weight,
    output_weight,
):
    groups = lax.axis_size("fsdp")
    fsdp_index = lax.axis_index("fsdp")
    row_count = patches.shape[0]
    out_halves = jnp.transpose(out_weight.reshape(-1, 2, 640), (1, 0, 2)).reshape(-1, 640)
    joint = jnp.concatenate([qkv_weight, out_halves], axis=1)
    joint = jnp.transpose(joint.reshape(-1, 4, 640), (1, 0, 2))
    kv_parts = jnp.transpose(kv_weight.reshape(-1, 4, 512), (1, 0, 2))
    joint_full, kv_full = gather_weights(joint, kv_parts)
    joint_full = joint_full.reshape(4, 1280, 640)
    kv_full = kv_full.reshape(4, 1280, 512)
    full_out = joint_full[3].reshape(32, 2, 20, 640)
    full_out = jnp.transpose(full_out, (0, 2, 1, 3)).reshape(640, 1280)
    vision, saved = encode(patches, ln_gain, joint_full, full_out, tile_counts[0])
    grad_qkv, grad_out = encode_grads(saved, full_out, cotangent)
    parts = grad_qkv.astype(jnp.bfloat16).reshape(2, 8, 2, 40, 3, 640)
    parts = jnp.transpose(parts, (0, 2, 4, 1, 3, 5))
    halves = grad_out.astype(jnp.bfloat16).reshape(2, 8, 2, 20, 2, 640)
    halves = jnp.transpose(halves, (0, 2, 1, 4, 3, 5)).reshape(2, 2, 1, 8, 40, 640)
    sums = reduce_grads(jnp.concatenate([parts, halves], axis=2))
    sum_qkv = jnp.transpose(sums[:3], (1, 0, 2)).reshape(40, 1920)
    sum_out = jnp.transpose(sums[3].reshape(2, 20, 640), (1, 0, 2)).reshape(20, 1280)
    key_total = groups * row_count
    local_kv = jnp.concatenate(
        [
            jnp.dot(vision, kv_full[part], preferred_element_type=jnp.float32).astype(jnp.bfloat16)
            for part in range(4)
        ],
        axis=1,
    )
    local_kv = jnp.transpose(local_kv.reshape(row_count, KVH, 2 * HD), (1, 0, 2))
    count_rows = jnp.broadcast_to(tile_counts.astype(jnp.bfloat16)[:, None, None], (KVH, 16, 2 * HD))
    arrived = exchange_kv(jnp.concatenate([local_kv, count_rows], axis=1))
    arrived = arrived.reshape(groups, row_count + 16, 2 * HD)
    counts_all = arrived[:, row_count, 0].astype(jnp.int32)
    keys_values = arrived[:, :row_count].reshape(key_total, 2 * HD)
    key_block = keys_values[:, :HD]
    value_block = keys_values[:, HD:]
    text_count = text_states.shape[0]
    queries = jnp.dot(text_states, query_weight, preferred_element_type=jnp.float32).astype(
        jnp.bfloat16
    )
    queries = queries.reshape(text_count, -1, HD)
    position = jnp.arange(key_total)
    image_of = position // row_count
    tile_of = position % row_count // PATCH
    key_live = tile_of < jnp.repeat(counts_all, row_count)
    allowed = key_live[None, :] & (image_of[None, :] < mask_ids[:, None])
    scores = jnp.einsum(
        "thd,kd->htk", queries, key_block, preferred_element_type=jnp.float32
    ) * HD ** (-0.5)
    scores = jnp.where(allowed[None], scores, NEG)
    row_top = jnp.max(scores, axis=-1, keepdims=True)
    weights = jnp.exp(scores - row_top)
    attn_low = (weights / jnp.sum(weights, axis=-1, keepdims=True)).astype(jnp.bfloat16)
    context = jnp.einsum("htk,kd->thd", attn_low, value_block, preferred_element_type=jnp.float32)
    context = context.astype(jnp.bfloat16).reshape(text_count, -1)
    partial_out = jnp.dot(context, output_weight, preferred_element_type=jnp.float32)
    blocks = jnp.transpose(
        partial_out.astype(jnp.bfloat16).reshape(text_count, 2, 8, 2, 256), (1, 2, 3, 0, 4)
    )
    attended = reduce_attended(blocks)
    col_width = attended.shape[1]
    text_cols = lax.dynamic_slice_in_dim(text_states, fsdp_index * col_width, col_width, 1)
    row_live = jnp.any(allowed, axis=-1) & (jnp.arange(text_count) < text_lengths[0])
    gate_tanh = jnp.tanh(gate_value[0])
    result = text_cols.astype(jnp.float32) + gate_tanh * jnp.where(row_live[:, None], attended, 0.0)
    return (sum_qkv, sum_out, result.astype(jnp.bfloat16))


def solution(mesh):
    placed = (
        P(("dp", "fsdp"), None),
        P(("dp", "fsdp"), None),
        P(("dp", "fsdp")),
        P(),
        P("fsdp", None),
        P("fsdp", None),
        P("dp", None),
        P("dp"),
        P("dp"),
        P(),
        P(None, "fsdp"),
        P("fsdp", None),
        P("fsdp", None),
    )
    return jax.shard_map(
        per_device,
        mesh=mesh,
        in_specs=placed,
        out_specs=(P("fsdp", None), P("fsdp", None), P("dp", "fsdp")),
        check_vma=False,
    )
```

```python
import jax
import jax.numpy as jnp
import numpy as np
from jax import lax
from jax.sharding import PartitionSpec as P
from jax.experimental import pallas as pl
from jax.experimental.pallas import tpu as pltpu

EH = 8
EHD = 80
PATCH = 32
HD = 128
KVH = 8
LAG = 3

EPS = 1e-05
NEG = -1e30

MESH = pl.DeviceIdType.MESH


def place():
    dp = lax.axis_index("dp")
    f = lax.axis_index("fsdp")
    x = lax.rem(dp, 4)
    y = (f // 16) * 2 + dp // 4
    z = lax.rem(f // 2, 8)
    return x, y, z, lax.rem(f, 2)


def device(x, y, z, core):
    return (lax.rem(y, 2) * 4 + x, (y // 2) * 16 + z * 2 + core)


def meet(peers):
    barrier = pltpu.get_barrier_semaphore()
    for peer in peers:
        pl.semaphore_signal(barrier, inc=1, device_id=peer, device_id_type=MESH)
    pl.semaphore_wait(barrier, len(peers))


def remote(src, dst, send_sem, recv_sem, peer):
    return pltpu.make_async_remote_copy(
        src_ref=src, dst_ref=dst, send_sem=send_sem, recv_sem=recv_sem,
        device_id=peer, device_id_type=MESH,
    )


def gather_scratch():
    dma = pltpu.SemaphoreType.DMA
    return [
        dma((2, 2)), dma((2, 2)), dma((2, 8)), dma((2, 8)),
        dma((2, 2, 8)), dma((2, 2, 8)), dma((2, 8)), dma((2, 8)), dma((2, 8)), dma((2, 8)),
    ]


def gather_peers():
    x, y, z, core = place()
    peers = [device(x, y, z, 1 - core), device(x, 3 - y, z, 0), device(x, 3 - y, z, 1)]
    for step in (1, 3):
        peers.append(device(x, lax.rem(y + step, 4), z, core))
        peers.append(device(lax.rem(x + step, 4), y, z, core))
    for step in (1, 7):
        peers.append(device(x, y, lax.rem(z + step, 8), core))
    return peers


def gather_steps(t, shard, full, pair, init_send, init_recv, z_send, z_recv, near_send, near_recv,
                 far_send, far_recv, core_send, core_recv):
    x, y, z, core = place()
    y_hi = y // 2
    partner = device(x, y, z, 1 - core)
    width = pair.shape[2]
    sign = 1 - 2 * t
    mine = core == y_hi

    def turned(where):
        return lax.rem(where + t, 2)

    def spot_at(where, my_y):
        return my_y + turned(where) * (x - my_y)

    def columns(spot):
        return shard.at[:, pl.ds(pl.multiple_of(spot * width, 128), width)]

    def unit_z(u):
        d = (u + 1) // 2 if u % 2 else -(u // 2)
        return lax.rem(z - sign * d + 8, 8)

    def along_z(step):
        return device(x, y, lax.rem(z + step + 8, 8), core)

    def along(where, step):
        by_x = turned(where)
        return device(lax.rem(x + by_x * step + 4, 4), lax.rem(y + (1 - by_x) * step + 4, 4), z, core)

    def unit(u, d):
        where = unit_z(u)
        return full.at[lax.rem(spot_at(where, y) + d, 4), core, where]

    def to_partner():
        return remote(columns(spot_at(z, y)), pair.at[core], init_send.at[t, 0],
                      init_recv.at[t, core], partner)

    def to_mirror():
        return remote(columns(spot_at(z, 3 - y)), pair.at[core], init_send.at[t, 1],
                      init_recv.at[t, core], device(x, 3 - y, z, y_hi))

    def own_copy():
        return pltpu.make_async_copy(columns(spot_at(z, y)), pair.at[core], init_send.at[t, 0])

    def from_core(other):
        return remote(pair.at[other], pair.at[other], init_send.at[t, 0], init_recv.at[t, other], partner)

    def z_copy(u, u_next):
        src = unit(u, 0)
        step = sign if u_next % 2 else -sign
        return remote(src, src, z_send.at[t, u_next], z_recv.at[t, u_next], along_z(step))

    def near_copy(side, u):
        src = unit(u, 0)
        return remote(src, src, near_send.at[t, side, u], near_recv.at[t, side, u],
                      along(unit_z(u), 1 - 2 * side))

    def near_arrival(side, u):
        dst = unit(u, 3 - 2 * side)
        return remote(dst, dst, near_send.at[t, side, u], near_recv.at[t, side, u], partner)

    def far_copy(u):
        where = unit_z(u)
        back = lax.rem(where // 2, 2)
        src = unit(u, 3 - 2 * back)
        return remote(src, src, far_send.at[t, u], far_recv.at[t, u], along(where, 1 - 2 * back))

    def far_arrival(u):
        dst = unit(u, 2)
        return remote(dst, dst, far_send.at[t, u], far_recv.at[t, u], partner)

    def pass_on(u):
        src = full.at[:, core, unit_z(u)]
        return remote(src, src, core_send.at[t, u], core_recv.at[t, u], partner)

    def passed(u):
        dst = full.at[:, 1 - core, unit_z(u)]
        return remote(dst, dst, core_send.at[t, u], core_recv.at[t, u], partner)

    to_mirror().start()

    @pl.when(mine)
    def _():
        own_copy().start()

    @pl.when(jnp.logical_not(mine))
    def _():
        to_partner().start()
    yield
    for u in range(10):
        if u == 0:
            @pl.when(mine)
            def _():
                own_copy().wait()
                from_core(1 - core).wait_recv()

            @pl.when(jnp.logical_not(mine))
            def _():
                from_core(0).wait_recv()
                from_core(1).wait_recv()
            both = jnp.concatenate([pair[0].astype(jnp.float32), pair[1].astype(jnp.float32)], axis=0)
            full[spot_at(z, y), core, z] = both.astype(jnp.bfloat16)
            z_copy(0, 1).start()
            z_copy(0, 2).start()
        elif u < 8:
            z_copy(u, u).wait_recv()
            if u + 2 < 8:
                z_copy(u, u + 2).start()
        if u < 8:
            near_copy(0, u).start()
            near_copy(1, u).start()
        if 1 <= u < 9:
            for side in range(2):
                near_arrival(side, u - 1).wait_recv()
            far_copy(u - 1).start()
        if 2 <= u:
            far_arrival(u - 2).wait_recv()
            pass_on(u - 2).start()
        yield
    to_mirror().wait_send()

    @pl.when(jnp.logical_not(mine))
    def _():
        to_partner().wait_send()
    for u in range(8):
        passed(u).wait_recv()
        pass_on(u).wait_send()
        if u:
            z_copy(0, u).wait_send()
        near_copy(0, u).wait_send()
        near_copy(1, u).wait_send()
        far_copy(u).wait_send()
    yield


def dot(a, b, over=((1,), (0,))):
    return lax.dot_general(a, b, (over, ((), ())), preferred_element_type=jnp.float32)


def head_stack(rows, head_mask):
    return jnp.concatenate([rows * head_mask[h:h + 1] for h in range(EH)], axis=0)


def head_pick(stack, head_mask):
    rows = stack.shape[0] // EH
    total = jnp.zeros((rows, stack.shape[1]), jnp.float32)
    for h in range(EH):
        total = total + stack[h * rows:(h + 1) * rows] * head_mask[h:h + 1].astype(jnp.float32)
    return total


def encode_kernel(count_ref, patches, gain, joint, kv_shard, text, query_weight, head_mask, pick,
                  half_mask, kv_out, queries_out, normed_out, qkv_out, probs_out, spread_out, out_weight,
                  joint_full, kv_full, joint_pair, kv_pair, text_in, query_in, local_sem, *sems):
    meet(gather_peers())
    first = gather_steps(0, joint, joint_full, joint_pair, *sems)
    second = gather_steps(1, kv_shard, kv_full, kv_pair, *sems)
    next(first)
    next(second)
    load_text = pltpu.make_async_copy(text, text_in, local_sem.at[0])
    load_query = pltpu.make_async_copy(query_weight, query_in, local_sem.at[1])
    load_text.start()
    load_query.start()

    next(first)
    inputs = patches[...].astype(jnp.float32)
    centred = inputs - jnp.mean(inputs, axis=-1, keepdims=True)
    spread = jnp.mean(centred * centred, axis=-1, keepdims=True)
    normed = (centred * lax.rsqrt(spread + EPS) * gain[...]).astype(jnp.bfloat16)
    normed_out[...] = normed
    next(first)
    load_text.wait()
    load_query.wait()
    queries = jnp.zeros(queries_out.shape, jnp.float32)
    for step in range(8):
        queries = queries + dot(text_in[:, step * 1024:(step + 1) * 1024],
                                query_in[step * 1024:(step + 1) * 1024, :])
        next(first)
        if step >= LAG:
            next(second)
    queries_out[...] = queries.astype(jnp.bfloat16)
    next(first)

    masks = head_mask[...]
    rows = inputs.shape[0]
    next(second)
    query = dot(normed_out[...], joint_full[0].reshape(1280, 640)).astype(jnp.bfloat16)
    qkv_out[0] = query
    next(second)
    key = dot(normed_out[...], joint_full[1].reshape(1280, 640)).astype(jnp.bfloat16)
    qkv_out[1] = key
    next(second)
    value = dot(normed_out[...], joint_full[2].reshape(1280, 640)).astype(jnp.bfloat16)
    qkv_out[2] = value
    out_weight[...] = joint_full[3].reshape(1280, 640)
    next(second)
    live_key = lax.broadcasted_iota(jnp.int32, (1, rows), 1) < count_ref[0] * PATCH
    live_row = lax.broadcasted_iota(jnp.int32, (rows, 1), 0) < count_ref[0] * PATCH
    scores = dot(head_stack(query, masks), key, ((1,), (1,))) * EHD ** (-0.5)
    scores = jnp.where(live_key, scores, NEG)
    weights = jnp.exp(scores - jnp.max(scores, axis=-1, keepdims=True))
    probs = weights / jnp.sum(weights, axis=-1, keepdims=True)
    probs_out[...] = probs
    next(second)
    context = head_pick(dot(probs.astype(jnp.bfloat16), value), masks).astype(jnp.bfloat16)
    both = dot(context, pick[...], ((1,), (1,))).astype(jnp.bfloat16)
    halves = jnp.concatenate([both * half_mask[0:1], both * half_mask[1:2]], axis=0)
    spread_out[...] = halves
    branch = dot(halves, out_weight[...])
    branch = jnp.concatenate([branch[:rows], branch[rows:]], axis=1)
    vision = jnp.where(live_row, patches[...].astype(jnp.float32) + branch, 0.0).astype(jnp.bfloat16)
    for _ in second:
        pass
    for part in range(4):
        piece = dot(vision, kv_full[part].reshape(1280, 512)).astype(jnp.bfloat16)
        for side in range(2):
            kv_out[2 * part + side, pl.ds(0, rows), :] = piece[:, side * 256:(side + 1) * 256]
    number = jnp.full((KVH, 16, 256), count_ref[0].astype(jnp.float32)).astype(jnp.bfloat16)
    kv_out[:, pl.ds(rows, 16), :] = number


def encode(count, patches, gain, joint, kv_shard, text, query_weight, head_mask, pick, half_mask):
    dma = pltpu.SemaphoreType.DMA
    vmem = pl.BlockSpec(memory_space=pltpu.VMEM)
    any_space = pl.BlockSpec(memory_space=pl.ANY)
    low = jnp.bfloat16
    rows = patches.shape[0]
    return pl.pallas_call(
        encode_kernel,
        out_shape=(
            jax.ShapeDtypeStruct((KVH, rows + 16, 256), low),
            jax.ShapeDtypeStruct((text.shape[0], 256), low),
            jax.ShapeDtypeStruct(patches.shape, low),
            jax.ShapeDtypeStruct((3, rows, 640), low),
            jax.ShapeDtypeStruct((EH * rows, rows), jnp.float32),
            jax.ShapeDtypeStruct((2 * rows, 1280), low),
            jax.ShapeDtypeStruct((1280, 640), low),
        ),
        in_specs=[pl.BlockSpec(memory_space=pltpu.SMEM), vmem, vmem, vmem, vmem, any_space, any_space,
                  vmem, vmem, vmem],
        out_specs=[vmem] * 7,
        scratch_shapes=[
            pltpu.VMEM((4, 2, 8, 80, 640), low), pltpu.VMEM((4, 2, 8, 80, 512), low),
            pltpu.VMEM((2, 40, 640), low), pltpu.VMEM((2, 40, 512), low),
            pltpu.VMEM(text.shape, low), pltpu.VMEM(query_weight.shape, low), dma((2,)),
        ] + gather_scratch(),
        compiler_params=pltpu.CompilerParams(
            collective_id=0, has_side_effects=True, vmem_limit_bytes=56 * 2**20),
        name="encode",
    )(count, patches, gain, joint, kv_shard, text, query_weight, head_mask, pick, half_mask)


def reduce_peers():
    x, y, z, core = place()
    peers = [device(x, y, z, 1 - core)]
    for step in range(1, 4):
        for other in range(2):
            peers.append(device(x, lax.rem(y + step, 4), z, other))
            peers.append(device(lax.rem(x + step, 4), y, z, other))
    for step in range(1, 8):
        peers.append(device(x, y, lax.rem(z + step, 8), core))
    return peers


def reduce_steps(grads, out, from_core, chip_sum, from_near, plane_sum, from_z, from_cross, total,
                 core_send, core_recv, near_send, near_recv, z_send, z_recv, cross_send, cross_recv,
                 last_send, last_recv):
    x, y, z, core = place()
    y_hi = y // 2
    partner = device(x, y, z, 1 - core)
    spots = (y, x)
    rows, width = out.shape[1:]

    def along(axis, step):
        if axis == 0:
            return device(x, lax.rem(y + step, 4), z, core)
        return device(lax.rem(x + step, 4), y, z, core)

    def part(v, d):
        return lax.rem(spots[v] + d, 4)

    def core_copy(v, d):
        return remote(grads.at[1 - core, v, part(v, d)], from_core.at[v, d],
                      core_send.at[v, d], core_recv.at[v, d], partner)

    def near_copy(v, d):
        return remote(chip_sum.at[v, d - 1], from_near.at[v, d - 1],
                      near_send.at[v, d - 1], near_recv.at[v, d - 1], along(v, d))

    def z_copy(v, d):
        return remote(plane_sum.at[v, lax.rem(z + d, 8)], from_z.at[v, d - 1],
                      z_send.at[v, d - 1], z_recv.at[v, d - 1], device(x, y, lax.rem(z + d, 8), core))

    def cross_copy(v, d):
        slot = spots[1 - v]
        return remote(from_cross.at[v, slot], from_cross.at[v, slot],
                      cross_send.at[v, d - 1], cross_recv.at[v, d - 1], along(1 - v, d))

    def cross_arrival(v, d):
        slot = lax.rem(spots[1 - v] + 4 - d, 4)
        return remote(from_cross.at[v, slot], from_cross.at[v, slot],
                      cross_send.at[v, d - 1], cross_recv.at[v, d - 1], partner)

    def last_copy(v, i):
        peer = device(x, 2 * core + i, z, 0) if v == 0 else device(i, y, z, 1)
        slot = spots[v]
        return remote(total.at[v], out.at[slot], last_send.at[v, i], last_recv.at[slot], peer)

    def last_self(v, i):
        if v == 0:
            return jnp.logical_and(2 * core + i == y, core == 0)
        return jnp.logical_and(i == x, core == 1)

    for d in (2, 1, 3, 0):
        for v in range(2):
            core_copy(v, d).start()
    yield
    for d in (2, 1, 3):
        for v in range(2):
            core_copy(v, d).wait_recv()

            def add(k, carry, v=v, d=d):
                chip_sum[v, d - 1, k] = (
                    grads[core, v, part(v, d), k].astype(jnp.float32)
                    + from_core[v, d, k].astype(jnp.float32)
                ).astype(jnp.bfloat16)
                return carry
            lax.fori_loop(0, 8, add, 0)
            near_copy(v, d).start()
        yield
    for v in range(2):
        core_copy(v, 0).wait_recv()
        for d in range(1, 4):
            near_copy(v, d).wait_recv()

        def add(k, carry, v=v):
            sums = (grads[core, v, spots[v], k].astype(jnp.float32)
                    + from_core[v, 0, k].astype(jnp.float32))
            for d in range(3):
                sums = sums + from_near[v, d, k].astype(jnp.float32)
            plane_sum[v, k] = sums.astype(jnp.bfloat16)
            return carry
        lax.fori_loop(0, 8, add, 0)
        for d in (4, 3, 5, 2, 6, 1, 7):
            z_copy(v, d).start()
        yield
    for v in range(2):
        for d in range(1, 8):
            z_copy(v, d).wait_recv()
        sums = plane_sum[v, z].astype(jnp.float32)
        for d in range(7):
            sums = sums + from_z[v, d].astype(jnp.float32)
        from_cross[v, spots[1 - v]] = sums
        for d in (2, 1, 3):
            cross_copy(v, d).start()
    yield
    for v in range(2):
        for d in range(1, 4):
            cross_arrival(v, d).wait_recv()
        total[v] = (from_cross[v, 0] + from_cross[v, 1]) + (from_cross[v, 2] + from_cross[v, 3])
        for i in range(2 if v == 0 else 4):
            active = True if v == 0 else y_hi == core

            @pl.when(jnp.logical_and(active, jnp.logical_not(last_self(v, i))))
            def _(v=v, i=i):
                last_copy(v, i).start()

            @pl.when(jnp.logical_and(active, last_self(v, i)))
            def _(v=v):
                out[spots[v]] = total[v]
    yield
    for j in range(4):
        skip = jnp.where(core == 0, jnp.logical_and(j == y, y_hi == 0),
                         jnp.logical_and(j == x, y_hi == 1))

        @pl.when(jnp.logical_not(skip))
        def _(j=j):
            remote(out.at[j], out.at[j], last_send.at[0, 0], last_recv.at[j], partner).wait_recv()
    for v in range(2):
        for d in range(4):
            core_copy(v, d).wait_send()
        for d in range(1, 4):
            near_copy(v, d).wait_send()
            cross_copy(v, d).wait_send()
        for d in range(1, 8):
            z_copy(v, d).wait_send()
        for i in range(2 if v == 0 else 4):
            active = True if v == 0 else y_hi == core

            @pl.when(jnp.logical_and(active, jnp.logical_not(last_self(v, i))))
            def _(v=v, i=i):
                last_copy(v, i).wait_send()


def reduce_scratch():
    dma = pltpu.SemaphoreType.DMA
    block = (40, 640)
    return [
        pltpu.VMEM((2, 4, 8) + block, jnp.bfloat16),
        pltpu.VMEM((2, 3, 8) + block, jnp.bfloat16),
        pltpu.VMEM((2, 3, 8) + block, jnp.bfloat16),
        pltpu.VMEM((2, 8) + block, jnp.bfloat16),
        pltpu.VMEM((2, 7) + block, jnp.bfloat16),
        pltpu.VMEM((2, 4) + block, jnp.float32),
        pltpu.VMEM((2,) + block, jnp.float32),
        dma((2, 4)), dma((2, 4)), dma((2, 3)), dma((2, 3)), dma((2, 7)), dma((2, 7)),
        dma((2, 3)), dma((2, 3)), dma((2, 4)), dma((4,)),
    ]


def attended_steps(partial, out, from_core, chip_sum, from_y, group_sum, from_z,
                   core_send, core_recv, y_send, y_recv, z_send, z_recv):
    x, y, z, core = place()
    y_hi = y // 2
    partner = device(x, y, z, 1 - core)
    across = device(x, lax.rem(y + 2, 4), z, core)
    order = (4, 3, 5, 2, 6, 1, 7, 0)

    def spot(d):
        return lax.rem(z + d, 8)

    def core_copy(half, d):
        row = y_hi if half else 1 - y_hi
        return remote(partial.at[row, spot(d), 1 - core], from_core.at[half, d],
                      core_send.at[half, d], core_recv.at[half, d], partner)

    def y_copy(d):
        return remote(chip_sum.at[d], from_y.at[d], y_send.at[d], y_recv.at[d], across)

    def z_copy(d):
        return remote(group_sum.at[d], from_z.at[d], z_send.at[d], z_recv.at[d],
                      device(x, y, spot(d), core))

    for half in range(2):
        for d in order:
            core_copy(half, d).start()
    yield
    for d in order:
        core_copy(0, d).wait_recv()
        chip_sum[d] = (partial[1 - y_hi, spot(d), core].astype(jnp.float32)
                       + from_core[0, d].astype(jnp.float32)).astype(jnp.bfloat16)
        y_copy(d).start()
    yield
    for d in order:
        core_copy(1, d).wait_recv()
        y_copy(d).wait_recv()
        sums = (partial[y_hi, spot(d), core].astype(jnp.float32)
                + from_core[1, d].astype(jnp.float32) + from_y[d].astype(jnp.float32))
        if d:
            group_sum[d] = sums.astype(jnp.bfloat16)
            z_copy(d).start()
        else:
            out[...] = sums
    yield
    sums = out[...]
    for d in range(1, 8):
        z_copy(d).wait_recv()
        sums = sums + from_z[d].astype(jnp.float32)
    out[...] = sums
    for d in range(8):
        core_copy(0, d).wait_send()
        core_copy(1, d).wait_send()
        y_copy(d).wait_send()
        if d:
            z_copy(d).wait_send()


def attended_scratch():
    dma = pltpu.SemaphoreType.DMA
    block = (128, 256)
    return [
        pltpu.VMEM((2, 8) + block, jnp.bfloat16),
        pltpu.VMEM((8,) + block, jnp.bfloat16),
        pltpu.VMEM((8,) + block, jnp.bfloat16),
        pltpu.VMEM((8,) + block, jnp.bfloat16),
        pltpu.VMEM((8,) + block, jnp.bfloat16),
        dma((2, 8)), dma((2, 8)), dma((8,)), dma((8,)), dma((8,)), dma((8,)),
    ]


ORDER = ((4, 1), (4, 0), (3, 1), (5, 1), (3, 0), (5, 0), (2, 1), (6, 1), (2, 0), (6, 0),
         (1, 1), (7, 1), (1, 0), (7, 0), (0, 1), (0, 0))


def exchange_steps(kv, arrived, local_sem, far_send, far_recv, core_send, core_recv):
    x, y, z, core = place()
    y_hi = y // 2
    partner = device(x, y, z, 1 - core)

    def far_copy(step, turn):
        to_y = lax.rem(y + 2 * turn, 4)
        to_z = lax.rem(z + step, 8)
        head = (to_y // 2) * 4 + to_z // 2
        return remote(kv.at[head], arrived.at[y_hi, z, core], far_send.at[step, turn],
                      far_recv.at[step, turn], device(x, to_y, to_z, core))

    def source(step, turn):
        return arrived.at[lax.rem(y_hi + turn, 2), lax.rem(z + 8 - step, 8), core]

    def pass_on(step, turn):
        src = source(step, turn)
        return remote(src, src, core_send.at[step, turn], core_recv.at[step, turn], partner)

    own = pltpu.make_async_copy(kv.at[y_hi * 4 + z // 2], arrived.at[y_hi, z, core], local_sem)
    own.start()
    for step, turn in ORDER:
        if step or turn:
            far_copy(step, turn).start()
    yield
    for step, turn in reversed(ORDER):
        if step or turn:
            src = source(step, turn)
            remote(src, src, far_send.at[step, turn], far_recv.at[step, turn], partner).wait_recv()
        else:
            own.wait()
        pass_on(step, turn).start()
    yield
    for step, turn in reversed(ORDER):
        dst = arrived.at[lax.rem(y_hi + turn, 2), lax.rem(z + 8 - step, 8), 1 - core]
        remote(dst, dst, core_send.at[step, turn], core_recv.at[step, turn], partner).wait_recv()
    for step, turn in ORDER:
        pass_on(step, turn).wait_send()
        if step or turn:
            far_copy(step, turn).wait_send()


def exchange_scratch():
    dma = pltpu.SemaphoreType.DMA
    return [dma(()), dma((8, 2)), dma((8, 2)), dma((8, 2)), dma((8, 2))]


def tables():
    lane = np.arange(640)
    row = np.arange(1280)
    head_mask = (lane[None] // 80 == np.arange(8)[:, None])
    pick = (row[:, None] // 40 * 20 + row[:, None] % 20) == lane[None]
    half_mask = (row[None] % 40 // 20) == np.arange(2)[:, None]
    return tuple(jnp.asarray(a, jnp.bfloat16) for a in (head_mask, pick, half_mask))


def finish_peers():
    x, y, z, core = place()
    peers = reduce_peers()
    for step in range(8):
        if step:
            peers.append(device(x, lax.rem(y + 2, 4), lax.rem(z + step, 8), core))
    return peers


def finish_kernel(count_ref, length_ref, kv, queries, normed, qkv, probs_ref, spread, out_weight,
                  cotangent, mask_ids, head_mask, pick, half_mask, output_weight,
                  sums_out, attended_out,
                  arrived, scores, grads, partial, head_rows, grad_rows, weight_in, load_sem, *rest):
    split = len(exchange_scratch())
    middle = split + len(reduce_scratch())
    meet(finish_peers())
    exchange = exchange_steps(kv, arrived, *rest[:split])
    reduce = reduce_steps(grads, sums_out, *rest[split:middle])
    attend = attended_steps(partial, attended_out, *rest[middle:])
    next(exchange)
    load = pltpu.make_async_copy(output_weight, weight_in, load_sem)
    load.start()

    rows = cotangent.shape[0]
    masks = head_mask[...]
    low = jnp.bfloat16
    live_row = lax.broadcasted_iota(jnp.int32, (rows, 1), 0) < count_ref[0] * PATCH
    upstream = jnp.where(live_row, cotangent[...].astype(jnp.float32), 0.0).astype(low)
    sides = jnp.concatenate([upstream[:, :640], upstream[:, 640:]], axis=0)
    backs = dot(sides, out_weight[...], ((1,), (1,)))
    backs = (backs[:rows] * half_mask[0:1].astype(jnp.float32)
             + backs[rows:] * half_mask[1:2].astype(jnp.float32))
    high = backs.astype(low)
    rest_low = (backs - high.astype(jnp.float32)).astype(low)
    picked = dot(jnp.concatenate([high, rest_low], axis=0), pick[...])
    grad_context = (picked[:rows] + picked[rows:]).astype(low)
    grad_rows[...] = head_stack(grad_context, masks)
    head_rows[...] = head_stack(qkv[0], masks)
    probs = probs_ref[...]
    grad_probs = dot(grad_rows[...], qkv[2], ((1,), (1,)))
    inner = jnp.sum(probs * grad_probs, axis=-1, keepdims=True)
    grad_scores = (probs * (grad_probs - inner) * EHD ** (-0.5)).astype(low)
    grad_values = dot(probs.astype(low).T, grad_rows[...]).astype(low)
    grad_keys = dot(grad_scores.T, head_rows[...]).astype(low)
    grad_queries = head_pick(dot(grad_scores, qkv[1]), masks).astype(low)

    def store(j, left, right):
        for y_hi in range(2):
            block = dot(left[640 * y_hi:640 * (y_hi + 1)], right).astype(low).astype(jnp.float32)
            for z in range(8):
                for core in range(2):
                    start = 80 * z + 40 * core
                    grads[y_hi, core, j, z] = block[start:start + 40].astype(low)

    turned = normed[...].T
    for j, right in enumerate((grad_queries, grad_keys, grad_values)):
        store(j, turned, right)
    store(3, spread[...].T, sides)
    next(reduce)
    next(reduce)
    next(reduce)
    next(reduce)

    next(exchange)
    for _ in exchange:
        pass
    next(reduce)
    next(reduce)
    text = queries.shape[0]
    stacked = jnp.concatenate([queries[:, :HD], queries[:, HD:]], axis=0)
    images = jnp.concatenate([mask_ids[...], mask_ids[...]], axis=0)
    tile_of = lax.broadcasted_iota(jnp.int32, (1, rows), 1)
    top = jnp.full((2 * text, 1), NEG, jnp.float32)
    seen = jnp.zeros((2 * text, 1), jnp.float32)
    for i in range(32):
        where = (i // 16, i // 2 % 8, i % 2)
        counts = arrived[where + (pl.ds(rows, 16), pl.ds(0, 128))][0:1].astype(jnp.float32)
        live = tile_of.astype(jnp.float32) < counts * float(PATCH)
        allowed = jnp.logical_and(live, i < images)
        keys = arrived[where + (pl.ds(0, rows), pl.ds(0, HD))]
        piece = dot(stacked, keys, ((1,), (1,))) * HD ** (-0.5)
        piece = jnp.where(allowed, piece, NEG)
        scores[:, i * 128:(i + 1) * 128] = piece
        top = jnp.maximum(top, jnp.max(piece, axis=-1, keepdims=True))
        seen = jnp.maximum(seen, jnp.max(jnp.where(allowed, 1.0, 0.0), axis=-1, keepdims=True))
    total = jnp.zeros((2 * text, 1), jnp.float32)
    for i in range(32):
        piece = jnp.exp(scores[:, i * 128:(i + 1) * 128] - top)
        scores[:, i * 128:(i + 1) * 128] = piece
        total = total + jnp.sum(piece, axis=-1, keepdims=True)
    context = jnp.zeros((2 * text, HD), jnp.float32)
    for i in range(32):
        where = (i // 16, i // 2 % 8, i % 2)
        low_probs = (scores[:, i * 128:(i + 1) * 128] / total).astype(low)
        context = context + dot(low_probs, arrived[where + (pl.ds(0, rows), pl.ds(HD, HD))])
    context = context.astype(low)
    context = jnp.concatenate([context[:text], context[text:]], axis=1)
    load.wait()

    def project(block, carry):
        columns = pl.ds(pl.multiple_of(block * 256, 256), 256)
        partial[block // 16, lax.rem(block // 2, 8), lax.rem(block, 2)] = dot(
            context, weight_in[:, columns]).astype(low)
        return carry
    lax.fori_loop(0, 32, project, 0)
    next(attend)
    next(reduce)
    next(attend)
    next(attend)
    for _ in reduce:
        pass
    for _ in attend:
        pass
    rows_live = jnp.logical_and(
        seen[:text] > 0.0,
        lax.broadcasted_iota(jnp.int32, (text, 1), 0) < length_ref[0])
    attended_out[...] = jnp.where(rows_live, attended_out[...], 0.0)


def finish(count, length, kv, queries, normed, qkv, probs, spread, out_weight, cotangent, mask_ids,
           head_mask, pick, half_mask, output_weight):
    dma = pltpu.SemaphoreType.DMA
    vmem = pl.BlockSpec(memory_space=pltpu.VMEM)
    smem = pl.BlockSpec(memory_space=pltpu.SMEM)
    low = jnp.bfloat16
    rows = cotangent.shape[0]
    text = queries.shape[0]
    return pl.pallas_call(
        finish_kernel,
        out_shape=(jax.ShapeDtypeStruct((4, 40, 640), jnp.float32),
                   jax.ShapeDtypeStruct((text, 256), jnp.float32)),
        in_specs=[smem, smem] + [vmem] * 12 + [pl.BlockSpec(memory_space=pl.ANY)],
        out_specs=[vmem] * 2,
        scratch_shapes=[
            pltpu.VMEM((2, 8, 2, rows + 16, 256), low), pltpu.VMEM((2 * text, 32 * 128), jnp.float32),
            pltpu.VMEM((2, 2, 4, 8, 40, 640), low), pltpu.VMEM((2, 8, 2, text, 256), low),
            pltpu.VMEM((EH * rows, 640), low), pltpu.VMEM((EH * rows, 640), low),
            pltpu.VMEM(output_weight.shape, low), dma(()),
        ] + exchange_scratch() + reduce_scratch() + attended_scratch(),
        compiler_params=pltpu.CompilerParams(
            collective_id=1, has_side_effects=True, vmem_limit_bytes=60 * 2**20),
        name="finish",
    )(count, length, kv, queries, normed, qkv, probs, spread, out_weight, cotangent, mask_ids,
      head_mask, pick, half_mask, output_weight)


def per_device(
    patches,
    cotangent,
    tile_counts,
    ln_gain,
    qkv_weight,
    out_weight,
    text_states,
    mask_ids,
    text_lengths,
    gate_value,
    query_weight,
    kv_weight,
    output_weight,
):
    fsdp_index = lax.axis_index("fsdp")
    head_mask, pick, half_mask = tables()
    out_halves = jnp.transpose(out_weight.reshape(-1, 2, 640), (1, 0, 2)).reshape(-1, 640)
    joint = jnp.concatenate([qkv_weight, out_halves], axis=1)
    kv, queries, normed, qkv, probs, spread, out_rows = encode(
        tile_counts, patches, ln_gain[None], joint, kv_weight, text_states, query_weight,
        head_mask, pick, half_mask)
    sums, attended = finish(
        tile_counts, text_lengths, kv, queries, normed, qkv, probs, spread, out_rows, cotangent,
        mask_ids[:, None], head_mask, pick, half_mask, output_weight)
    sum_qkv = jnp.transpose(sums[:3], (1, 0, 2)).reshape(40, 1920)
    sum_out = jnp.transpose(sums[3].reshape(2, 20, 640), (1, 0, 2)).reshape(20, 1280)
    col_width = attended.shape[1]
    text_cols = lax.dynamic_slice_in_dim(text_states, fsdp_index * col_width, col_width, 1)
    result = text_cols.astype(jnp.float32) + jnp.tanh(gate_value[0]) * attended
    return (sum_qkv, sum_out, result.astype(jnp.bfloat16))


def solution(mesh):
    placed = (
        P(("dp", "fsdp"), None),
        P(("dp", "fsdp"), None),
        P(("dp", "fsdp")),
        P(),
        P("fsdp", None),
        P("fsdp", None),
        P("dp", None),
        P("dp"),
        P("dp"),
        P(),
        P(None, "fsdp"),
        P("fsdp", None),
        P("fsdp", None),
    )
    return jax.shard_map(
        per_device,
        mesh=mesh,
        in_specs=placed,
        out_specs=(P("fsdp", None), P("fsdp", None), P("dp", "fsdp")),
        check_vma=False,
    )
```

```python
import jax
import jax.numpy as jnp
import numpy as np
from jax import lax
from jax.sharding import PartitionSpec as P
from jax.experimental import pallas as pl
from jax.experimental.pallas import tpu as pltpu

EH = 8
EHD = 80
PATCH = 32
HD = 128
KVH = 8
LAG = 0
NEAR_LAG = 3
FAR_LAG = 3

EPS = 1e-05
NEG = -1e30

MESH = pl.DeviceIdType.MESH


def place():
    dp = lax.axis_index("dp")
    f = lax.axis_index("fsdp")
    x = lax.rem(dp, 4)
    y = (f // 16) * 2 + dp // 4
    z = lax.rem(f // 2, 8)
    return x, y, z, lax.rem(f, 2)


def device(x, y, z, core):
    return (lax.rem(y, 2) * 4 + x, (y // 2) * 16 + z * 2 + core)


def meet(peers):
    barrier = pltpu.get_barrier_semaphore()
    for peer in peers:
        pl.semaphore_signal(barrier, inc=1, device_id=peer, device_id_type=MESH)
    pl.semaphore_wait(barrier, len(peers))


def remote(src, dst, send_sem, recv_sem, peer):
    return pltpu.make_async_remote_copy(
        src_ref=src, dst_ref=dst, send_sem=send_sem, recv_sem=recv_sem,
        device_id=peer, device_id_type=MESH,
    )


def gather_scratch():
    dma = pltpu.SemaphoreType.DMA
    return [
        dma((2, 2)), dma((2, 2)), dma((2, 8)), dma((2, 8)),
        dma((2, 2, 8)), dma((2, 2, 8)), dma((2, 8)), dma((2, 8)), dma((2, 8)), dma((2, 8)),
    ]


def gather_peers():
    x, y, z, core = place()
    peers = [device(x, y, z, 1 - core), device(x, 3 - y, z, 0), device(x, 3 - y, z, 1)]
    for step in (1, 3):
        peers.append(device(x, lax.rem(y + step, 4), z, core))
        peers.append(device(lax.rem(x + step, 4), y, z, core))
    for step in (1, 7):
        peers.append(device(x, y, lax.rem(z + step, 8), core))
    peers.append(device(x, y, z + 1 - 2 * lax.rem(z, 2), 1 - core))
    return peers


def gather_steps(t, shard, full, pair, init_send, init_recv, z_send, z_recv, near_send, near_recv,
                 far_send, far_recv, core_send, core_recv):
    x, y, z, core = place()
    y_hi = y // 2
    partner = device(x, y, z, 1 - core)
    width = pair.shape[2]
    sign = 1 - 2 * t
    mine = core == y_hi

    def turned(where):
        return lax.rem(where + t, 2)

    def spot_at(where, my_y):
        return my_y + turned(where) * (x - my_y)

    def columns(spot):
        if t == 0:
            return shard.at[spot]
        return shard.at[:, pl.ds(pl.multiple_of(spot * width, 128), width)]

    def unit_z(u):
        d = (u + 1) // 2 if u % 2 else -(u // 2)
        return lax.rem(z - sign * d + 8, 8)

    def along_z(step):
        return device(x, y, lax.rem(z + step + 8, 8), core)

    def along(where, step):
        by_x = turned(where)
        return device(lax.rem(x + by_x * step + 4, 4), lax.rem(y + (1 - by_x) * step + 4, 4), z, core)

    def unit(u, d):
        where = unit_z(u)
        return full.at[lax.rem(spot_at(where, y) + d, 4), core, where]

    def to_partner():
        return remote(columns(spot_at(z, y)), pair.at[core], init_send.at[t, 0],
                      init_recv.at[t, core], partner)

    def to_mirror():
        return remote(columns(spot_at(z, 3 - y)), pair.at[core], init_send.at[t, 1],
                      init_recv.at[t, core], device(x, 3 - y, z, y_hi))

    def own_copy():
        return pltpu.make_async_copy(columns(spot_at(z, y)), pair.at[core], init_send.at[t, 0])

    def from_core(other):
        return remote(pair.at[other], pair.at[other], init_send.at[t, 0], init_recv.at[t, other], partner)

    def z_copy(u, u_next):
        src = unit(u, 0)
        step = sign if u_next % 2 else -sign
        return remote(src, src, z_send.at[t, u_next], z_recv.at[t, u_next], along_z(step))

    def near_copy(side, u):
        src = unit(u, 0)
        return remote(src, src, near_send.at[t, side, u], near_recv.at[t, side, u],
                      along(unit_z(u), 1 - 2 * side))

    def near_arrival(side, u):
        dst = unit(u, 3 - 2 * side)
        return remote(dst, dst, near_send.at[t, side, u], near_recv.at[t, side, u], partner)

    def far_copy(u):
        where = unit_z(u)
        back = lax.rem(where // 2, 2)
        src = unit(u, 3 - 2 * back)
        return remote(src, src, far_send.at[t, u], far_recv.at[t, u], along(where, 1 - 2 * back))

    def far_arrival(u):
        dst = unit(u, 2)
        return remote(dst, dst, far_send.at[t, u], far_recv.at[t, u], partner)

    def pass_on(u):
        src = full.at[:, core, unit_z(u)]
        return remote(src, src, core_send.at[t, u], core_recv.at[t, u], partner)

    def passed(u):
        dst = full.at[:, 1 - core, unit_z(u)]
        return remote(dst, dst, core_send.at[t, u], core_recv.at[t, u], partner)

    to_mirror().start()

    @pl.when(mine)
    def _():
        own_copy().start()

    @pl.when(jnp.logical_not(mine))
    def _():
        to_partner().start()
    yield
    for u in range(8 + NEAR_LAG + FAR_LAG):
        if u == 0:
            @pl.when(mine)
            def _():
                own_copy().wait()
                from_core(1 - core).wait_recv()

            @pl.when(jnp.logical_not(mine))
            def _():
                from_core(0).wait_recv()
                from_core(1).wait_recv()
            both = jnp.concatenate([pair[0].astype(jnp.float32), pair[1].astype(jnp.float32)], axis=0)
            full[spot_at(z, y), core, z] = both.astype(jnp.bfloat16)
            z_copy(0, 1).start()
            z_copy(0, 2).start()
        elif u < 8:
            z_copy(u, u).wait_recv()
            if u + 2 < 8:
                z_copy(u, u + 2).start()
        if u < 8:
            near_copy(0, u).start()
            near_copy(1, u).start()
        if 0 <= u - NEAR_LAG < 8:
            for side in range(2):
                near_arrival(side, u - NEAR_LAG).wait_recv()
            far_copy(u - NEAR_LAG).start()
        if 0 <= u - NEAR_LAG - FAR_LAG:
            far_arrival(u - NEAR_LAG - FAR_LAG).wait_recv()
            pass_on(u - NEAR_LAG - FAR_LAG).start()
        yield
    to_mirror().wait_send()

    @pl.when(jnp.logical_not(mine))
    def _():
        to_partner().wait_send()
    for u in range(8):
        passed(u).wait_recv()
        pass_on(u).wait_send()
        if u:
            z_copy(0, u).wait_send()
        near_copy(0, u).wait_send()
        near_copy(1, u).wait_send()
        far_copy(u).wait_send()
    yield


def dot(a, b, over=((1,), (0,))):
    return lax.dot_general(a, b, (over, ((), ())), preferred_element_type=jnp.float32)


def head_stack(rows, head_mask):
    return jnp.concatenate([rows * head_mask[h:h + 1] for h in range(EH)], axis=0)


def head_pick(stack, head_mask):
    rows = stack.shape[0] // EH
    total = jnp.zeros((rows, stack.shape[1]), jnp.float32)
    for h in range(EH):
        total = total + stack[h * rows:(h + 1) * rows] * head_mask[h:h + 1].astype(jnp.float32)
    return total


def query_copy(queries, send_sem, recv_sem, offset):
    x, y, z, core = place()
    side = lax.rem(z, 2)
    peer = device(x, y, z + (offset // 2) * (1 - 2 * side), lax.rem(core + offset, 2))
    slot = queries.at[2 * side + core]
    return remote(slot, slot, send_sem.at[offset - 1], recv_sem.at[offset - 1], peer)


def encode_kernel(count_ref, patches, gain, qkv_shard, out_shard, kv_shard, text, query_weight, head_mask,
                  pick, half_mask, kv_out, queries_out, normed_out, qkv_out, probs_out, spread_out,
                  out_weight, joint, joint_full, kv_full, joint_pair, kv_pair, text_in, query_in,
                  local_sem, query_send, query_recv, *sems):
    for part in range(3):
        joint[part] = qkv_shard[:, part * 640:(part + 1) * 640]
    shard = out_shard[...].astype(jnp.float32)
    joint[3] = jnp.concatenate([shard[:, :640], shard[:, 640:]], axis=0).astype(jnp.bfloat16)
    meet(gather_peers())
    first = gather_steps(0, joint, joint_full, joint_pair, *sems)
    second = gather_steps(1, kv_shard, kv_full, kv_pair, *sems)
    next(first, None)
    next(second, None)
    load_text = pltpu.make_async_copy(text, text_in, local_sem.at[0])
    load_query = pltpu.make_async_copy(query_weight, query_in, local_sem.at[1])
    load_text.start()
    load_query.start()

    next(first, None)
    inputs = patches[...].astype(jnp.float32)
    centred = inputs - jnp.mean(inputs, axis=-1, keepdims=True)
    spread = jnp.mean(centred * centred, axis=-1, keepdims=True)
    normed = (centred * lax.rsqrt(spread + EPS) * gain[...].reshape(1, -1)).astype(jnp.bfloat16)
    normed_out[...] = normed
    next(first, None)
    load_text.wait()
    load_query.wait()
    queries = jnp.zeros(queries_out.shape[1:], jnp.float32)
    for step in range(6 + NEAR_LAG + FAR_LAG):
        if step < 8:
            queries = queries + dot(text_in[:, step * 1024:(step + 1) * 1024],
                                    query_in[step * 1024:(step + 1) * 1024, :])
        next(first, None)
        if step >= LAG:
            next(second, None)
    _, _, z, core = place()
    queries_out[2 * lax.rem(z, 2) + core] = queries.astype(jnp.bfloat16)
    for offset in range(1, 4):
        query_copy(queries_out, query_send, query_recv, offset).start()
    next(first, None)

    masks = head_mask[...]
    rows = inputs.shape[0]
    next(second, None)
    query = dot(normed_out[...], joint_full[0].reshape(1280, 640)).astype(jnp.bfloat16)
    qkv_out[0] = query
    next(second, None)
    key = dot(normed_out[...], joint_full[1].reshape(1280, 640)).astype(jnp.bfloat16)
    qkv_out[1] = key
    next(second, None)
    value = dot(normed_out[...], joint_full[2].reshape(1280, 640)).astype(jnp.bfloat16)
    qkv_out[2] = value
    out_weight[...] = joint_full[3].reshape(1280, 640)
    next(second, None)
    live_key = lax.broadcasted_iota(jnp.int32, (1, rows), 1) < count_ref[0] * PATCH
    live_row = lax.broadcasted_iota(jnp.int32, (rows, 1), 0) < count_ref[0] * PATCH
    scores = dot(head_stack(query, masks), key, ((1,), (1,))) * EHD ** (-0.5)
    scores = jnp.where(live_key, scores, NEG)
    weights = jnp.exp(scores - jnp.max(scores, axis=-1, keepdims=True))
    probs = weights / jnp.sum(weights, axis=-1, keepdims=True)
    probs_out[...] = probs
    next(second, None)
    context = head_pick(dot(probs.astype(jnp.bfloat16), value), masks).astype(jnp.bfloat16)
    both = dot(context, pick[...], ((1,), (1,))).astype(jnp.bfloat16)
    halves = jnp.concatenate([both * half_mask[0:1], both * half_mask[1:2]], axis=0)
    spread_out[...] = halves
    branch = dot(halves, out_weight[...])
    branch = jnp.concatenate([branch[:rows], branch[rows:]], axis=1)
    vision = jnp.where(live_row, patches[...].astype(jnp.float32) + branch, 0.0).astype(jnp.bfloat16)
    for _ in second:
        pass
    for part in range(4):
        piece = dot(vision, kv_full[part].reshape(1280, 512)).astype(jnp.bfloat16)
        for side in range(2):
            kv_out[2 * part + side, pl.ds(0, rows), :] = piece[:, side * 256:(side + 1) * 256]
    for offset in range(1, 4):
        query_copy(queries_out, query_send, query_recv, offset).wait()
    number = jnp.full((KVH, 16, 256), count_ref[0].astype(jnp.float32)).astype(jnp.bfloat16)
    kv_out[:, pl.ds(rows, 16), :] = number


def encode(count, patches, gain, qkv_shard, out_shard, kv_shard, text, query_weight, head_mask, pick, half_mask):
    dma = pltpu.SemaphoreType.DMA
    vmem = pl.BlockSpec(memory_space=pltpu.VMEM)
    any_space = pl.BlockSpec(memory_space=pl.ANY)
    low = jnp.bfloat16
    rows = patches.shape[0]
    return pl.pallas_call(
        encode_kernel,
        out_shape=(
            jax.ShapeDtypeStruct((KVH, rows + 16, 256), low),
            jax.ShapeDtypeStruct((4, text.shape[0], 256), low),
            jax.ShapeDtypeStruct(patches.shape, low),
            jax.ShapeDtypeStruct((3, rows, 640), low),
            jax.ShapeDtypeStruct((EH * rows, rows), jnp.float32),
            jax.ShapeDtypeStruct((2 * rows, 1280), low),
            jax.ShapeDtypeStruct((1280, 640), low),
        ),
        in_specs=[pl.BlockSpec(memory_space=pltpu.SMEM)] + [vmem] * 5 + [any_space] * 2 + [vmem] * 3,
        out_specs=[vmem] * 7,
        scratch_shapes=[
            pltpu.VMEM((4, 40, 640), low), pltpu.VMEM((4, 2, 8, 80, 640), low), pltpu.VMEM((4, 2, 8, 80, 512), low),
            pltpu.VMEM((2, 40, 640), low), pltpu.VMEM((2, 40, 512), low),
            pltpu.VMEM(text.shape, low), pltpu.VMEM(query_weight.shape, low), dma((2,)),
            dma((3,)), dma((3,)),
        ] + gather_scratch(),
        compiler_params=pltpu.CompilerParams(
            collective_id=0, has_side_effects=True, vmem_limit_bytes=56 * 2**20),
        name="encode",
    )(count, patches, gain, qkv_shard, out_shard, kv_shard, text, query_weight, head_mask, pick, half_mask)


def reduce_peers():
    x, y, z, core = place()
    peers = [device(x, y, z, 1 - core)]
    for step in range(1, 4):
        for other in range(2):
            peers.append(device(x, lax.rem(y + step, 4), z, other))
            peers.append(device(lax.rem(x + step, 4), y, z, other))
    for step in range(1, 8):
        peers.append(device(x, y, lax.rem(z + step, 8), core))
    return peers


def reduce_steps(grads, out, from_core, chip_sum, from_near, plane_sum, from_z, from_cross, total,
                 core_send, core_recv, near_send, near_recv, z_send, z_recv, cross_send, cross_recv,
                 last_send, last_recv):
    x, y, z, core = place()
    y_hi = y // 2
    partner = device(x, y, z, 1 - core)
    spots = (y, x)
    rows, width = out.shape[1:]

    def along(axis, step):
        if axis == 0:
            return device(x, lax.rem(y + step, 4), z, core)
        return device(lax.rem(x + step, 4), y, z, core)

    def part(v, d):
        return lax.rem(spots[v] + d, 4)

    def core_copy(v, d):
        return remote(grads.at[1 - core, v, part(v, d)], from_core.at[v, d],
                      core_send.at[v, d], core_recv.at[v, d], partner)

    def near_copy(v, d):
        return remote(chip_sum.at[v, d - 1], from_near.at[v, d - 1],
                      near_send.at[v, d - 1], near_recv.at[v, d - 1], along(v, d))

    def z_copy(v, d):
        return remote(plane_sum.at[v, lax.rem(z + d, 8)], from_z.at[v, d - 1],
                      z_send.at[v, d - 1], z_recv.at[v, d - 1], device(x, y, lax.rem(z + d, 8), core))

    def cross_copy(v, d):
        slot = spots[1 - v]
        return remote(from_cross.at[v, slot], from_cross.at[v, slot],
                      cross_send.at[v, d - 1], cross_recv.at[v, d - 1], along(1 - v, d))

    def cross_arrival(v, d):
        slot = lax.rem(spots[1 - v] + 4 - d, 4)
        return remote(from_cross.at[v, slot], from_cross.at[v, slot],
                      cross_send.at[v, d - 1], cross_recv.at[v, d - 1], partner)

    def last_copy(v, i):
        peer = device(x, 2 * core + i, z, 0) if v == 0 else device(i, y, z, 1)
        slot = spots[v]
        return remote(total.at[v], out.at[slot], last_send.at[v, i], last_recv.at[slot], peer)

    def last_self(v, i):
        if v == 0:
            return jnp.logical_and(2 * core + i == y, core == 0)
        return jnp.logical_and(i == x, core == 1)

    for d in (2, 1, 3, 0):
        for v in range(2):
            core_copy(v, d).start()
    yield
    for d in (2, 1, 3):
        for v in range(2):
            core_copy(v, d).wait_recv()

            def add(k, carry, v=v, d=d):
                chip_sum[v, d - 1, k] = (
                    grads[core, v, part(v, d), k].astype(jnp.float32)
                    + from_core[v, d, k].astype(jnp.float32)
                ).astype(jnp.bfloat16)
                return carry
            lax.fori_loop(0, 8, add, 0)
            near_copy(v, d).start()
        yield
    for v in range(2):
        core_copy(v, 0).wait_recv()
        for d in range(1, 4):
            near_copy(v, d).wait_recv()

        def add(k, carry, v=v):
            sums = (grads[core, v, spots[v], k].astype(jnp.float32)
                    + from_core[v, 0, k].astype(jnp.float32))
            for d in range(3):
                sums = sums + from_near[v, d, k].astype(jnp.float32)
            plane_sum[v, k] = sums.astype(jnp.bfloat16)
            return carry
        lax.fori_loop(0, 8, add, 0)
        for d in (4, 3, 5, 2, 6, 1, 7):
            z_copy(v, d).start()
        yield
    for v in range(2):
        for d in range(1, 8):
            z_copy(v, d).wait_recv()
        sums = plane_sum[v, z].astype(jnp.float32)
        for d in range(7):
            sums = sums + from_z[v, d].astype(jnp.float32)
        from_cross[v, spots[1 - v]] = sums
        for d in (2, 1, 3):
            cross_copy(v, d).start()
    yield
    for v in range(2):
        for d in range(1, 4):
            cross_arrival(v, d).wait_recv()
        total[v] = (from_cross[v, 0] + from_cross[v, 1]) + (from_cross[v, 2] + from_cross[v, 3])
        for i in range(2 if v == 0 else 4):
            active = True if v == 0 else y_hi == core

            @pl.when(jnp.logical_and(active, jnp.logical_not(last_self(v, i))))
            def _(v=v, i=i):
                last_copy(v, i).start()

            @pl.when(jnp.logical_and(active, last_self(v, i)))
            def _(v=v):
                out[spots[v]] = total[v]
    yield
    for j in range(4):
        skip = jnp.where(core == 0, jnp.logical_and(j == y, y_hi == 0),
                         jnp.logical_and(j == x, y_hi == 1))

        @pl.when(jnp.logical_not(skip))
        def _(j=j):
            remote(out.at[j], out.at[j], last_send.at[0, 0], last_recv.at[j], partner).wait_recv()
    for v in range(2):
        for d in range(4):
            core_copy(v, d).wait_send()
        for d in range(1, 4):
            near_copy(v, d).wait_send()
            cross_copy(v, d).wait_send()
        for d in range(1, 8):
            z_copy(v, d).wait_send()
        for i in range(2 if v == 0 else 4):
            active = True if v == 0 else y_hi == core

            @pl.when(jnp.logical_and(active, jnp.logical_not(last_self(v, i))))
            def _(v=v, i=i):
                last_copy(v, i).wait_send()


def reduce_scratch():
    dma = pltpu.SemaphoreType.DMA
    block = (40, 640)
    return [
        pltpu.VMEM((2, 4, 8) + block, jnp.bfloat16),
        pltpu.VMEM((2, 3, 8) + block, jnp.bfloat16),
        pltpu.VMEM((2, 3, 8) + block, jnp.bfloat16),
        pltpu.VMEM((2, 8) + block, jnp.bfloat16),
        pltpu.VMEM((2, 7) + block, jnp.bfloat16),
        pltpu.VMEM((2, 4) + block, jnp.float32),
        pltpu.VMEM((2,) + block, jnp.float32),
        dma((2, 4)), dma((2, 4)), dma((2, 3)), dma((2, 3)), dma((2, 7)), dma((2, 7)),
        dma((2, 3)), dma((2, 3)), dma((2, 4)), dma((4,)),
    ]


def attended_steps(partial, out, from_core, chip_sum, from_y, group_sum, from_z,
                   core_send, core_recv, y_send, y_recv, z_send, z_recv):
    x, y, z, core = place()
    y_hi = y // 2
    partner = device(x, y, z, 1 - core)
    across = device(x, lax.rem(y + 2, 4), z, core)
    order = (4, 3, 5, 2, 6, 1, 7, 0)

    def spot(d):
        return lax.rem(z + d, 8)

    def core_copy(half, d):
        row = y_hi if half else 1 - y_hi
        return remote(partial.at[row, spot(d), 1 - core], from_core.at[half, d],
                      core_send.at[half, d], core_recv.at[half, d], partner)

    def y_copy(d):
        return remote(chip_sum.at[d], from_y.at[d], y_send.at[d], y_recv.at[d], across)

    def z_copy(d):
        return remote(group_sum.at[d], from_z.at[d], z_send.at[d], z_recv.at[d],
                      device(x, y, spot(d), core))

    for half in range(2):
        for d in order:
            core_copy(half, d).start()
    yield
    for d in order:
        core_copy(0, d).wait_recv()
        chip_sum[d] = (partial[1 - y_hi, spot(d), core].astype(jnp.float32)
                       + from_core[0, d].astype(jnp.float32)).astype(jnp.bfloat16)
        y_copy(d).start()
    yield
    for d in order:
        core_copy(1, d).wait_recv()
        y_copy(d).wait_recv()
        sums = (partial[y_hi, spot(d), core].astype(jnp.float32)
                + from_core[1, d].astype(jnp.float32) + from_y[d].astype(jnp.float32))
        if d:
            group_sum[d] = sums.astype(jnp.bfloat16)
            z_copy(d).start()
        else:
            out[...] = sums
    yield
    sums = out[...]
    for d in range(1, 8):
        z_copy(d).wait_recv()
        sums = sums + from_z[d].astype(jnp.float32)
    out[...] = sums
    for d in range(8):
        core_copy(0, d).wait_send()
        core_copy(1, d).wait_send()
        y_copy(d).wait_send()
        if d:
            z_copy(d).wait_send()


def attended_scratch():
    dma = pltpu.SemaphoreType.DMA
    block = (128, 256)
    return [
        pltpu.VMEM((2, 8) + block, jnp.bfloat16),
        pltpu.VMEM((8,) + block, jnp.bfloat16),
        pltpu.VMEM((8,) + block, jnp.bfloat16),
        pltpu.VMEM((8,) + block, jnp.bfloat16),
        pltpu.VMEM((8,) + block, jnp.bfloat16),
        dma((2, 8)), dma((2, 8)), dma((8,)), dma((8,)), dma((8,)), dma((8,)),
    ]


NEAREST = ((0, 0), (1, 0), (0, 1), (1, 1), (2, 0), (2, 1), (3, 0), (3, 1))


def image_at(step, turn):
    x, y, z, core = place()
    from_z = lax.rem(z + (2 * lax.rem(z, 2) - 1) * step + 8, 8)
    return lax.rem(y // 2 + turn, 2) * 16 + from_z * 2 + core


def exchange_steps(kv, arrived, local_sem, far_send, far_recv):
    x, y, z, core = place()

    def far_copy(step, turn):
        to_y = lax.rem(y + 2 * turn, 4)
        to_z = lax.rem(z + step * (1 - 2 * lax.rem(z + step, 2)) + 8, 8)
        head = (to_y // 2) * 4 + to_z // 2
        return remote(kv.at[head], arrived.at[turn, step], far_send.at[turn, step],
                      far_recv.at[turn, step], device(x, to_y, to_z, core))

    own = pltpu.make_async_copy(kv.at[(y // 2) * 4 + z // 2], arrived.at[0, 0], local_sem)
    own.start()
    for step, turn in reversed(NEAREST):
        if step or turn:
            far_copy(step, turn).start()
    yield
    for step, turn in NEAREST:
        if step or turn:
            far_copy(step, turn).wait_recv()
        else:
            own.wait()
        yield
    for step, turn in NEAREST:
        if step or turn:
            far_copy(step, turn).wait_send()


def exchange_scratch():
    dma = pltpu.SemaphoreType.DMA
    return [dma(()), dma((2, 4)), dma((2, 4))]


def tables():
    lane = np.arange(640)
    row = np.arange(1280)
    head_mask = (lane[None] // 80 == np.arange(8)[:, None])
    pick = (row[:, None] // 40 * 20 + row[:, None] % 20) == lane[None]
    half_mask = (row[None] % 40 // 20) == np.arange(2)[:, None]
    return tuple(jnp.asarray(a, jnp.bfloat16) for a in (head_mask, pick, half_mask))


def finish_peers():
    x, y, z, core = place()
    peers = reduce_peers()
    for step in range(8):
        if step:
            peers.append(device(x, lax.rem(y + 2, 4), lax.rem(z + step, 8), core))
    peers.append(device(x, y, z + 1 - 2 * lax.rem(z, 2), 1 - core))
    return peers


def finish_kernel(count_ref, length_ref, gate_ref, kv, queries, normed, qkv, probs_ref, spread, out_weight,
                  cotangent, mask_ids, head_mask, pick, half_mask, output_weight, text_states,
                  qkv_out, out_out, result_out,
                  arrived, scores, grads, partial, head_rows, grad_rows, weight_in, sums, attended, text_in,
                  part_out, part_in, stat_out, stat_in, part_send, part_recv, stat_send, stat_recv,
                  load_sem, *rest):
    split = len(exchange_scratch())
    middle = split + len(reduce_scratch())
    meet(finish_peers())
    exchange = exchange_steps(kv, arrived, *rest[:split])
    reduce = reduce_steps(grads, sums, *rest[split:middle])
    attend = attended_steps(partial, attended, *rest[middle:])
    next(exchange)
    load = pltpu.make_async_copy(output_weight, weight_in, load_sem.at[0])
    load.start()
    columns = pl.ds(pl.multiple_of(lax.axis_index("fsdp") * 256, 256), 256)
    load_text = pltpu.make_async_copy(text_states.at[:, columns], text_in, load_sem.at[1])
    load_text.start()

    rows = cotangent.shape[0]
    masks = head_mask[...]
    low = jnp.bfloat16
    live_row = lax.broadcasted_iota(jnp.int32, (rows, 1), 0) < count_ref[0] * PATCH
    upstream = jnp.where(live_row, cotangent[...].astype(jnp.float32), 0.0).astype(low)
    sides = jnp.concatenate([upstream[:, :640], upstream[:, 640:]], axis=0)
    backs = dot(sides, out_weight[...], ((1,), (1,)))
    backs = (backs[:rows] * half_mask[0:1].astype(jnp.float32)
             + backs[rows:] * half_mask[1:2].astype(jnp.float32))
    high = backs.astype(low)
    rest_low = (backs - high.astype(jnp.float32)).astype(low)
    picked = dot(jnp.concatenate([high, rest_low], axis=0), pick[...])
    grad_context = (picked[:rows] + picked[rows:]).astype(low)
    grad_rows[...] = head_stack(grad_context, masks)
    head_rows[...] = head_stack(qkv[0], masks)
    probs = probs_ref[...]
    grad_probs = dot(grad_rows[...], qkv[2], ((1,), (1,)))
    inner = jnp.sum(probs * grad_probs, axis=-1, keepdims=True)
    grad_scores = (probs * (grad_probs - inner) * EHD ** (-0.5)).astype(low)
    grad_values = dot(probs.astype(low).T, grad_rows[...]).astype(low)
    grad_keys = dot(grad_scores.T, head_rows[...]).astype(low)
    grad_queries = head_pick(dot(grad_scores, qkv[1]), masks).astype(low)

    def store(j, left, right):
        for y_hi in range(2):
            block = dot(left[640 * y_hi:640 * (y_hi + 1)], right).astype(low).astype(jnp.float32)
            for z in range(8):
                for core in range(2):
                    start = 80 * z + 40 * core
                    grads[y_hi, core, j, z] = block[start:start + 40].astype(low)

    turned = normed[...].T
    for j, right in enumerate((grad_queries, grad_keys, grad_values)):
        store(j, turned, right)
    store(3, spread[...].T, sides)
    next(reduce)
    next(reduce)
    next(reduce)
    next(reduce)

    text = queries.shape[1]
    stacked = jnp.concatenate(
        [queries[g, :, side * HD:(side + 1) * HD] for g in range(4) for side in range(2)], axis=0)
    square = (text, text)
    diagonal = (lax.broadcasted_iota(jnp.int32, square, 0) == lax.broadcasted_iota(jnp.int32, square, 1))
    images = jnp.sum(jnp.where(diagonal, mask_ids[...].astype(jnp.float32).reshape(1, text), 0.0),
                     axis=1, keepdims=True)
    images = jnp.concatenate([images] * 8, axis=0)
    tile_of = lax.broadcasted_iota(jnp.int32, (1, rows), 1).astype(jnp.float32)
    top = jnp.full((8 * text, 1), NEG, jnp.float32)
    for i, (step, turn) in enumerate(NEAREST):
        next(exchange)
        counts = arrived[turn, step, pl.ds(rows, 16), pl.ds(0, 128)][0:1].astype(jnp.float32)
        number = image_at(step, turn).astype(jnp.float32)
        allowed = jnp.logical_and(tile_of < counts * float(PATCH), number < images)
        piece = dot(stacked, arrived[turn, step, pl.ds(0, rows), pl.ds(0, HD)], ((1,), (1,)))
        piece = jnp.where(allowed, piece * HD ** (-0.5), NEG)
        scores[:, i * 128:(i + 1) * 128] = piece
        top = jnp.maximum(top, jnp.max(piece, axis=-1, keepdims=True))
    total = jnp.zeros((8 * text, 1), jnp.float32)
    context = jnp.zeros((8 * text, HD), jnp.float32)
    for i, (step, turn) in enumerate(NEAREST):
        piece = jnp.exp(scores[:, i * 128:(i + 1) * 128] - top)
        total = total + jnp.sum(piece, axis=-1, keepdims=True)
        context = context + dot(piece.astype(low), arrived[turn, step, pl.ds(0, rows), pl.ds(HD, HD)])
    context = context / total
    total = jnp.where(top > 0.5 * NEG, total, 0.0)
    for _ in exchange:
        pass
    scores[:, 0:128] = context
    lane = lax.broadcasted_iota(jnp.int32, (1, 128), 1)
    scores[:, 128:256] = jnp.where(lane < 4, top, total)
    x, y, z, core = place()
    side = lax.rem(z, 2)

    def own_rows(group):
        return pl.ds(pl.multiple_of(group * 2 * text, 256), 2 * text)

    def context_copy(offset):
        peer = device(x, y, z + (offset // 2) * (1 - 2 * side), lax.rem(core + offset, 2))
        return remote(part_out.at[offset - 1], part_in.at[offset - 1], part_send.at[offset - 1],
                      part_recv.at[offset - 1], peer)

    def stat_copy(offset):
        peer = device(x, y, z + (offset // 2) * (1 - 2 * side), lax.rem(core + offset, 2))
        return remote(stat_out.at[offset - 1], stat_in.at[offset - 1], stat_send.at[offset - 1],
                      stat_recv.at[offset - 1], peer)

    for offset in (2, 3, 1):
        group = 2 * lax.rem(side + offset // 2, 2) + lax.rem(core + offset, 2)
        part_out[offset - 1] = scores[own_rows(group), 0:128].astype(low)
        context_copy(offset).start()
        stat_out[offset - 1] = scores[own_rows(group), 128:256].T[0:8]
        stat_copy(offset).start()
    group = 2 * side + core
    parts = [scores[own_rows(group), 0:128]]
    tops = [scores[own_rows(group), 128:129]]
    totals = [scores[own_rows(group), 132:133]]
    for offset in range(1, 4):
        context_copy(offset).wait_recv()
        stat_copy(offset).wait_recv()
        stats = jnp.concatenate([stat_in[offset - 1]] * 16, axis=0).T
        parts.append(part_in[offset - 1].astype(jnp.float32))
        tops.append(stats[:, 0:1])
        totals.append(stats[:, 4:5])
    top = jnp.maximum(jnp.maximum(tops[0], tops[1]), jnp.maximum(tops[2], tops[3]))
    seen = jnp.zeros((2 * text, 1), jnp.float32)
    context = jnp.zeros((2 * text, HD), jnp.float32)
    for k in range(4):
        share = totals[k] * jnp.exp(tops[k] - top)
        seen = seen + share
        context = context + share * parts[k]
    context = (context / jnp.where(seen > 0.0, seen, 1.0)).astype(low)
    context = jnp.concatenate([context[:text], context[text:]], axis=1)
    for offset in range(1, 4):
        context_copy(offset).wait_send()
        stat_copy(offset).wait_send()
    load.wait()

    def project(block, carry):
        columns = pl.ds(pl.multiple_of(block * 256, 256), 256)
        partial[block // 16, lax.rem(block // 2, 8), lax.rem(block, 2)] = dot(
            context, weight_in[:, columns]).astype(low)
        return carry
    lax.fori_loop(0, 32, project, 0)
    next(attend)
    next(reduce)
    next(reduce)
    next(attend)
    next(reduce)
    next(attend)
    for _ in reduce:
        pass
    for _ in attend:
        pass
    rows_live = jnp.logical_and(
        seen[:text] > 0.0,
        lax.broadcasted_iota(jnp.int32, (text, 1), 0) < length_ref[0])
    gate = jnp.tanh(jnp.full((1, 256), gate_ref[0], jnp.float32))
    load_text.wait()
    result_out[...] = (text_in[...].astype(jnp.float32)
                       + gate * jnp.where(rows_live, attended[...], 0.0)).astype(low)
    for j in range(3):
        qkv_out[:, j * 640:(j + 1) * 640] = sums[j]
    last = sums[3]
    out_out[:, 0:640] = last[0:20]
    out_out[:, 640:1280] = last[20:40]


def finish(count, length, gate, kv, queries, normed, qkv, probs, spread, out_weight, cotangent, mask_ids,
           head_mask, pick, half_mask, output_weight, text_states):
    dma = pltpu.SemaphoreType.DMA
    vmem = pl.BlockSpec(memory_space=pltpu.VMEM)
    smem = pl.BlockSpec(memory_space=pltpu.SMEM)
    low = jnp.bfloat16
    rows = cotangent.shape[0]
    text = queries.shape[1]
    return pl.pallas_call(
        finish_kernel,
        out_shape=(jax.ShapeDtypeStruct((40, 1920), jnp.float32),
                   jax.ShapeDtypeStruct((20, 1280), jnp.float32),
                   jax.ShapeDtypeStruct((text, 256), low)),
        in_specs=[smem] * 3 + [vmem] * 12 + [pl.BlockSpec(memory_space=pl.ANY)] * 2,
        out_specs=[vmem] * 3,
        scratch_shapes=[
            pltpu.VMEM((2, 4, rows + 16, 256), low), pltpu.VMEM((8 * text, 8 * 128), jnp.float32),
            pltpu.VMEM((2, 2, 4, 8, 40, 640), low), pltpu.VMEM((2, 8, 2, text, 256), low),
            pltpu.VMEM((EH * rows, 640), low), pltpu.VMEM((EH * rows, 640), low),
            pltpu.VMEM(output_weight.shape, low), pltpu.VMEM((4, 40, 640), jnp.float32),
            pltpu.VMEM((text, 256), jnp.float32), pltpu.VMEM((text, 256), low),
            pltpu.VMEM((3, 2 * text, HD), low), pltpu.VMEM((3, 2 * text, HD), low),
            pltpu.VMEM((3, 8, 2 * text), jnp.float32), pltpu.VMEM((3, 8, 2 * text), jnp.float32),
            dma((3,)), dma((3,)), dma((3,)), dma((3,)), dma((2,)),
        ] + exchange_scratch() + reduce_scratch() + attended_scratch(),
        compiler_params=pltpu.CompilerParams(
            collective_id=1, has_side_effects=True, vmem_limit_bytes=60 * 2**20),
        name="finish",
    )(count, length, gate, kv, queries, normed, qkv, probs, spread, out_weight, cotangent, mask_ids,
      head_mask, pick, half_mask, output_weight, text_states)


def per_device(
    patches,
    cotangent,
    tile_counts,
    ln_gain,
    qkv_weight,
    out_weight,
    text_states,
    mask_ids,
    text_lengths,
    gate_value,
    query_weight,
    kv_weight,
    output_weight,
):
    head_mask, pick, half_mask = tables()
    kv, queries, normed, qkv, probs, spread, out_rows = encode(
        tile_counts, patches, ln_gain, qkv_weight, out_weight, kv_weight, text_states, query_weight,
        head_mask, pick, half_mask)
    return finish(
        tile_counts, text_lengths, gate_value, kv, queries, normed, qkv, probs, spread, out_rows,
        cotangent, mask_ids, head_mask, pick, half_mask, output_weight, text_states)


def solution(mesh):
    placed = (
        P(("dp", "fsdp"), None),
        P(("dp", "fsdp"), None),
        P(("dp", "fsdp")),
        P(),
        P("fsdp", None),
        P("fsdp", None),
        P("dp", None),
        P("dp"),
        P("dp"),
        P(),
        P(None, "fsdp"),
        P("fsdp", None),
        P("fsdp", None),
    )
    return jax.shard_map(
        per_device,
        mesh=mesh,
        in_specs=placed,
        out_specs=(P("fsdp", None), P("fsdp", None), P("dp", "fsdp")),
        check_vma=False,
    )
```

```python
import jax
import jax.numpy as jnp
import numpy as np
from jax import lax
from jax.sharding import PartitionSpec as P
from jax.experimental import pallas as pl
from jax.experimental.pallas import tpu as pltpu

EH = 8
EHD = 80
PATCH = 32
HD = 128
KVH = 8
LAG = 4
NEAR_LAG = 2
FAR_LAG = 2
KV_AT = 1
REDUCE_AT = 8

EPS = 1e-05
NEG = -1e30

MESH = pl.DeviceIdType.MESH


def place():
    dp = lax.axis_index("dp")
    f = lax.axis_index("fsdp")
    x = lax.rem(dp, 4)
    y = (f // 16) * 2 + dp // 4
    z = lax.rem(f // 2, 8)
    return x, y, z, lax.rem(f, 2)


def device(x, y, z, core):
    return (lax.rem(y, 2) * 4 + x, (y // 2) * 16 + z * 2 + core)


def meet(peers):
    barrier = pltpu.get_barrier_semaphore()
    for peer in peers:
        pl.semaphore_signal(barrier, inc=1, device_id=peer, device_id_type=MESH)
    pl.semaphore_wait(barrier, len(peers))


def remote(src, dst, send_sem, recv_sem, peer):
    return pltpu.make_async_remote_copy(
        src_ref=src, dst_ref=dst, send_sem=send_sem, recv_sem=recv_sem,
        device_id=peer, device_id_type=MESH,
    )


def gather_scratch():
    dma = pltpu.SemaphoreType.DMA
    return [
        dma((2, 2)), dma((2, 2)), dma((2, 8)), dma((2, 8)),
        dma((2, 2, 8)), dma((2, 2, 8)), dma((2, 8)), dma((2, 8)), dma((2, 8)), dma((2, 8)),
    ]


def gather_steps(t, shard, full, pair, init_send, init_recv, z_send, z_recv, near_send, near_recv,
                 far_send, far_recv, core_send, core_recv):
    x, y, z, core = place()
    y_hi = y // 2
    partner = device(x, y, z, 1 - core)
    width = pair.shape[2]
    sign = 1 - 2 * t
    mine = core == y_hi

    def turned(where):
        return lax.rem(where + t, 2)

    def spot_at(where, my_y):
        return my_y + turned(where) * (x - my_y)

    def columns(spot):
        if t == 0:
            return shard.at[spot]
        return shard.at[:, pl.ds(pl.multiple_of(spot * width, 128), width)]

    def unit_z(u):
        d = (u + 1) // 2 if u % 2 else -(u // 2)
        return lax.rem(z - sign * d + 8, 8)

    def along_z(step):
        return device(x, y, lax.rem(z + step + 8, 8), core)

    def along(where, step):
        by_x = turned(where)
        return device(lax.rem(x + by_x * step + 4, 4), lax.rem(y + (1 - by_x) * step + 4, 4), z, core)

    def unit(u, d):
        where = unit_z(u)
        return full.at[lax.rem(spot_at(where, y) + d, 4), core, where]

    def to_partner():
        return remote(columns(spot_at(z, y)), pair.at[core], init_send.at[t, 0],
                      init_recv.at[t, core], partner)

    def to_mirror():
        return remote(columns(spot_at(z, 3 - y)), pair.at[core], init_send.at[t, 1],
                      init_recv.at[t, core], device(x, 3 - y, z, y_hi))

    def own_copy():
        return pltpu.make_async_copy(columns(spot_at(z, y)), pair.at[core], init_send.at[t, 0])

    def from_core(other):
        return remote(pair.at[other], pair.at[other], init_send.at[t, 0], init_recv.at[t, other], partner)

    def z_copy(u, u_next):
        src = unit(u, 0)
        step = sign if u_next % 2 else -sign
        return remote(src, src, z_send.at[t, u_next], z_recv.at[t, u_next], along_z(step))

    def near_copy(side, u):
        src = unit(u, 0)
        return remote(src, src, near_send.at[t, side, u], near_recv.at[t, side, u],
                      along(unit_z(u), 1 - 2 * side))

    def near_arrival(side, u):
        dst = unit(u, 3 - 2 * side)
        return remote(dst, dst, near_send.at[t, side, u], near_recv.at[t, side, u], partner)

    def far_copy(u):
        where = unit_z(u)
        back = lax.rem(where // 2, 2)
        src = unit(u, 3 - 2 * back)
        return remote(src, src, far_send.at[t, u], far_recv.at[t, u], along(where, 1 - 2 * back))

    def far_arrival(u):
        dst = unit(u, 2)
        return remote(dst, dst, far_send.at[t, u], far_recv.at[t, u], partner)

    def pass_on(u):
        src = full.at[:, core, unit_z(u)]
        return remote(src, src, core_send.at[t, u], core_recv.at[t, u], partner)

    def passed(u):
        dst = full.at[:, 1 - core, unit_z(u)]
        return remote(dst, dst, core_send.at[t, u], core_recv.at[t, u], partner)

    to_mirror().start()

    @pl.when(mine)
    def _():
        own_copy().start()

    @pl.when(jnp.logical_not(mine))
    def _():
        to_partner().start()
    yield
    for u in range(8 + NEAR_LAG + FAR_LAG):
        if u == 0:
            @pl.when(mine)
            def _():
                own_copy().wait()
                from_core(1 - core).wait_recv()

            @pl.when(jnp.logical_not(mine))
            def _():
                from_core(0).wait_recv()
                from_core(1).wait_recv()
            both = jnp.concatenate([pair[0].astype(jnp.float32), pair[1].astype(jnp.float32)], axis=0)
            full[spot_at(z, y), core, z] = both.astype(jnp.bfloat16)
            z_copy(0, 1).start()
            z_copy(0, 2).start()
        elif u < 8:
            z_copy(u, u).wait_recv()
            if u + 2 < 8:
                z_copy(u, u + 2).start()
        if u < 8:
            near_copy(0, u).start()
            near_copy(1, u).start()
        if 0 <= u - NEAR_LAG < 8:
            for side in range(2):
                near_arrival(side, u - NEAR_LAG).wait_recv()
            far_copy(u - NEAR_LAG).start()
        if 0 <= u - NEAR_LAG - FAR_LAG:
            far_arrival(u - NEAR_LAG - FAR_LAG).wait_recv()
            pass_on(u - NEAR_LAG - FAR_LAG).start()
        yield
    to_mirror().wait_send()

    @pl.when(jnp.logical_not(mine))
    def _():
        to_partner().wait_send()
    for u in range(8):
        passed(u).wait_recv()
        pass_on(u).wait_send()
        if u:
            z_copy(0, u).wait_send()
        near_copy(0, u).wait_send()
        near_copy(1, u).wait_send()
        far_copy(u).wait_send()
    yield


def dot(a, b, over=((1,), (0,))):
    return lax.dot_general(a, b, (over, ((), ())), preferred_element_type=jnp.float32)


def head_stack(rows, head_mask):
    return jnp.concatenate([rows * head_mask[h:h + 1] for h in range(EH)], axis=0)


def head_pick(stack, head_mask):
    rows = stack.shape[0] // EH
    total = jnp.zeros((rows, stack.shape[1]), jnp.float32)
    for h in range(EH):
        total = total + stack[h * rows:(h + 1) * rows] * head_mask[h:h + 1].astype(jnp.float32)
    return total


def query_copy(queries, send_sem, recv_sem, offset):
    x, y, z, core = place()
    side = lax.rem(z, 2)
    peer = device(x, y, z + (offset // 2) * (1 - 2 * side), lax.rem(core + offset, 2))
    slot = queries.at[2 * side + core]
    return remote(slot, slot, send_sem.at[offset - 1], recv_sem.at[offset - 1], peer)


def reduce_peers():
    x, y, z, core = place()
    peers = [device(x, y, z, 1 - core)]
    for step in range(1, 4):
        for other in range(2):
            peers.append(device(x, lax.rem(y + step, 4), z, other))
            peers.append(device(lax.rem(x + step, 4), y, z, other))
    for step in range(1, 8):
        peers.append(device(x, y, lax.rem(z + step, 8), core))
    return peers


def reduce_steps(grads, out, from_core, chip_sum, from_near, plane_sum, from_z, from_cross, total,
                 core_send, core_recv, near_send, near_recv, z_send, z_recv, cross_send, cross_recv,
                 last_send, last_recv):
    x, y, z, core = place()
    y_hi = y // 2
    partner = device(x, y, z, 1 - core)
    spots = (y, x)
    low = jnp.bfloat16

    def along(axis, step):
        if axis == 0:
            return device(x, lax.rem(y + step, 4), z, core)
        return device(lax.rem(x + step, 4), y, z, core)

    def part(v, d):
        return lax.rem(spots[v] + d, 4)

    def core_copy(v, d):
        return remote(grads.at[1 - core, v, part(v, d)], from_core.at[v, d],
                      core_send.at[v, d], core_recv.at[v, d], partner)

    def near_copy(v, d, h):
        return remote(chip_sum.at[v, d - 1, h], from_near.at[v, d - 1, h],
                      near_send.at[v, d - 1, h], near_recv.at[v, d - 1, h], along(v, d))

    def z_copy(v, d):
        to_z = lax.rem(z + d, 8)
        return remote(plane_sum.at[v, lax.rem(to_z, 2), to_z // 2], from_z.at[v, d],
                      z_send.at[v, d], z_recv.at[v, d], device(x, y, to_z, core))

    def cross_copy(v, d):
        slot = spots[1 - v]
        return remote(from_cross.at[v, slot], from_cross.at[v, slot],
                      cross_send.at[v, d - 1], cross_recv.at[v, d - 1], along(1 - v, d))

    def cross_arrival(v, d):
        slot = lax.rem(spots[1 - v] + 4 - d, 4)
        return remote(from_cross.at[v, slot], from_cross.at[v, slot],
                      cross_send.at[v, d - 1], cross_recv.at[v, d - 1], partner)

    def last_copy(v, i):
        peer = device(x, 2 * core + i, z, 0) if v == 0 else device(i, y, z, 1)
        slot = spots[v]
        return remote(total.at[v], out.at[slot], last_send.at[v, i], last_recv.at[slot], peer)

    def last_self(v, i):
        if v == 0:
            return jnp.logical_and(2 * core + i == y, core == 0)
        return jnp.logical_and(i == x, core == 1)

    for d in (2, 1, 3, 0):
        for v in range(2):
            core_copy(v, d).start()
    yield
    for h in range(2):
        for d in (2, 1, 3):
            for v in range(2):
                if h == 0:
                    core_copy(v, d).wait_recv()

                def add(k, carry, v=v, d=d, h=h):
                    chip_sum[v, d - 1, h, k] = (
                        grads[core, v, part(v, d), 2 * k + h].astype(jnp.float32)
                        + from_core[v, d, 2 * k + h].astype(jnp.float32)
                    ).astype(low)
                    return carry
                lax.fori_loop(0, 4, add, 0)
                near_copy(v, d, h).start()
        yield
    for h in range(2):
        for v in range(2):
            if h == 0:
                core_copy(v, 0).wait_recv()
            for d in range(1, 4):
                near_copy(v, d, h).wait_recv()

            def add(k, carry, v=v, h=h):
                sums = (grads[core, v, spots[v], 2 * k + h].astype(jnp.float32)
                        + from_core[v, 0, 2 * k + h].astype(jnp.float32))
                for d in range(3):
                    sums = sums + from_near[v, d, h, k].astype(jnp.float32)
                plane_sum[v, h, k] = sums.astype(low)
                return carry
            lax.fori_loop(0, 4, add, 0)
            for m in (2, 1, 3, 0):
                step = 2 * m + lax.rem(h + z, 2)

                @pl.when(step != 0)
                def _(v=v, step=step):
                    z_copy(v, step).start()
        yield
    for v in range(2):
        for d in range(1, 8):
            z_copy(v, d).wait_recv()
        sums = plane_sum[v, lax.rem(z, 2), z // 2].astype(jnp.float32)
        for d in range(1, 8):
            sums = sums + from_z[v, d].astype(jnp.float32)
        from_cross[v, spots[1 - v]] = sums.astype(low)
        for d in (2, 1, 3):
            cross_copy(v, d).start()
    yield
    for v in range(2):
        for d in range(1, 4):
            cross_arrival(v, d).wait_recv()
        terms = [from_cross[v, k].astype(jnp.float32) for k in range(4)]
        total[v] = ((terms[0] + terms[1]) + (terms[2] + terms[3])).astype(low)
        for i in range(2 if v == 0 else 4):
            active = True if v == 0 else y_hi == core

            @pl.when(jnp.logical_and(active, jnp.logical_not(last_self(v, i))))
            def _(v=v, i=i):
                last_copy(v, i).start()

            @pl.when(jnp.logical_and(active, last_self(v, i)))
            def _(v=v):
                out[spots[v]] = total[v]
    yield
    for j in range(4):
        skip = jnp.where(core == 0, jnp.logical_and(j == y, y_hi == 0),
                         jnp.logical_and(j == x, y_hi == 1))

        @pl.when(jnp.logical_not(skip))
        def _(j=j):
            remote(out.at[j], out.at[j], last_send.at[0, 0], last_recv.at[j], partner).wait_recv()
    for v in range(2):
        for d in range(4):
            core_copy(v, d).wait_send()
        for d in range(1, 4):
            near_copy(v, d, 0).wait_send()
            near_copy(v, d, 1).wait_send()
            cross_copy(v, d).wait_send()
        for d in range(1, 8):
            z_copy(v, d).wait_send()
        for i in range(2 if v == 0 else 4):
            active = True if v == 0 else y_hi == core

            @pl.when(jnp.logical_and(active, jnp.logical_not(last_self(v, i))))
            def _(v=v, i=i):
                last_copy(v, i).wait_send()


def reduce_scratch():
    dma = pltpu.SemaphoreType.DMA
    block = (40, 640)
    low = jnp.bfloat16
    return [
        pltpu.VMEM((2, 4, 8) + block, low),
        pltpu.VMEM((2, 3, 2, 4) + block, low),
        pltpu.VMEM((2, 3, 2, 4) + block, low),
        pltpu.VMEM((2, 2, 4) + block, low),
        pltpu.VMEM((2, 8) + block, low),
        pltpu.VMEM((2, 4) + block, low),
        pltpu.VMEM((2,) + block, low),
        dma((2, 4)), dma((2, 4)), dma((2, 3, 2)), dma((2, 3, 2)), dma((2, 8)), dma((2, 8)),
        dma((2, 3)), dma((2, 3)), dma((2, 4)), dma((4,)),
    ]


def attended_steps(partial, out, from_core, chip_sum, from_y, group_sum, from_z,
                   core_send, core_recv, y_send, y_recv, z_send, z_recv):
    x, y, z, core = place()
    y_hi = y // 2
    partner = device(x, y, z, 1 - core)
    across = device(x, lax.rem(y + 2, 4), z, core)
    order = (4, 3, 5, 2, 6, 1, 7, 0)

    def spot(d):
        return lax.rem(z + d, 8)

    def core_copy(half, d):
        row = y_hi if half else 1 - y_hi
        return remote(partial.at[row * 16 + spot(d) * 2 + 1 - core], from_core.at[half, d],
                      core_send.at[half, d], core_recv.at[half, d], partner)

    def y_copy(d):
        return remote(chip_sum.at[d], from_y.at[d], y_send.at[d], y_recv.at[d], across)

    def z_copy(d):
        return remote(group_sum.at[d], from_z.at[d], z_send.at[d], z_recv.at[d],
                      device(x, y, spot(d), core))

    for half in range(2):
        for d in order:
            core_copy(half, d).start()
    yield
    for d in order:
        core_copy(0, d).wait_recv()
        chip_sum[d] = (partial[(1 - y_hi) * 16 + spot(d) * 2 + core].astype(jnp.float32)
                       + from_core[0, d].astype(jnp.float32)).astype(jnp.bfloat16)
        y_copy(d).start()
    yield
    for d in order:
        core_copy(1, d).wait_recv()
        y_copy(d).wait_recv()
        sums = (partial[y_hi * 16 + spot(d) * 2 + core].astype(jnp.float32)
                + from_core[1, d].astype(jnp.float32) + from_y[d].astype(jnp.float32))
        if d:
            group_sum[d] = sums.astype(jnp.bfloat16)
            z_copy(d).start()
        else:
            out[...] = sums
    yield
    sums = out[...]
    for d in range(1, 8):
        z_copy(d).wait_recv()
        sums = sums + from_z[d].astype(jnp.float32)
    out[...] = sums
    for d in range(8):
        core_copy(0, d).wait_send()
        core_copy(1, d).wait_send()
        y_copy(d).wait_send()
        if d:
            z_copy(d).wait_send()


def attended_scratch():
    dma = pltpu.SemaphoreType.DMA
    block = (128, 256)
    return [
        pltpu.VMEM((2, 8) + block, jnp.bfloat16),
        pltpu.VMEM((8,) + block, jnp.bfloat16),
        pltpu.VMEM((8,) + block, jnp.bfloat16),
        pltpu.VMEM((8,) + block, jnp.bfloat16),
        pltpu.VMEM((8,) + block, jnp.bfloat16),
        dma((2, 8)), dma((2, 8)), dma((8,)), dma((8,)), dma((8,)), dma((8,)),
    ]


NEAREST = ((0, 0), (1, 0), (0, 1), (1, 1), (2, 0), (2, 1), (3, 0), (3, 1))


def image_at(step, turn):
    x, y, z, core = place()
    from_z = lax.rem(z + (2 * lax.rem(z, 2) - 1) * step + 8, 8)
    return lax.rem(y // 2 + turn, 2) * 16 + from_z * 2 + core


def exchange_steps(kv, arrived, local_sem, far_send, far_recv):
    x, y, z, core = place()

    def far_copy(step, turn):
        to_y = lax.rem(y + 2 * turn, 4)
        to_z = lax.rem(z + step * (1 - 2 * lax.rem(z + step, 2)) + 8, 8)
        head = (to_y // 2) * 4 + to_z // 2
        return remote(kv.at[head], arrived.at[turn, step], far_send.at[turn, step],
                      far_recv.at[turn, step], device(x, to_y, to_z, core))

    own = pltpu.make_async_copy(kv.at[(y // 2) * 4 + z // 2], arrived.at[0, 0], local_sem)
    own.start()
    for step, turn in reversed(NEAREST):
        if step or turn:
            far_copy(step, turn).start()
    yield
    for step, turn in NEAREST:
        if step or turn:
            far_copy(step, turn).wait_recv()
        else:
            own.wait()
        yield
    for step, turn in NEAREST:
        if step or turn:
            far_copy(step, turn).wait_send()


def exchange_scratch():
    dma = pltpu.SemaphoreType.DMA
    return [dma(()), dma((2, 4)), dma((2, 4))]


def tables():
    lane = np.arange(640)
    row = np.arange(1280)
    head_mask = (lane[None] // 80 == np.arange(8)[:, None])
    pick = (row[:, None] // 40 * 20 + row[:, None] % 20) == lane[None]
    half_mask = (row[None] % 40 // 20) == np.arange(2)[:, None]
    return tuple(jnp.asarray(a, jnp.bfloat16) for a in (head_mask, pick, half_mask))


def load_blocks(text, query_weight, texts, weights, sem):
    def start(k, carry):
        columns = pl.ds(pl.multiple_of(k * 256, 256), 256)
        pltpu.make_async_copy(text.at[:, columns], texts.at[k], sem.at[0]).start()
        return carry
    pltpu.make_async_copy(query_weight, weights, sem.at[1]).start()
    lax.fori_loop(0, 32, start, 0)


def step_kernel(count_ref, length_ref, gate_ref, patches, cotangent, gain, qkv_shard, out_shard, kv_shard,
                mask_ids, head_mask, pick, half_mask, text, query_weight, output_weight,
                sums, result_out,
                joint, joint_full, kv_full, joint_pair, kv_pair, texts, weights, kv, queries, normed, qkv,
                probs_ref, spread, arrived, scores, grads, head_rows, grad_rows, attended, text_in,
                part_out, part_in, stat_out, stat_in, part_send, part_recv, stat_send, stat_recv,
                query_send, query_recv, load_sem, *rest):
    a = len(gather_scratch())
    b = a + len(exchange_scratch())
    c = b + len(reduce_scratch())
    low = jnp.bfloat16
    x, y, z, core = place()
    side = lax.rem(z, 2)
    for part in range(3):
        joint[part] = qkv_shard[:, part * 640:(part + 1) * 640]
    shard = out_shard[...].astype(jnp.float32)
    joint[3] = jnp.concatenate([shard[:, :640], shard[:, 640:]], axis=0).astype(low)
    meet(step_peers())
    first = gather_steps(0, joint, joint_full, joint_pair, *rest[:a])
    second = gather_steps(1, kv_shard, kv_full, kv_pair, *rest[:a])
    exchange = exchange_steps(kv, arrived, *rest[a:b])
    reduce = reduce_steps(grads, sums, *rest[b:c])
    partial = texts
    attend = attended_steps(partial, attended, *rest[c:])
    next(first)
    next(second)
    load_blocks(text, query_weight, texts, weights, load_sem)
    columns = pl.ds(pl.multiple_of(lax.axis_index("fsdp") * 256, 256), 256)
    load_text = pltpu.make_async_copy(text.at[:, columns], text_in, load_sem.at[2])
    load_text.start()

    next(first)
    inputs = patches[...].astype(jnp.float32)
    rows = inputs.shape[0]
    centred = inputs - jnp.mean(inputs, axis=-1, keepdims=True)
    variance = jnp.mean(centred * centred, axis=-1, keepdims=True)
    normed[...] = (centred * lax.rsqrt(variance + EPS) * gain[...].reshape(1, -1)).astype(low)
    next(first)
    pltpu.make_async_copy(texts, texts, load_sem.at[0]).wait()
    pltpu.make_async_copy(query_weight, weights, load_sem.at[1]).wait()
    total = jnp.zeros(queries.shape[1:], jnp.float32)
    steps = 6 + NEAR_LAG + FAR_LAG
    for step in range(steps):
        if step < 8:
            for k in range(4 * step, 4 * step + 4):
                total = total + dot(texts[k], weights[k])
        if step == 8:
            queries[2 * side + core] = total.astype(low)
            for offset in range(1, 4):
                query_copy(queries, query_send, query_recv, offset).start()

            def start(k, carry):
                block = pl.ds(pl.multiple_of(k * 256, 256), 256)
                pltpu.make_async_copy(output_weight.at[:, block], weights.at[k], load_sem.at[1]).start()
                return carry
            lax.fori_loop(0, 32, start, 0)
        next(first)
        if step >= LAG:
            next(second, None)
    next(first, None)

    masks = head_mask[...]
    next(second, None)
    query = dot(normed[...], joint_full[0].reshape(1280, 640)).astype(low)
    qkv[0] = query
    next(second, None)
    key = dot(normed[...], joint_full[1].reshape(1280, 640)).astype(low)
    qkv[1] = key
    next(second, None)
    value = dot(normed[...], joint_full[2].reshape(1280, 640)).astype(low)
    qkv[2] = value
    next(second, None)
    live_key = lax.broadcasted_iota(jnp.int32, (1, rows), 1) < count_ref[0] * PATCH
    live_row = lax.broadcasted_iota(jnp.int32, (rows, 1), 0) < count_ref[0] * PATCH
    head_rows[...] = head_stack(query, masks)
    inner_scores = dot(head_rows[...], key, ((1,), (1,))) * EHD ** (-0.5)
    inner_scores = jnp.where(live_key, inner_scores, NEG)
    shares = jnp.exp(inner_scores - jnp.max(inner_scores, axis=-1, keepdims=True))
    probs_ref[...] = shares / jnp.sum(shares, axis=-1, keepdims=True)
    next(second, None)
    context = head_pick(dot(probs_ref[...].astype(low), qkv[2]), masks).astype(low)
    both = dot(context, pick[...], ((1,), (1,))).astype(low)
    spread[...] = jnp.concatenate([both * half_mask[0:1], both * half_mask[1:2]], axis=0)
    next(second, None)
    branch = dot(spread[...], joint_full[3].reshape(1280, 640))
    branch = jnp.concatenate([branch[:rows], branch[rows:]], axis=1)
    vision = jnp.where(live_row, patches[...].astype(jnp.float32) + branch, 0.0).astype(low)
    normed_t = normed[...].T
    next(second, None)

    upstream = jnp.where(live_row, cotangent[...].astype(jnp.float32), 0.0).astype(low)
    sides = jnp.concatenate([upstream[:, :640], upstream[:, 640:]], axis=0)
    backs = dot(sides, joint_full[3].reshape(1280, 640), ((1,), (1,)))
    backs = (backs[:rows] * half_mask[0:1].astype(jnp.float32)
             + backs[rows:] * half_mask[1:2].astype(jnp.float32))
    high = backs.astype(low)
    rest_low = (backs - high.astype(jnp.float32)).astype(low)
    picked = dot(jnp.concatenate([high, rest_low], axis=0), pick[...])
    grad_context = (picked[:rows] + picked[rows:]).astype(low)
    grad_rows[...] = head_stack(grad_context, masks)
    next(second, None)

    def project_kv():
        for part in range(4):
            piece = dot(vision, kv_full[part].reshape(1280, 512)).astype(low)
            for half in range(2):
                kv[2 * part + half, pl.ds(0, rows), :] = piece[:, half * 256:(half + 1) * 256]
        number = jnp.full((KVH, 16, 256), count_ref[0].astype(jnp.float32)).astype(low)
        kv[:, pl.ds(rows, 16), :] = number
        next(exchange)

    if KV_AT == 0:
        for _ in second:
            pass
        project_kv()
    probs = probs_ref[...]
    grad_probs = dot(grad_rows[...], qkv[2], ((1,), (1,)))
    inner = jnp.sum(probs * grad_probs, axis=-1, keepdims=True)
    grad_scores = (probs * (grad_probs - inner) * EHD ** (-0.5)).astype(low)
    next(second, None)
    grad_values = dot(probs.astype(low).T, grad_rows[...]).astype(low)
    grad_keys = dot(grad_scores.T, head_rows[...]).astype(low)
    grad_queries = head_pick(dot(grad_scores, qkv[1]), masks).astype(low)
    if KV_AT == 1:
        for _ in second:
            pass
        project_kv()

    def store(j, left, right):
        for upper in range(2):
            block = dot(left[640 * upper:640 * (upper + 1)], right)
            for k in range(8):
                for other in range(2):
                    at = 80 * k + 40 * other
                    grads[upper, other, j, k] = block[at:at + 40].astype(low)

    for j, right in enumerate((grad_queries, grad_keys, grad_values)):
        store(j, normed_t, right)
        next(second, None)
    store(3, spread[...].T, sides)
    next(reduce)
    next(second, None)
    next(reduce)
    next(second, None)
    next(reduce)
    if KV_AT == 2:
        for _ in second:
            pass
        project_kv()

    for offset in range(1, 4):
        query_copy(queries, query_send, query_recv, offset).wait()
    text_rows = queries.shape[1]
    stacked = jnp.concatenate(
        [queries[g, :, half * HD:(half + 1) * HD] for g in range(4) for half in range(2)], axis=0)
    square = (text_rows, text_rows)
    diagonal = (lax.broadcasted_iota(jnp.int32, square, 0) == lax.broadcasted_iota(jnp.int32, square, 1))
    images = jnp.sum(jnp.where(diagonal, mask_ids[...].astype(jnp.float32).reshape(1, text_rows), 0.0),
                     axis=1, keepdims=True)
    images = jnp.concatenate([images] * 8, axis=0)
    tile_of = lax.broadcasted_iota(jnp.int32, (1, rows), 1).astype(jnp.float32)
    top = jnp.full((8 * text_rows, 1), NEG, jnp.float32)
    for i, (step, turn) in enumerate(NEAREST):
        if i == REDUCE_AT:
            next(reduce)
        next(exchange)
        counts = arrived[turn, step, pl.ds(rows, 16), pl.ds(0, 128)][0:1].astype(jnp.float32)
        number = image_at(step, turn).astype(jnp.float32)
        allowed = jnp.logical_and(tile_of < counts * float(PATCH), number < images)
        piece = dot(stacked, arrived[turn, step, pl.ds(0, rows), pl.ds(0, HD)], ((1,), (1,)))
        piece = jnp.where(allowed, piece * HD ** (-0.5), NEG)
        scores[:, i * 128:(i + 1) * 128] = piece
        top = jnp.maximum(top, jnp.max(piece, axis=-1, keepdims=True))
    total = jnp.zeros((8 * text_rows, 1), jnp.float32)
    context = jnp.zeros((8 * text_rows, HD), jnp.float32)
    for i, (step, turn) in enumerate(NEAREST):
        piece = jnp.exp(scores[:, i * 128:(i + 1) * 128] - top)
        total = total + jnp.sum(piece, axis=-1, keepdims=True)
        context = context + dot(piece.astype(low), arrived[turn, step, pl.ds(0, rows), pl.ds(HD, HD)])
    context = context / total
    total = jnp.where(top > 0.5 * NEG, total, 0.0)
    for _ in exchange:
        pass
    scores[:, 0:128] = context
    lane = lax.broadcasted_iota(jnp.int32, (1, 128), 1)
    scores[:, 128:256] = jnp.where(lane < 4, top, total)

    def own_rows(group):
        return pl.ds(pl.multiple_of(group * 2 * text_rows, 256), 2 * text_rows)

    def merge_copy(offset, out, into, send_sem, recv_sem):
        peer = device(x, y, z + (offset // 2) * (1 - 2 * side), lax.rem(core + offset, 2))
        return remote(out.at[offset - 1], into.at[offset - 1], send_sem.at[offset - 1],
                      recv_sem.at[offset - 1], peer)

    def context_copy(offset):
        return merge_copy(offset, part_out, part_in, part_send, part_recv)

    def stat_copy(offset):
        return merge_copy(offset, stat_out, stat_in, stat_send, stat_recv)

    for offset in (2, 3, 1):
        group = 2 * lax.rem(side + offset // 2, 2) + lax.rem(core + offset, 2)
        part_out[offset - 1] = scores[own_rows(group), 0:128].astype(low)
        context_copy(offset).start()
        stat_out[offset - 1] = scores[own_rows(group), 128:256].T[0:8]
        stat_copy(offset).start()
    if REDUCE_AT == 8:
        next(reduce)
    group = 2 * side + core
    parts = [scores[own_rows(group), 0:128]]
    tops = [scores[own_rows(group), 128:129]]
    totals = [scores[own_rows(group), 132:133]]
    for offset in range(1, 4):
        context_copy(offset).wait_recv()
        stat_copy(offset).wait_recv()
        stats = jnp.concatenate([stat_in[offset - 1]] * 16, axis=0).T
        parts.append(part_in[offset - 1].astype(jnp.float32))
        tops.append(stats[:, 0:1])
        totals.append(stats[:, 4:5])
    top = jnp.maximum(jnp.maximum(tops[0], tops[1]), jnp.maximum(tops[2], tops[3]))
    seen = jnp.zeros((2 * text_rows, 1), jnp.float32)
    context = jnp.zeros((2 * text_rows, HD), jnp.float32)
    for k in range(4):
        share = totals[k] * jnp.exp(tops[k] - top)
        seen = seen + share
        context = context + share * parts[k]
    context = (context / jnp.where(seen > 0.0, seen, 1.0)).astype(low)
    context = jnp.concatenate([context[:text_rows], context[text_rows:]], axis=1)
    pltpu.make_async_copy(weights, weights, load_sem.at[1]).wait()

    def project(block, carry):
        partial[block] = dot(context, weights[block]).astype(low)
        return carry
    lax.fori_loop(0, 32, project, 0)
    next(attend)
    if REDUCE_AT == 9:
        next(reduce)
    next(attend)
    next(reduce)
    next(attend)
    next(reduce)
    for _ in attend:
        pass
    for _ in reduce:
        pass
    for offset in range(1, 4):
        context_copy(offset).wait_send()
        stat_copy(offset).wait_send()
    rows_live = jnp.logical_and(
        seen[:text_rows] > 0.0,
        lax.broadcasted_iota(jnp.int32, (text_rows, 1), 0) < length_ref[0])
    gate = jnp.tanh(jnp.full((1, 256), gate_ref[0], jnp.float32))
    load_text.wait()
    result_out[...] = (text_in[...].astype(jnp.float32)
                       + gate * jnp.where(rows_live, attended[...], 0.0)).astype(low)


def step_peers():
    x, y, z, core = place()
    peers = reduce_peers()
    for step in range(1, 8):
        peers.append(device(x, lax.rem(y + 2, 4), lax.rem(z + step, 8), core))
    peers.append(device(x, y, z + 1 - 2 * lax.rem(z, 2), 1 - core))
    return peers


def whole_step(*operands):
    dma = pltpu.SemaphoreType.DMA
    vmem = pl.BlockSpec(memory_space=pltpu.VMEM)
    smem = pl.BlockSpec(memory_space=pltpu.SMEM)
    low = jnp.bfloat16
    rows = operands[3].shape[0]
    text = operands[13].shape[0]
    return pl.pallas_call(
        step_kernel,
        out_shape=(jax.ShapeDtypeStruct((4, 40, 640), low),
                   jax.ShapeDtypeStruct((text, 256), low)),
        in_specs=[smem] * 3 + [vmem] * 10 + [pl.BlockSpec(memory_space=pl.ANY)] * 3,
        out_specs=[vmem] * 2,
        scratch_shapes=[
            pltpu.VMEM((4, 40, 640), low), pltpu.VMEM((4, 2, 8, 80, 640), low),
            pltpu.VMEM((4, 2, 8, 80, 512), low), pltpu.VMEM((2, 40, 640), low),
            pltpu.VMEM((2, 40, 512), low), pltpu.VMEM((32, text, 256), low),
            pltpu.VMEM((32, 256, 256), low), pltpu.VMEM((KVH, rows + 16, 256), low),
            pltpu.VMEM((4, text, 256), low), pltpu.VMEM((rows, 1280), low),
            pltpu.VMEM((3, rows, 640), low), pltpu.VMEM((EH * rows, rows), jnp.float32),
            pltpu.VMEM((2 * rows, 1280), low), pltpu.VMEM((2, 4, rows + 16, 256), low),
            pltpu.VMEM((8 * text, 8 * 128), jnp.float32), pltpu.VMEM((2, 2, 4, 8, 40, 640), low),
            pltpu.VMEM((EH * rows, 640), low), pltpu.VMEM((EH * rows, 640), low),
            pltpu.VMEM((text, 256), jnp.float32), pltpu.VMEM((text, 256), low),
            pltpu.VMEM((3, 2 * text, HD), low), pltpu.VMEM((3, 2 * text, HD), low),
            pltpu.VMEM((3, 8, 2 * text), jnp.float32), pltpu.VMEM((3, 8, 2 * text), jnp.float32),
            dma((3,)), dma((3,)), dma((3,)), dma((3,)), dma((3,)), dma((3,)), dma((3,)),
        ] + gather_scratch() + exchange_scratch() + reduce_scratch() + attended_scratch(),
        compiler_params=pltpu.CompilerParams(
            collective_id=0, has_side_effects=True, vmem_limit_bytes=63 * 2**20),
        name="whole_step",
    )(*operands)


def result_kernel(sums, result, qkv_out, out_out, result_out):
    for j in range(3):
        qkv_out[:, j * 640:(j + 1) * 640] = sums[j].astype(jnp.float32)
    last = sums[3].astype(jnp.float32)
    out_out[:, 0:640] = last[0:20]
    out_out[:, 640:1280] = last[20:40]
    result_out[...] = result[...]


def write_results(sums, result):
    vmem = pl.BlockSpec(memory_space=pltpu.VMEM)
    return pl.pallas_call(
        result_kernel,
        out_shape=(jax.ShapeDtypeStruct((40, 1920), jnp.float32),
                   jax.ShapeDtypeStruct((20, 1280), jnp.float32),
                   jax.ShapeDtypeStruct(result.shape, result.dtype)),
        in_specs=[vmem] * 2,
        out_specs=[vmem] * 3,
        name="write_results",
    )(sums, result)


def per_device(
    patches,
    cotangent,
    tile_counts,
    ln_gain,
    qkv_weight,
    out_weight,
    text_states,
    mask_ids,
    text_lengths,
    gate_value,
    query_weight,
    kv_weight,
    output_weight,
):
    head_mask, pick, half_mask = tables()
    sums, result = whole_step(
        tile_counts, text_lengths, gate_value, patches, cotangent, ln_gain, qkv_weight, out_weight,
        kv_weight, mask_ids, head_mask, pick, half_mask, text_states,
        query_weight.reshape(32, 256, 256), output_weight)
    return write_results(sums, result)


def solution(mesh):
    placed = (
        P(("dp", "fsdp"), None),
        P(("dp", "fsdp"), None),
        P(("dp", "fsdp")),
        P(),
        P("fsdp", None),
        P("fsdp", None),
        P("dp", None),
        P("dp"),
        P("dp"),
        P(),
        P(None, "fsdp"),
        P("fsdp", None),
        P("fsdp", None),
    )
    return jax.shard_map(
        per_device,
        mesh=mesh,
        in_specs=placed,
        out_specs=(P("fsdp", None), P("fsdp", None), P("dp", "fsdp")),
        check_vma=False,
    )
```

```python
import jax
import jax.numpy as jnp
import numpy as np
from jax import lax
from jax.sharding import PartitionSpec as P
from jax.experimental import pallas as pl
from jax.experimental.pallas import tpu as pltpu

EH = 8
EHD = 80
PATCH = 32
HD = 128
KVH = 8
LAG = 0
NEAR_LAG = 3
FAR_LAG = 3
KV_AT = 0
REDUCE_AT = 8
GRAD_ORDER = (3, 0, 1, 2)

EPS = 1e-05
NEG = -1e30

MESH = pl.DeviceIdType.MESH


def place():
    dp = lax.axis_index("dp")
    f = lax.axis_index("fsdp")
    x = lax.rem(dp, 4)
    y = (f // 16) * 2 + dp // 4
    z = lax.rem(f // 2, 8)
    return x, y, z, lax.rem(f, 2)


def device(x, y, z, core):
    return (lax.rem(y, 2) * 4 + x, (y // 2) * 16 + z * 2 + core)


def meet(peers):
    barrier = pltpu.get_barrier_semaphore()
    for peer in peers:
        pl.semaphore_signal(barrier, inc=1, device_id=peer, device_id_type=MESH)
    pl.semaphore_wait(barrier, len(peers))


def remote(src, dst, send_sem, recv_sem, peer):
    return pltpu.make_async_remote_copy(
        src_ref=src, dst_ref=dst, send_sem=send_sem, recv_sem=recv_sem,
        device_id=peer, device_id_type=MESH,
    )


def gather_scratch():
    dma = pltpu.SemaphoreType.DMA
    return [
        dma((2, 2)), dma((2, 2)), dma((2, 8)), dma((2, 8)),
        dma((2, 2, 8)), dma((2, 2, 8)), dma((2, 8)), dma((2, 8)), dma((2, 8)), dma((2, 8)),
    ]


def gather_steps(t, shard, full, pair, init_send, init_recv, z_send, z_recv, near_send, near_recv,
                 far_send, far_recv, core_send, core_recv):
    x, y, z, core = place()
    y_hi = y // 2
    partner = device(x, y, z, 1 - core)
    width = pair.shape[2]
    sign = 1 - 2 * t
    mine = core == y_hi

    def turned(where):
        return lax.rem(where + t, 2)

    def spot_at(where, my_y):
        return my_y + turned(where) * (x - my_y)

    def columns(spot):
        if t == 0:
            return shard.at[spot]
        return shard.at[:, pl.ds(pl.multiple_of(spot * width, 128), width)]

    def unit_z(u):
        d = (u + 1) // 2 if u % 2 else -(u // 2)
        return lax.rem(z - sign * d + 8, 8)

    def along_z(step):
        return device(x, y, lax.rem(z + step + 8, 8), core)

    def along(where, step):
        by_x = turned(where)
        return device(lax.rem(x + by_x * step + 4, 4), lax.rem(y + (1 - by_x) * step + 4, 4), z, core)

    def unit(u, d):
        where = unit_z(u)
        return full.at[lax.rem(spot_at(where, y) + d, 4), core, where]

    def to_partner():
        return remote(columns(spot_at(z, y)), pair.at[core], init_send.at[t, 0],
                      init_recv.at[t, core], partner)

    def to_mirror():
        return remote(columns(spot_at(z, 3 - y)), pair.at[core], init_send.at[t, 1],
                      init_recv.at[t, core], device(x, 3 - y, z, y_hi))

    def own_copy():
        return pltpu.make_async_copy(columns(spot_at(z, y)), pair.at[core], init_send.at[t, 0])

    def from_core(other):
        return remote(pair.at[other], pair.at[other], init_send.at[t, 0], init_recv.at[t, other], partner)

    def z_copy(u, u_next):
        src = unit(u, 0)
        step = sign if u_next % 2 else -sign
        return remote(src, src, z_send.at[t, u_next], z_recv.at[t, u_next], along_z(step))

    def near_copy(side, u):
        src = unit(u, 0)
        return remote(src, src, near_send.at[t, side, u], near_recv.at[t, side, u],
                      along(unit_z(u), 1 - 2 * side))

    def near_arrival(side, u):
        dst = unit(u, 3 - 2 * side)
        return remote(dst, dst, near_send.at[t, side, u], near_recv.at[t, side, u], partner)

    def far_copy(u):
        where = unit_z(u)
        back = lax.rem(where // 2, 2)
        src = unit(u, 3 - 2 * back)
        return remote(src, src, far_send.at[t, u], far_recv.at[t, u], along(where, 1 - 2 * back))

    def far_arrival(u):
        dst = unit(u, 2)
        return remote(dst, dst, far_send.at[t, u], far_recv.at[t, u], partner)

    def pass_on(u):
        src = full.at[:, core, unit_z(u)]
        return remote(src, src, core_send.at[t, u], core_recv.at[t, u], partner)

    def passed(u):
        dst = full.at[:, 1 - core, unit_z(u)]
        return remote(dst, dst, core_send.at[t, u], core_recv.at[t, u], partner)

    to_mirror().start()

    @pl.when(mine)
    def _():
        own_copy().start()

    @pl.when(jnp.logical_not(mine))
    def _():
        to_partner().start()
    yield
    for u in range(8 + NEAR_LAG + FAR_LAG):
        if u == 0:
            @pl.when(mine)
            def _():
                own_copy().wait()
                from_core(1 - core).wait_recv()

            @pl.when(jnp.logical_not(mine))
            def _():
                from_core(0).wait_recv()
                from_core(1).wait_recv()
            both = jnp.concatenate([pair[0].astype(jnp.float32), pair[1].astype(jnp.float32)], axis=0)
            full[spot_at(z, y), core, z] = both.astype(jnp.bfloat16)
            z_copy(0, 1).start()
            z_copy(0, 2).start()
        elif u < 8:
            z_copy(u, u).wait_recv()
            if u + 2 < 8:
                z_copy(u, u + 2).start()
        if u < 8:
            near_copy(0, u).start()
            near_copy(1, u).start()
        if 0 <= u - NEAR_LAG < 8:
            for side in range(2):
                near_arrival(side, u - NEAR_LAG).wait_recv()
            far_copy(u - NEAR_LAG).start()
        if 0 <= u - NEAR_LAG - FAR_LAG:
            far_arrival(u - NEAR_LAG - FAR_LAG).wait_recv()
            pass_on(u - NEAR_LAG - FAR_LAG).start()
        yield
    to_mirror().wait_send()

    @pl.when(jnp.logical_not(mine))
    def _():
        to_partner().wait_send()
    for u in range(8):
        passed(u).wait_recv()
        pass_on(u).wait_send()
        if u:
            z_copy(0, u).wait_send()
        near_copy(0, u).wait_send()
        near_copy(1, u).wait_send()
        far_copy(u).wait_send()
    yield


def dot(a, b, over=((1,), (0,))):
    return lax.dot_general(a, b, (over, ((), ())), preferred_element_type=jnp.float32)


def head_stack(rows, head_mask):
    return jnp.concatenate([rows * head_mask[h:h + 1] for h in range(EH)], axis=0)


def head_pick(stack, head_mask):
    rows = stack.shape[0] // EH
    total = jnp.zeros((rows, stack.shape[1]), jnp.float32)
    for h in range(EH):
        total = total + stack[h * rows:(h + 1) * rows] * head_mask[h:h + 1].astype(jnp.float32)
    return total


def query_copy(queries, send_sem, recv_sem, offset):
    x, y, z, core = place()
    side = lax.rem(z, 2)
    peer = device(x, y, z + (offset // 2) * (1 - 2 * side), lax.rem(core + offset, 2))
    slot = queries.at[2 * side + core]
    return remote(slot, slot, send_sem.at[offset - 1], recv_sem.at[offset - 1], peer)


def reduce_peers():
    x, y, z, core = place()
    peers = [device(x, y, z, 1 - core)]
    for step in range(1, 4):
        for other in range(2):
            peers.append(device(x, lax.rem(y + step, 4), z, other))
            peers.append(device(lax.rem(x + step, 4), y, z, other))
    for step in range(1, 8):
        peers.append(device(x, y, lax.rem(z + step, 8), core))
    return peers


def reduce_steps(grads, out, from_core, chip_sum, from_near, plane_sum, from_z, from_cross, total,
                 core_send, core_recv, near_send, near_recv, z_send, z_recv, cross_send, cross_recv,
                 last_send, last_recv):
    x, y, z, core = place()
    y_hi = y // 2
    partner = device(x, y, z, 1 - core)
    spots = (y, x)
    low = jnp.bfloat16

    def along(axis, step):
        if axis == 0:
            return device(x, lax.rem(y + step, 4), z, core)
        return device(lax.rem(x + step, 4), y, z, core)

    def part(v, d):
        return lax.rem(spots[v] + d, 4)

    def core_copy(v, d):
        return remote(grads.at[1 - core, v, part(v, d)], from_core.at[v, d],
                      core_send.at[v, d], core_recv.at[v, d], partner)

    def near_copy(v, d, h):
        return remote(chip_sum.at[v, d - 1, h], from_near.at[v, d - 1, h],
                      near_send.at[v, d - 1, h], near_recv.at[v, d - 1, h], along(v, d))

    def z_copy(v, d):
        to_z = lax.rem(z + d, 8)
        return remote(plane_sum.at[v, lax.rem(to_z, 2), to_z // 2], from_z.at[v, d],
                      z_send.at[v, d], z_recv.at[v, d], device(x, y, to_z, core))

    def cross_copy(v, d):
        slot = spots[1 - v]
        return remote(from_cross.at[v, slot], from_cross.at[v, slot],
                      cross_send.at[v, d - 1], cross_recv.at[v, d - 1], along(1 - v, d))

    def cross_arrival(v, d):
        slot = lax.rem(spots[1 - v] + 4 - d, 4)
        return remote(from_cross.at[v, slot], from_cross.at[v, slot],
                      cross_send.at[v, d - 1], cross_recv.at[v, d - 1], partner)

    def last_copy(v, i):
        peer = device(x, 2 * core + i, z, 0) if v == 0 else device(i, y, z, 1)
        slot = spots[v]
        return remote(total.at[v], out.at[slot], last_send.at[v, i], last_recv.at[slot], peer)

    def last_self(v, i):
        if v == 0:
            return jnp.logical_and(2 * core + i == y, core == 0)
        return jnp.logical_and(i == x, core == 1)

    for j in GRAD_ORDER:
        for v in range(2):
            core_copy(v, lax.rem(j - spots[v] + 4, 4)).start()
        yield
    for h in range(2):
        for d in (2, 1, 3):
            for v in range(2):
                if h == 0:
                    core_copy(v, d).wait_recv()

                def add(k, carry, v=v, d=d, h=h):
                    chip_sum[v, d - 1, h, k] = (
                        grads[core, v, part(v, d), 2 * k + h].astype(jnp.float32)
                        + from_core[v, d, 2 * k + h].astype(jnp.float32)
                    ).astype(low)
                    return carry
                lax.fori_loop(0, 4, add, 0)
                near_copy(v, d, h).start()
        yield
    for h in range(2):
        for v in range(2):
            if h == 0:
                core_copy(v, 0).wait_recv()
            for d in range(1, 4):
                near_copy(v, d, h).wait_recv()

            def add(k, carry, v=v, h=h):
                sums = (grads[core, v, spots[v], 2 * k + h].astype(jnp.float32)
                        + from_core[v, 0, 2 * k + h].astype(jnp.float32))
                for d in range(3):
                    sums = sums + from_near[v, d, h, k].astype(jnp.float32)
                plane_sum[v, h, k] = sums.astype(low)
                return carry
            lax.fori_loop(0, 4, add, 0)
            for m in (2, 1, 3, 0):
                step = 2 * m + lax.rem(h + z, 2)

                @pl.when(step != 0)
                def _(v=v, step=step):
                    z_copy(v, step).start()
        yield
    for v in range(2):
        for d in range(1, 8):
            z_copy(v, d).wait_recv()
        sums = plane_sum[v, lax.rem(z, 2), z // 2].astype(jnp.float32)
        for d in range(1, 8):
            sums = sums + from_z[v, d].astype(jnp.float32)
        from_cross[v, spots[1 - v]] = sums.astype(low)
        for d in (2, 1, 3):
            cross_copy(v, d).start()
    yield
    for v in range(2):
        for d in range(1, 4):
            cross_arrival(v, d).wait_recv()
        terms = [from_cross[v, k].astype(jnp.float32) for k in range(4)]
        total[v] = ((terms[0] + terms[1]) + (terms[2] + terms[3])).astype(low)
        for i in range(2 if v == 0 else 4):
            active = True if v == 0 else y_hi == core

            @pl.when(jnp.logical_and(active, jnp.logical_not(last_self(v, i))))
            def _(v=v, i=i):
                last_copy(v, i).start()

            @pl.when(jnp.logical_and(active, last_self(v, i)))
            def _(v=v):
                out[spots[v]] = total[v]
    yield
    for j in range(4):
        skip = jnp.where(core == 0, jnp.logical_and(j == y, y_hi == 0),
                         jnp.logical_and(j == x, y_hi == 1))

        @pl.when(jnp.logical_not(skip))
        def _(j=j):
            remote(out.at[j], out.at[j], last_send.at[0, 0], last_recv.at[j], partner).wait_recv()
    for v in range(2):
        for d in range(4):
            core_copy(v, d).wait_send()
        for d in range(1, 4):
            near_copy(v, d, 0).wait_send()
            near_copy(v, d, 1).wait_send()
            cross_copy(v, d).wait_send()
        for d in range(1, 8):
            z_copy(v, d).wait_send()
        for i in range(2 if v == 0 else 4):
            active = True if v == 0 else y_hi == core

            @pl.when(jnp.logical_and(active, jnp.logical_not(last_self(v, i))))
            def _(v=v, i=i):
                last_copy(v, i).wait_send()


def reduce_scratch():
    dma = pltpu.SemaphoreType.DMA
    block = (40, 640)
    low = jnp.bfloat16
    return [
        pltpu.VMEM((2, 4, 8) + block, low),
        pltpu.VMEM((2, 3, 2, 4) + block, low),
        pltpu.VMEM((2, 3, 2, 4) + block, low),
        pltpu.VMEM((2, 2, 4) + block, low),
        pltpu.VMEM((2, 8) + block, low),
        pltpu.VMEM((2, 4) + block, low),
        pltpu.VMEM((2,) + block, low),
        dma((2, 4)), dma((2, 4)), dma((2, 3, 2)), dma((2, 3, 2)), dma((2, 8)), dma((2, 8)),
        dma((2, 3)), dma((2, 3)), dma((2, 4)), dma((4,)),
    ]


def attended_steps(partial, out, from_core, chip_sum, from_y, group_sum, from_z,
                   core_send, core_recv, y_send, y_recv, z_send, z_recv):
    x, y, z, core = place()
    y_hi = y // 2
    partner = device(x, y, z, 1 - core)
    across = device(x, lax.rem(y + 2, 4), z, core)
    order = (4, 3, 5, 2, 6, 1, 7, 0)

    def spot(d):
        return lax.rem(z + d, 8)

    def core_copy(half, d):
        row = y_hi if half else 1 - y_hi
        return remote(partial.at[row * 16 + spot(d) * 2 + 1 - core], from_core.at[half, d],
                      core_send.at[half, d], core_recv.at[half, d], partner)

    def y_copy(d):
        return remote(chip_sum.at[d], from_y.at[d], y_send.at[d], y_recv.at[d], across)

    def z_copy(d):
        return remote(group_sum.at[d], from_z.at[d], z_send.at[d], z_recv.at[d],
                      device(x, y, spot(d), core))

    for half in range(2):
        for d in order:
            core_copy(half, d).start()
    yield
    for d in order:
        core_copy(0, d).wait_recv()
        chip_sum[d] = (partial[(1 - y_hi) * 16 + spot(d) * 2 + core].astype(jnp.float32)
                       + from_core[0, d].astype(jnp.float32)).astype(jnp.bfloat16)
        y_copy(d).start()
    yield
    for d in order:
        core_copy(1, d).wait_recv()
        y_copy(d).wait_recv()
        sums = (partial[y_hi * 16 + spot(d) * 2 + core].astype(jnp.float32)
                + from_core[1, d].astype(jnp.float32) + from_y[d].astype(jnp.float32))
        if d:
            group_sum[d] = sums.astype(jnp.bfloat16)
            z_copy(d).start()
        else:
            out[...] = sums
        if d == 2:
            yield
    yield
    sums = out[...]
    for d in range(1, 8):
        z_copy(d).wait_recv()
        sums = sums + from_z[d].astype(jnp.float32)
    out[...] = sums
    for d in range(8):
        core_copy(0, d).wait_send()
        core_copy(1, d).wait_send()
        y_copy(d).wait_send()
        if d:
            z_copy(d).wait_send()


def attended_scratch():
    dma = pltpu.SemaphoreType.DMA
    block = (128, 256)
    return [
        pltpu.VMEM((2, 8) + block, jnp.bfloat16),
        pltpu.VMEM((8,) + block, jnp.bfloat16),
        pltpu.VMEM((8,) + block, jnp.bfloat16),
        pltpu.VMEM((8,) + block, jnp.bfloat16),
        pltpu.VMEM((8,) + block, jnp.bfloat16),
        dma((2, 8)), dma((2, 8)), dma((8,)), dma((8,)), dma((8,)), dma((8,)),
    ]


NEAREST = ((0, 0), (1, 0), (0, 1), (1, 1), (2, 0), (2, 1), (3, 0), (3, 1))


def image_at(step, turn):
    x, y, z, core = place()
    from_z = lax.rem(z + (2 * lax.rem(z, 2) - 1) * step + 8, 8)
    return lax.rem(y // 2 + turn, 2) * 16 + from_z * 2 + core


def exchange_steps(kv, arrived, local_sem, far_send, far_recv):
    x, y, z, core = place()

    def far_copy(step, turn):
        to_y = lax.rem(y + 2 * turn, 4)
        to_z = lax.rem(z + step * (1 - 2 * lax.rem(z + step, 2)) + 8, 8)
        head = (to_y // 2) * 4 + to_z // 2
        return remote(kv.at[head], arrived.at[turn, step], far_send.at[turn, step],
                      far_recv.at[turn, step], device(x, to_y, to_z, core))

    own = pltpu.make_async_copy(kv.at[(y // 2) * 4 + z // 2], arrived.at[0, 0], local_sem)
    own.start()
    for step, turn in reversed(NEAREST):
        if step or turn:
            far_copy(step, turn).start()
    yield
    for step, turn in NEAREST:
        if step or turn:
            far_copy(step, turn).wait_recv()
        else:
            own.wait()
        yield
    for step, turn in NEAREST:
        if step or turn:
            far_copy(step, turn).wait_send()


def exchange_scratch():
    dma = pltpu.SemaphoreType.DMA
    return [dma(()), dma((2, 4)), dma((2, 4))]


def tables():
    lane = np.arange(640)
    row = np.arange(1280)
    head_mask = (lane[None] // 80 == np.arange(8)[:, None])
    pick = (row[:, None] // 40 * 20 + row[:, None] % 20) == lane[None]
    half_mask = (row[None] % 40 // 20) == np.arange(2)[:, None]
    return tuple(jnp.asarray(a, jnp.bfloat16) for a in (head_mask, pick, half_mask))


def load_blocks(text, query_weight, texts, weights, sem):
    def start(k, carry):
        columns = pl.ds(pl.multiple_of(k * 256, 256), 256)
        pltpu.make_async_copy(text.at[:, columns], texts.at[k], sem.at[0]).start()
        return carry
    pltpu.make_async_copy(query_weight, weights, sem.at[1]).start()
    lax.fori_loop(0, 32, start, 0)


def step_kernel(count_ref, length_ref, gate_ref, patches, cotangent, gain, qkv_shard, out_shard, kv_shard,
                mask_ids, head_mask, pick, half_mask, text, query_weight, output_weight,
                sums, result_out,
                joint, joint_full, kv_full, joint_pair, kv_pair, texts, weights, kv, queries, normed, qkv,
                probs_ref, spread, arrived, scores, grads, head_rows, grad_rows, attended, text_in,
                part_out, part_in, stat_out, stat_in, part_send, part_recv, stat_send, stat_recv,
                query_send, query_recv, load_sem, *rest):
    a = len(gather_scratch())
    b = a + len(exchange_scratch())
    c = b + len(reduce_scratch())
    low = jnp.bfloat16
    x, y, z, core = place()
    side = lax.rem(z, 2)
    for part in range(3):
        joint[part] = qkv_shard[:, part * 640:(part + 1) * 640]
    shard = out_shard[...].astype(jnp.float32)
    joint[3] = jnp.concatenate([shard[:, :640], shard[:, 640:]], axis=0).astype(low)
    meet(step_peers())
    first = gather_steps(0, joint, joint_full, joint_pair, *rest[:a])
    second = gather_steps(1, kv_shard, kv_full, kv_pair, *rest[:a])
    exchange = exchange_steps(kv, arrived, *rest[a:b])
    reduce = reduce_steps(grads, sums, *rest[b:c])
    partial = texts
    attend = attended_steps(partial, attended, *rest[c:])
    next(first)
    next(second)
    load_blocks(text, query_weight, texts, weights, load_sem)
    columns = pl.ds(pl.multiple_of(lax.axis_index("fsdp") * 256, 256), 256)
    load_text = pltpu.make_async_copy(text.at[:, columns], text_in, load_sem.at[2])
    load_text.start()

    next(first)
    inputs = patches[...].astype(jnp.float32)
    rows = inputs.shape[0]
    centred = inputs - jnp.mean(inputs, axis=-1, keepdims=True)
    variance = jnp.mean(centred * centred, axis=-1, keepdims=True)
    normed[...] = (centred * lax.rsqrt(variance + EPS) * gain[...].reshape(1, -1)).astype(low)
    next(first)
    pltpu.make_async_copy(texts, texts, load_sem.at[0]).wait()
    pltpu.make_async_copy(query_weight, weights, load_sem.at[1]).wait()
    total = jnp.zeros(queries.shape[1:], jnp.float32)
    steps = 6 + NEAR_LAG + FAR_LAG
    for step in range(steps):
        if step < 8:
            for k in range(4 * step, 4 * step + 4):
                total = total + dot(texts[k], weights[k])
        if step == 8:
            queries[2 * side + core] = total.astype(low)
            for offset in range(1, 4):
                query_copy(queries, query_send, query_recv, offset).start()

            def start(k, carry):
                block = pl.ds(pl.multiple_of(k * 256, 256), 256)
                pltpu.make_async_copy(output_weight.at[:, block], weights.at[k], load_sem.at[1]).start()
                return carry
            lax.fori_loop(0, 32, start, 0)
        next(first)
        if step >= LAG:
            next(second, None)
    next(first, None)

    masks = head_mask[...]
    next(second, None)
    query = dot(normed[...], joint_full[0].reshape(1280, 640)).astype(low)
    qkv[0] = query
    next(second, None)
    key = dot(normed[...], joint_full[1].reshape(1280, 640)).astype(low)
    qkv[1] = key
    next(second, None)
    value = dot(normed[...], joint_full[2].reshape(1280, 640)).astype(low)
    qkv[2] = value
    next(second, None)
    live_key = lax.broadcasted_iota(jnp.int32, (1, rows), 1) < count_ref[0] * PATCH
    live_row = lax.broadcasted_iota(jnp.int32, (rows, 1), 0) < count_ref[0] * PATCH
    head_rows[...] = head_stack(query, masks)
    inner_scores = dot(head_rows[...], key, ((1,), (1,))) * EHD ** (-0.5)
    inner_scores = jnp.where(live_key, inner_scores, NEG)
    shares = jnp.exp(inner_scores - jnp.max(inner_scores, axis=-1, keepdims=True))
    probs_ref[...] = shares / jnp.sum(shares, axis=-1, keepdims=True)
    next(second, None)
    context = head_pick(dot(probs_ref[...].astype(low), qkv[2]), masks).astype(low)
    both = dot(context, pick[...], ((1,), (1,))).astype(low)
    spread[...] = jnp.concatenate([both * half_mask[0:1], both * half_mask[1:2]], axis=0)
    next(second, None)
    branch = dot(spread[...], joint_full[3].reshape(1280, 640))
    branch = jnp.concatenate([branch[:rows], branch[rows:]], axis=1)
    vision = jnp.where(live_row, patches[...].astype(jnp.float32) + branch, 0.0).astype(low)
    next(second, None)

    upstream = jnp.where(live_row, cotangent[...].astype(jnp.float32), 0.0).astype(low)
    sides = jnp.concatenate([upstream[:, :640], upstream[:, 640:]], axis=0)
    backs = dot(sides, joint_full[3].reshape(1280, 640), ((1,), (1,)))
    backs = (backs[:rows] * half_mask[0:1].astype(jnp.float32)
             + backs[rows:] * half_mask[1:2].astype(jnp.float32))
    high = backs.astype(low)
    rest_low = (backs - high.astype(jnp.float32)).astype(low)
    picked = dot(jnp.concatenate([high, rest_low], axis=0), pick[...])
    grad_context = (picked[:rows] + picked[rows:]).astype(low)
    grad_rows[...] = head_stack(grad_context, masks)
    next(second, None)

    def project_kv():
        for part in range(4):
            piece = dot(vision, kv_full[part].reshape(1280, 512)).astype(low)
            for half in range(2):
                kv[2 * part + half, pl.ds(0, rows), :] = piece[:, half * 256:(half + 1) * 256]
        number = jnp.full((KVH, 16, 256), count_ref[0].astype(jnp.float32)).astype(low)
        kv[:, pl.ds(rows, 16), :] = number
        next(exchange)

    if KV_AT == 0:
        for _ in second:
            pass
        project_kv()
    probs = probs_ref[...]
    grad_probs = dot(grad_rows[...], qkv[2], ((1,), (1,)))
    inner = jnp.sum(probs * grad_probs, axis=-1, keepdims=True)
    grad_scores = (probs * (grad_probs - inner) * EHD ** (-0.5)).astype(low)
    next(second, None)
    grad_values = dot(probs.astype(low).T, grad_rows[...]).astype(low)
    grad_keys = dot(grad_scores.T, head_rows[...]).astype(low)
    grad_queries = head_pick(dot(grad_scores, qkv[1]), masks).astype(low)
    if KV_AT == 1:
        for _ in second:
            pass
        project_kv()

    def store(j, left, right):
        for upper in range(2):
            block = dot(left[640 * upper:640 * (upper + 1)], right)
            for k in range(8):
                for other in range(2):
                    at = 80 * k + 40 * other
                    grads[upper, other, j, k] = block[at:at + 40].astype(low)

    store(3, spread[...].T, sides)
    next(reduce)
    normed_t = normed[...].T
    for j, right in enumerate((grad_queries, grad_keys, grad_values)):
        store(j, normed_t, right)
        next(reduce)
        next(second, None)
    next(reduce)
    next(reduce)
    if KV_AT == 2:
        for _ in second:
            pass
        project_kv()

    for offset in range(1, 4):
        query_copy(queries, query_send, query_recv, offset).wait()
    text_rows = queries.shape[1]
    stacked = jnp.concatenate(
        [queries[g, :, half * HD:(half + 1) * HD] for g in range(4) for half in range(2)], axis=0)
    square = (text_rows, text_rows)
    diagonal = (lax.broadcasted_iota(jnp.int32, square, 0) == lax.broadcasted_iota(jnp.int32, square, 1))
    images = jnp.sum(jnp.where(diagonal, mask_ids[...].astype(jnp.float32).reshape(1, text_rows), 0.0),
                     axis=1, keepdims=True)
    images = jnp.concatenate([images] * 8, axis=0)
    tile_of = lax.broadcasted_iota(jnp.int32, (1, rows), 1).astype(jnp.float32)
    top = jnp.full((8 * text_rows, 1), NEG, jnp.float32)
    for i, (step, turn) in enumerate(NEAREST):
        if i == REDUCE_AT:
            next(reduce)
        next(exchange)
        counts = arrived[turn, step, pl.ds(rows, 16), pl.ds(0, 128)][0:1].astype(jnp.float32)
        number = image_at(step, turn).astype(jnp.float32)
        allowed = jnp.logical_and(tile_of < counts * float(PATCH), number < images)
        piece = dot(stacked, arrived[turn, step, pl.ds(0, rows), pl.ds(0, HD)], ((1,), (1,)))
        piece = jnp.where(allowed, piece * HD ** (-0.5), NEG)
        scores[:, i * 128:(i + 1) * 128] = piece
        top = jnp.maximum(top, jnp.max(piece, axis=-1, keepdims=True))
    total = jnp.zeros((8 * text_rows, 1), jnp.float32)
    context = jnp.zeros((8 * text_rows, HD), jnp.float32)
    for i, (step, turn) in enumerate(NEAREST):
        piece = jnp.exp(scores[:, i * 128:(i + 1) * 128] - top)
        total = total + jnp.sum(piece, axis=-1, keepdims=True)
        context = context + dot(piece.astype(low), arrived[turn, step, pl.ds(0, rows), pl.ds(HD, HD)])
    context = context / total
    total = jnp.where(top > 0.5 * NEG, total, 0.0)
    for _ in exchange:
        pass
    scores[:, 0:128] = context
    lane = lax.broadcasted_iota(jnp.int32, (1, 128), 1)
    scores[:, 128:256] = jnp.where(lane < 4, top, total)

    def own_rows(group):
        return pl.ds(pl.multiple_of(group * 2 * text_rows, 256), 2 * text_rows)

    def merge_copy(offset, out, into, send_sem, recv_sem):
        peer = device(x, y, z + (offset // 2) * (1 - 2 * side), lax.rem(core + offset, 2))
        return remote(out.at[offset - 1], into.at[offset - 1], send_sem.at[offset - 1],
                      recv_sem.at[offset - 1], peer)

    def context_copy(offset):
        return merge_copy(offset, part_out, part_in, part_send, part_recv)

    def stat_copy(offset):
        return merge_copy(offset, stat_out, stat_in, stat_send, stat_recv)

    for offset in (2, 3, 1):
        group = 2 * lax.rem(side + offset // 2, 2) + lax.rem(core + offset, 2)
        part_out[offset - 1] = scores[own_rows(group), 0:128].astype(low)
        context_copy(offset).start()
        stat_out[offset - 1] = scores[own_rows(group), 128:256].T[0:8]
        stat_copy(offset).start()
    if REDUCE_AT == 8:
        next(reduce)
    group = 2 * side + core
    parts = [scores[own_rows(group), 0:128]]
    tops = [scores[own_rows(group), 128:129]]
    totals = [scores[own_rows(group), 132:133]]
    for offset in range(1, 4):
        context_copy(offset).wait_recv()
        stat_copy(offset).wait_recv()
        stats = jnp.concatenate([stat_in[offset - 1]] * 16, axis=0).T
        parts.append(part_in[offset - 1].astype(jnp.float32))
        tops.append(stats[:, 0:1])
        totals.append(stats[:, 4:5])
    top = jnp.maximum(jnp.maximum(tops[0], tops[1]), jnp.maximum(tops[2], tops[3]))
    seen = jnp.zeros((2 * text_rows, 1), jnp.float32)
    context = jnp.zeros((2 * text_rows, HD), jnp.float32)
    for k in range(4):
        share = totals[k] * jnp.exp(tops[k] - top)
        seen = seen + share
        context = context + share * parts[k]
    context = (context / jnp.where(seen > 0.0, seen, 1.0)).astype(low)
    context = jnp.concatenate([context[:text_rows], context[text_rows:]], axis=1)
    pltpu.make_async_copy(weights, weights, load_sem.at[1]).wait()

    def project(block, carry):
        partial[block] = dot(context, weights[block]).astype(low)
        return carry
    lax.fori_loop(0, 32, project, 0)
    next(attend)
    next(attend)
    next(reduce)
    next(attend)
    next(reduce)
    next(attend)
    next(reduce)
    for _ in attend:
        pass
    for _ in reduce:
        pass
    for offset in range(1, 4):
        context_copy(offset).wait_send()
        stat_copy(offset).wait_send()
    rows_live = jnp.logical_and(
        seen[:text_rows] > 0.0,
        lax.broadcasted_iota(jnp.int32, (text_rows, 1), 0) < length_ref[0])
    gate = jnp.tanh(jnp.full((1, 256), gate_ref[0], jnp.float32))
    load_text.wait()
    result_out[...] = (text_in[...].astype(jnp.float32)
                       + gate * jnp.where(rows_live, attended[...], 0.0)).astype(low)


def step_peers():
    x, y, z, core = place()
    peers = reduce_peers()
    for step in range(1, 8):
        peers.append(device(x, lax.rem(y + 2, 4), lax.rem(z + step, 8), core))
    peers.append(device(x, y, z + 1 - 2 * lax.rem(z, 2), 1 - core))
    return peers


def whole_step(*operands):
    dma = pltpu.SemaphoreType.DMA
    vmem = pl.BlockSpec(memory_space=pltpu.VMEM)
    smem = pl.BlockSpec(memory_space=pltpu.SMEM)
    low = jnp.bfloat16
    rows = operands[3].shape[0]
    text = operands[13].shape[0]
    return pl.pallas_call(
        step_kernel,
        out_shape=(jax.ShapeDtypeStruct((4, 40, 640), low),
                   jax.ShapeDtypeStruct((text, 256), low)),
        in_specs=[smem] * 3 + [vmem] * 10 + [pl.BlockSpec(memory_space=pl.ANY)] * 3,
        out_specs=[vmem] * 2,
        scratch_shapes=[
            pltpu.VMEM((4, 40, 640), low), pltpu.VMEM((4, 2, 8, 80, 640), low),
            pltpu.VMEM((4, 2, 8, 80, 512), low), pltpu.VMEM((2, 40, 640), low),
            pltpu.VMEM((2, 40, 512), low), pltpu.VMEM((32, text, 256), low),
            pltpu.VMEM((32, 256, 256), low), pltpu.VMEM((KVH, rows + 16, 256), low),
            pltpu.VMEM((4, text, 256), low), pltpu.VMEM((rows, 1280), low),
            pltpu.VMEM((3, rows, 640), low), pltpu.VMEM((EH * rows, rows), jnp.float32),
            pltpu.VMEM((2 * rows, 1280), low), pltpu.VMEM((2, 4, rows + 16, 256), low),
            pltpu.VMEM((8 * text, 8 * 128), jnp.float32), pltpu.VMEM((2, 2, 4, 8, 40, 640), low),
            pltpu.VMEM((EH * rows, 640), low), pltpu.VMEM((EH * rows, 640), low),
            pltpu.VMEM((text, 256), jnp.float32), pltpu.VMEM((text, 256), low),
            pltpu.VMEM((3, 2 * text, HD), low), pltpu.VMEM((3, 2 * text, HD), low),
            pltpu.VMEM((3, 8, 2 * text), jnp.float32), pltpu.VMEM((3, 8, 2 * text), jnp.float32),
            dma((3,)), dma((3,)), dma((3,)), dma((3,)), dma((3,)), dma((3,)), dma((3,)),
        ] + gather_scratch() + exchange_scratch() + reduce_scratch() + attended_scratch(),
        compiler_params=pltpu.CompilerParams(
            collective_id=0, has_side_effects=True, vmem_limit_bytes=63 * 2**20),
        name="whole_step",
    )(*operands)


def result_kernel(sums, result, qkv_out, out_out, result_out):
    for j in range(3):
        qkv_out[:, j * 640:(j + 1) * 640] = sums[j].astype(jnp.float32)
    last = sums[3].astype(jnp.float32)
    out_out[:, 0:640] = last[0:20]
    out_out[:, 640:1280] = last[20:40]
    result_out[...] = result[...]


def write_results(sums, result):
    vmem = pl.BlockSpec(memory_space=pltpu.VMEM)
    return pl.pallas_call(
        result_kernel,
        out_shape=(jax.ShapeDtypeStruct((40, 1920), jnp.float32),
                   jax.ShapeDtypeStruct((20, 1280), jnp.float32),
                   jax.ShapeDtypeStruct(result.shape, result.dtype)),
        in_specs=[vmem] * 2,
        out_specs=[vmem] * 3,
        name="write_results",
    )(sums, result)


def per_device(
    patches,
    cotangent,
    tile_counts,
    ln_gain,
    qkv_weight,
    out_weight,
    text_states,
    mask_ids,
    text_lengths,
    gate_value,
    query_weight,
    kv_weight,
    output_weight,
):
    head_mask, pick, half_mask = tables()
    sums, result = whole_step(
        tile_counts, text_lengths, gate_value, patches, cotangent, ln_gain, qkv_weight, out_weight,
        kv_weight, mask_ids, head_mask, pick, half_mask, text_states,
        query_weight.reshape(32, 256, 256), output_weight)
    return write_results(sums, result)


def solution(mesh):
    placed = (
        P(("dp", "fsdp"), None),
        P(("dp", "fsdp"), None),
        P(("dp", "fsdp")),
        P(),
        P("fsdp", None),
        P("fsdp", None),
        P("dp", None),
        P("dp"),
        P("dp"),
        P(),
        P(None, "fsdp"),
        P("fsdp", None),
        P("fsdp", None),
    )
    return jax.shard_map(
        per_device,
        mesh=mesh,
        in_specs=placed,
        out_specs=(P("fsdp", None), P("fsdp", None), P("dp", "fsdp")),
        check_vma=False,
    )
```

```python
import jax
import jax.numpy as jnp
import numpy as np
from jax import lax
from jax.sharding import PartitionSpec as P
from jax.experimental import pallas as pl
from jax.experimental.pallas import tpu as pltpu

EH = 8
EHD = 80
PATCH = 32
HD = 128
KVH = 8
LAG = 0
NEAR_LAG = 3
FAR_LAG = 3
KV_AT = 0
REDUCE_AT = 8
GRAD_ORDER = (3, 0, 1, 2)

EPS = 1e-05
NEG = -1e30

MESH = pl.DeviceIdType.MESH


def place():
    dp = lax.axis_index("dp")
    f = lax.axis_index("fsdp")
    x = lax.rem(dp, 4)
    y = (f // 16) * 2 + dp // 4
    z = lax.rem(f // 2, 8)
    return x, y, z, lax.rem(f, 2)


def device(x, y, z, core):
    return (lax.rem(y, 2) * 4 + x, (y // 2) * 16 + z * 2 + core)


def meet(peers):
    barrier = pltpu.get_barrier_semaphore()
    for peer in peers:
        pl.semaphore_signal(barrier, inc=1, device_id=peer, device_id_type=MESH)
    pl.semaphore_wait(barrier, len(peers))


def remote(src, dst, send_sem, recv_sem, peer):
    return pltpu.make_async_remote_copy(
        src_ref=src, dst_ref=dst, send_sem=send_sem, recv_sem=recv_sem,
        device_id=peer, device_id_type=MESH,
    )


def gather_scratch():
    dma = pltpu.SemaphoreType.DMA
    return [
        dma((2, 2)), dma((2, 2)), dma((2, 8)), dma((2, 8)),
        dma((2, 2, 8)), dma((2, 2, 8)), dma((2, 8)), dma((2, 8)), dma((2, 8)), dma((2, 8)),
    ]


def gather_steps(t, shard, full, pair, init_send, init_recv, z_send, z_recv, near_send, near_recv,
                 far_send, far_recv, core_send, core_recv):
    x, y, z, core = place()
    y_hi = y // 2
    partner = device(x, y, z, 1 - core)
    width = pair.shape[2]
    sign = 1 - 2 * t
    mine = core == y_hi

    def turned(where):
        return lax.rem(where + t, 2)

    def spot_at(where, my_y):
        return my_y + turned(where) * (x - my_y)

    def columns(spot):
        if t == 0:
            return shard.at[spot]
        return shard.at[:, pl.ds(pl.multiple_of(spot * width, 128), width)]

    def unit_z(u):
        d = (u + 1) // 2 if u % 2 else -(u // 2)
        return lax.rem(z - sign * d + 8, 8)

    def along_z(step):
        return device(x, y, lax.rem(z + step + 8, 8), core)

    def along(where, step):
        by_x = turned(where)
        return device(lax.rem(x + by_x * step + 4, 4), lax.rem(y + (1 - by_x) * step + 4, 4), z, core)

    def unit(u, d):
        where = unit_z(u)
        return full.at[lax.rem(spot_at(where, y) + d, 4), core, where]

    def to_partner():
        return remote(columns(spot_at(z, y)), pair.at[core], init_send.at[t, 0],
                      init_recv.at[t, core], partner)

    def to_mirror():
        return remote(columns(spot_at(z, 3 - y)), pair.at[core], init_send.at[t, 1],
                      init_recv.at[t, core], device(x, 3 - y, z, y_hi))

    def own_copy():
        return pltpu.make_async_copy(columns(spot_at(z, y)), pair.at[core], init_send.at[t, 0])

    def from_core(other):
        return remote(pair.at[other], pair.at[other], init_send.at[t, 0], init_recv.at[t, other], partner)

    def z_copy(u, u_next):
        src = unit(u, 0)
        step = sign if u_next % 2 else -sign
        return remote(src, src, z_send.at[t, u_next], z_recv.at[t, u_next], along_z(step))

    def near_copy(side, u):
        src = unit(u, 0)
        return remote(src, src, near_send.at[t, side, u], near_recv.at[t, side, u],
                      along(unit_z(u), 1 - 2 * side))

    def near_arrival(side, u):
        dst = unit(u, 3 - 2 * side)
        return remote(dst, dst, near_send.at[t, side, u], near_recv.at[t, side, u], partner)

    def far_copy(u):
        where = unit_z(u)
        back = lax.rem(where // 2, 2)
        src = unit(u, 3 - 2 * back)
        return remote(src, src, far_send.at[t, u], far_recv.at[t, u], along(where, 1 - 2 * back))

    def far_arrival(u):
        dst = unit(u, 2)
        return remote(dst, dst, far_send.at[t, u], far_recv.at[t, u], partner)

    def pass_on(u):
        src = full.at[:, core, unit_z(u)]
        return remote(src, src, core_send.at[t, u], core_recv.at[t, u], partner)

    def passed(u):
        dst = full.at[:, 1 - core, unit_z(u)]
        return remote(dst, dst, core_send.at[t, u], core_recv.at[t, u], partner)

    to_mirror().start()

    @pl.when(mine)
    def _():
        own_copy().start()

    @pl.when(jnp.logical_not(mine))
    def _():
        to_partner().start()
    yield
    for u in range(8 + NEAR_LAG + FAR_LAG):
        if u == 0:
            @pl.when(mine)
            def _():
                own_copy().wait()
                from_core(1 - core).wait_recv()

            @pl.when(jnp.logical_not(mine))
            def _():
                from_core(0).wait_recv()
                from_core(1).wait_recv()
            both = jnp.concatenate([pair[0].astype(jnp.float32), pair[1].astype(jnp.float32)], axis=0)
            full[spot_at(z, y), core, z] = both.astype(jnp.bfloat16)
            z_copy(0, 1).start()
            z_copy(0, 2).start()
        elif u < 8:
            z_copy(u, u).wait_recv()
            if u + 2 < 8:
                z_copy(u, u + 2).start()
        if u < 8:
            near_copy(0, u).start()
            near_copy(1, u).start()
        if 0 <= u - NEAR_LAG < 8:
            for side in range(2):
                near_arrival(side, u - NEAR_LAG).wait_recv()
            far_copy(u - NEAR_LAG).start()
        if 0 <= u - NEAR_LAG - FAR_LAG:
            far_arrival(u - NEAR_LAG - FAR_LAG).wait_recv()
            pass_on(u - NEAR_LAG - FAR_LAG).start()
        yield
    to_mirror().wait_send()

    @pl.when(jnp.logical_not(mine))
    def _():
        to_partner().wait_send()
    for u in range(8):
        passed(u).wait_recv()
        pass_on(u).wait_send()
        if u:
            z_copy(0, u).wait_send()
        near_copy(0, u).wait_send()
        near_copy(1, u).wait_send()
        far_copy(u).wait_send()
    yield


def dot(a, b, over=((1,), (0,))):
    return lax.dot_general(a, b, (over, ((), ())), preferred_element_type=jnp.float32)


def head_stack(rows, head_mask):
    return jnp.concatenate([rows * head_mask[h:h + 1] for h in range(EH)], axis=0)


def head_pick(stack, head_mask):
    rows = stack.shape[0] // EH
    total = jnp.zeros((rows, stack.shape[1]), jnp.float32)
    for h in range(EH):
        total = total + stack[h * rows:(h + 1) * rows] * head_mask[h:h + 1].astype(jnp.float32)
    return total


def query_copy(queries, send_sem, recv_sem, offset):
    x, y, z, core = place()
    side = lax.rem(z, 2)
    peer = device(x, y, z + (offset // 2) * (1 - 2 * side), lax.rem(core + offset, 2))
    slot = queries.at[2 * side + core]
    return remote(slot, slot, send_sem.at[offset - 1], recv_sem.at[offset - 1], peer)


def reduce_peers():
    x, y, z, core = place()
    peers = [device(x, y, z, 1 - core)]
    for step in range(1, 4):
        for other in range(2):
            peers.append(device(x, lax.rem(y + step, 4), z, other))
            peers.append(device(lax.rem(x + step, 4), y, z, other))
    for step in range(1, 8):
        peers.append(device(x, y, lax.rem(z + step, 8), core))
    return peers


def reduce_steps(grads, out, from_core, chip_sum, from_near, plane_sum, from_z, from_cross, total,
                 core_send, core_recv, near_send, near_recv, z_send, z_recv, cross_send, cross_recv,
                 last_send, last_recv):
    x, y, z, core = place()
    y_hi = y // 2
    partner = device(x, y, z, 1 - core)
    spots = (y, x)
    low = jnp.bfloat16

    def along(axis, step):
        if axis == 0:
            return device(x, lax.rem(y + step, 4), z, core)
        return device(lax.rem(x + step, 4), y, z, core)

    def part(v, d):
        return lax.rem(spots[v] + d, 4)

    def core_copy(v, d):
        return remote(grads.at[1 - core, v, part(v, d)], from_core.at[v, d],
                      core_send.at[v, d], core_recv.at[v, d], partner)

    def near_copy(v, d, h):
        return remote(chip_sum.at[v, d - 1, h], from_near.at[v, d - 1, h],
                      near_send.at[v, d - 1, h], near_recv.at[v, d - 1, h], along(v, d))

    def z_copy(v, d):
        to_z = lax.rem(z + d, 8)
        return remote(plane_sum.at[v, lax.rem(to_z, 2), to_z // 2], from_z.at[v, d],
                      z_send.at[v, d], z_recv.at[v, d], device(x, y, to_z, core))

    def cross_copy(v, d):
        slot = spots[1 - v]
        return remote(from_cross.at[v, slot], from_cross.at[v, slot],
                      cross_send.at[v, d - 1], cross_recv.at[v, d - 1], along(1 - v, d))

    def cross_arrival(v, d):
        slot = lax.rem(spots[1 - v] + 4 - d, 4)
        return remote(from_cross.at[v, slot], from_cross.at[v, slot],
                      cross_send.at[v, d - 1], cross_recv.at[v, d - 1], partner)

    def last_copy(v, i):
        peer = device(x, 2 * core + i, z, 0) if v == 0 else device(i, y, z, 1)
        slot = spots[v]
        return remote(total.at[v], out.at[slot], last_send.at[v, i], last_recv.at[slot], peer)

    def last_self(v, i):
        if v == 0:
            return jnp.logical_and(2 * core + i == y, core == 0)
        return jnp.logical_and(i == x, core == 1)

    for j in GRAD_ORDER:
        for v in range(2):
            core_copy(v, lax.rem(j - spots[v] + 4, 4)).start()
        yield
    for h in range(2):
        for d in (2, 1, 3):
            for v in range(2):
                if h == 0:
                    core_copy(v, d).wait_recv()

                def add(k, carry, v=v, d=d, h=h):
                    chip_sum[v, d - 1, h, k] = (
                        grads[core, v, part(v, d), 2 * k + h].astype(jnp.float32)
                        + from_core[v, d, 2 * k + h].astype(jnp.float32)
                    ).astype(low)
                    return carry
                lax.fori_loop(0, 4, add, 0)
                near_copy(v, d, h).start()
        yield
    for h in range(2):
        for v in range(2):
            if h == 0:
                core_copy(v, 0).wait_recv()
            for d in range(1, 4):
                near_copy(v, d, h).wait_recv()

            def add(k, carry, v=v, h=h):
                sums = (grads[core, v, spots[v], 2 * k + h].astype(jnp.float32)
                        + from_core[v, 0, 2 * k + h].astype(jnp.float32))
                for d in range(3):
                    sums = sums + from_near[v, d, h, k].astype(jnp.float32)
                plane_sum[v, h, k] = sums.astype(low)
                return carry
            lax.fori_loop(0, 4, add, 0)
            for m in (2, 1, 3, 0):
                step = 2 * m + lax.rem(h + z, 2)

                @pl.when(step != 0)
                def _(v=v, step=step):
                    z_copy(v, step).start()
        yield
    for v in range(2):
        for d in range(1, 8):
            z_copy(v, d).wait_recv()
        sums = plane_sum[v, lax.rem(z, 2), z // 2].astype(jnp.float32)
        for d in range(1, 8):
            sums = sums + from_z[v, d].astype(jnp.float32)
        from_cross[v, spots[1 - v]] = sums.astype(low)
        for d in (2, 1, 3):
            cross_copy(v, d).start()
    yield
    for v in range(2):
        for d in range(1, 4):
            cross_arrival(v, d).wait_recv()
        terms = [from_cross[v, k].astype(jnp.float32) for k in range(4)]
        total[v] = ((terms[0] + terms[1]) + (terms[2] + terms[3])).astype(low)
        for i in range(2 if v == 0 else 4):
            active = True if v == 0 else y_hi == core

            @pl.when(jnp.logical_and(active, jnp.logical_not(last_self(v, i))))
            def _(v=v, i=i):
                last_copy(v, i).start()

            @pl.when(jnp.logical_and(active, last_self(v, i)))
            def _(v=v):
                out[spots[v]] = total[v]
    yield
    for j in range(4):
        skip = jnp.where(core == 0, jnp.logical_and(j == y, y_hi == 0),
                         jnp.logical_and(j == x, y_hi == 1))

        @pl.when(jnp.logical_not(skip))
        def _(j=j):
            remote(out.at[j], out.at[j], last_send.at[0, 0], last_recv.at[j], partner).wait_recv()
    for v in range(2):
        for d in range(4):
            core_copy(v, d).wait_send()
        for d in range(1, 4):
            near_copy(v, d, 0).wait_send()
            near_copy(v, d, 1).wait_send()
            cross_copy(v, d).wait_send()
        for d in range(1, 8):
            z_copy(v, d).wait_send()
        for i in range(2 if v == 0 else 4):
            active = True if v == 0 else y_hi == core

            @pl.when(jnp.logical_and(active, jnp.logical_not(last_self(v, i))))
            def _(v=v, i=i):
                last_copy(v, i).wait_send()


def reduce_scratch():
    dma = pltpu.SemaphoreType.DMA
    block = (40, 640)
    low = jnp.bfloat16
    return [
        pltpu.VMEM((2, 4, 8) + block, low),
        pltpu.VMEM((2, 3, 2, 4) + block, low),
        pltpu.VMEM((2, 3, 2, 4) + block, low),
        pltpu.VMEM((2, 2, 4) + block, low),
        pltpu.VMEM((2, 8) + block, low),
        pltpu.VMEM((2, 4) + block, low),
        pltpu.VMEM((2,) + block, low),
        dma((2, 4)), dma((2, 4)), dma((2, 3, 2)), dma((2, 3, 2)), dma((2, 8)), dma((2, 8)),
        dma((2, 3)), dma((2, 3)), dma((2, 4)), dma((4,)),
    ]


def attended_steps(partial, out, from_core, chip_sum, from_y, group_sum, from_z,
                   core_send, core_recv, y_send, y_recv, z_send, z_recv):
    x, y, z, core = place()
    y_hi = y // 2
    partner = device(x, y, z, 1 - core)
    across = device(x, lax.rem(y + 2, 4), z, core)
    order = (4, 3, 5, 2, 6, 1, 7, 0)

    def spot(d):
        return lax.rem(z + d, 8)

    def core_copy(half, d):
        row = y_hi if half else 1 - y_hi
        return remote(partial.at[row * 16 + spot(d) * 2 + 1 - core], from_core.at[half, d],
                      core_send.at[half, d], core_recv.at[half, d], partner)

    def y_copy(d):
        return remote(chip_sum.at[d], from_y.at[d], y_send.at[d], y_recv.at[d], across)

    def z_copy(d):
        return remote(group_sum.at[d], from_z.at[d], z_send.at[d], z_recv.at[d],
                      device(x, y, spot(d), core))

    for half in range(2):
        for d in order:
            core_copy(half, d).start()
    yield
    for d in order:
        core_copy(0, d).wait_recv()
        chip_sum[d] = (partial[(1 - y_hi) * 16 + spot(d) * 2 + core].astype(jnp.float32)
                       + from_core[0, d].astype(jnp.float32)).astype(jnp.bfloat16)
        y_copy(d).start()
    yield
    for d in order:
        core_copy(1, d).wait_recv()
        y_copy(d).wait_recv()
        sums = (partial[y_hi * 16 + spot(d) * 2 + core].astype(jnp.float32)
                + from_core[1, d].astype(jnp.float32) + from_y[d].astype(jnp.float32))
        if d:
            group_sum[d] = sums.astype(jnp.bfloat16)
            z_copy(d).start()
        else:
            out[...] = sums
        if d == 2:
            yield
    yield
    sums = out[...]
    for d in range(1, 8):
        z_copy(d).wait_recv()
        sums = sums + from_z[d].astype(jnp.float32)
    out[...] = sums
    for d in range(8):
        core_copy(0, d).wait_send()
        core_copy(1, d).wait_send()
        y_copy(d).wait_send()
        if d:
            z_copy(d).wait_send()


def attended_scratch():
    dma = pltpu.SemaphoreType.DMA
    block = (128, 256)
    return [
        pltpu.VMEM((2, 8) + block, jnp.bfloat16),
        pltpu.VMEM((8,) + block, jnp.bfloat16),
        pltpu.VMEM((8,) + block, jnp.bfloat16),
        pltpu.VMEM((8,) + block, jnp.bfloat16),
        pltpu.VMEM((8,) + block, jnp.bfloat16),
        dma((2, 8)), dma((2, 8)), dma((8,)), dma((8,)), dma((8,)), dma((8,)),
    ]


NEAREST = ((0, 0), (1, 0), (0, 1), (1, 1), (2, 0), (2, 1), (3, 0), (3, 1))


def image_at(step, turn):
    x, y, z, core = place()
    from_z = lax.rem(z + (2 * lax.rem(z, 2) - 1) * step + 8, 8)
    return lax.rem(y // 2 + turn, 2) * 16 + from_z * 2 + core


def exchange_steps(kv, arrived, local_sem, far_send, far_recv):
    x, y, z, core = place()

    def far_copy(step, turn):
        to_y = lax.rem(y + 2 * turn, 4)
        to_z = lax.rem(z + step * (1 - 2 * lax.rem(z + step, 2)) + 8, 8)
        head = (to_y // 2) * 4 + to_z // 2
        return remote(kv.at[head], arrived.at[turn, step], far_send.at[turn, step],
                      far_recv.at[turn, step], device(x, to_y, to_z, core))

    own = pltpu.make_async_copy(kv.at[(y // 2) * 4 + z // 2], arrived.at[0, 0], local_sem)
    own.start()
    for step, turn in reversed(NEAREST):
        if step or turn:
            far_copy(step, turn).start()
    yield
    for step, turn in NEAREST:
        if step or turn:
            far_copy(step, turn).wait_recv()
        else:
            own.wait()
        yield
    for step, turn in NEAREST:
        if step or turn:
            far_copy(step, turn).wait_send()


def exchange_scratch():
    dma = pltpu.SemaphoreType.DMA
    return [dma(()), dma((2, 4)), dma((2, 4))]


def tables():
    lane = np.arange(640)
    row = np.arange(1280)
    head_mask = (lane[None] // 80 == np.arange(8)[:, None])
    pick = (row[:, None] // 40 * 20 + row[:, None] % 20) == lane[None]
    half_mask = (row[None] % 40 // 20) == np.arange(2)[:, None]
    return tuple(jnp.asarray(a, jnp.bfloat16) for a in (head_mask, pick, half_mask))


def load_blocks(text, query_weight, texts, weights, sem):
    def start(k, carry):
        columns = pl.ds(pl.multiple_of(k * 256, 256), 256)
        pltpu.make_async_copy(text.at[:, columns], texts.at[k], sem.at[0]).start()
        return carry
    pltpu.make_async_copy(query_weight, weights, sem.at[1]).start()
    lax.fori_loop(0, 32, start, 0)


def step_kernel(count_ref, length_ref, gate_ref, patches, cotangent, gain, qkv_shard, out_shard, kv_shard,
                mask_ids, head_mask, pick, half_mask, text, query_weight, output_weight,
                sums, result_out,
                joint, joint_full, kv_full, joint_pair, kv_pair, texts, weights, kv, queries, normed, qkv,
                probs_ref, spread, arrived, scores, grads, head_rows, grad_rows, attended, text_in,
                part_out, part_in, stat_out, stat_in, part_send, part_recv, stat_send, stat_recv,
                query_send, query_recv, load_sem, *rest):
    a = len(gather_scratch())
    b = a + len(exchange_scratch())
    c = b + len(reduce_scratch())
    low = jnp.bfloat16
    x, y, z, core = place()
    side = lax.rem(z, 2)
    for part in range(3):
        joint[part] = qkv_shard[:, part * 640:(part + 1) * 640]
    shard = out_shard[...].astype(jnp.float32)
    joint[3] = jnp.concatenate([shard[:, :640], shard[:, 640:]], axis=0).astype(low)
    meet(step_peers())
    first = gather_steps(0, joint, joint_full, joint_pair, *rest[:a])
    second = gather_steps(1, kv_shard, kv_full, kv_pair, *rest[:a])
    exchange = exchange_steps(kv, arrived, *rest[a:b])
    reduce = reduce_steps(grads, sums, *rest[b:c])
    partial = texts
    attend = attended_steps(partial, attended, *rest[c:])
    next(first)
    next(second)
    load_blocks(text, query_weight, texts, weights, load_sem)
    columns = pl.ds(pl.multiple_of(lax.axis_index("fsdp") * 256, 256), 256)
    load_text = pltpu.make_async_copy(text.at[:, columns], text_in, load_sem.at[2])
    load_text.start()

    next(first)
    inputs = patches[...].astype(jnp.float32)
    rows = inputs.shape[0]
    centred = inputs - jnp.mean(inputs, axis=-1, keepdims=True)
    variance = jnp.mean(centred * centred, axis=-1, keepdims=True)
    normed[...] = (centred * lax.rsqrt(variance + EPS) * gain[...].reshape(1, -1)).astype(low)
    next(first)
    pltpu.make_async_copy(texts, texts, load_sem.at[0]).wait()
    pltpu.make_async_copy(query_weight, weights, load_sem.at[1]).wait()
    total = jnp.zeros(queries.shape[1:], jnp.float32)
    steps = 6 + NEAR_LAG + FAR_LAG
    for step in range(steps):
        if step < 8:
            for k in range(4 * step, 4 * step + 4):
                total = total + dot(texts[k], weights[k])
        if step == 8:
            queries[2 * side + core] = total.astype(low)
            for offset in range(1, 4):
                query_copy(queries, query_send, query_recv, offset).start()

            def start(k, carry):
                block = pl.ds(pl.multiple_of(k * 256, 256), 256)
                pltpu.make_async_copy(output_weight.at[:, block], weights.at[k], load_sem.at[1]).start()
                return carry
            lax.fori_loop(0, 32, start, 0)
        next(first)
        if step >= LAG:
            next(second, None)
    next(first, None)

    masks = head_mask[...]
    next(second, None)
    query = dot(normed[...], joint_full[0].reshape(1280, 640)).astype(low)
    qkv[0] = query
    next(second, None)
    key = dot(normed[...], joint_full[1].reshape(1280, 640)).astype(low)
    qkv[1] = key
    next(second, None)
    value = dot(normed[...], joint_full[2].reshape(1280, 640)).astype(low)
    qkv[2] = value
    next(second, None)
    live_key = lax.broadcasted_iota(jnp.int32, (1, rows), 1) < count_ref[0] * PATCH
    live_row = lax.broadcasted_iota(jnp.int32, (rows, 1), 0) < count_ref[0] * PATCH
    head_rows[...] = head_stack(query, masks)
    inner_scores = dot(head_rows[...], key, ((1,), (1,))) * EHD ** (-0.5)
    inner_scores = jnp.where(live_key, inner_scores, NEG)
    shares = jnp.exp(inner_scores - jnp.max(inner_scores, axis=-1, keepdims=True))
    probs_ref[...] = shares / jnp.sum(shares, axis=-1, keepdims=True)
    next(second, None)
    context = head_pick(dot(probs_ref[...].astype(low), qkv[2]), masks).astype(low)
    both = dot(context, pick[...], ((1,), (1,))).astype(low)
    spread[...] = jnp.concatenate([both * half_mask[0:1], both * half_mask[1:2]], axis=0)
    next(second, None)
    branch = dot(spread[...], joint_full[3].reshape(1280, 640))
    branch = jnp.concatenate([branch[:rows], branch[rows:]], axis=1)
    vision = jnp.where(live_row, patches[...].astype(jnp.float32) + branch, 0.0).astype(low)
    next(second, None)

    upstream = jnp.where(live_row, cotangent[...].astype(jnp.float32), 0.0).astype(low)
    sides = jnp.concatenate([upstream[:, :640], upstream[:, 640:]], axis=0)
    backs = dot(sides, joint_full[3].reshape(1280, 640), ((1,), (1,)))
    backs = (backs[:rows] * half_mask[0:1].astype(jnp.float32)
             + backs[rows:] * half_mask[1:2].astype(jnp.float32))
    high = backs.astype(low)
    rest_low = (backs - high.astype(jnp.float32)).astype(low)
    picked = dot(jnp.concatenate([high, rest_low], axis=0), pick[...])
    grad_context = (picked[:rows] + picked[rows:]).astype(low)
    grad_rows[...] = head_stack(grad_context, masks)
    next(second, None)

    def project_kv():
        for part in range(4):
            piece = dot(vision, kv_full[part].reshape(1280, 512)).astype(low)
            for half in range(2):
                kv[2 * part + half, pl.ds(0, rows), :] = piece[:, half * 256:(half + 1) * 256]
        number = jnp.full((KVH, 16, 256), count_ref[0].astype(jnp.float32)).astype(low)
        kv[:, pl.ds(rows, 16), :] = number
        next(exchange)

    if KV_AT == 0:
        for _ in second:
            pass
        project_kv()
    probs = probs_ref[...]
    grad_probs = dot(grad_rows[...], qkv[2], ((1,), (1,)))
    inner = jnp.sum(probs * grad_probs, axis=-1, keepdims=True)
    grad_scores = (probs * (grad_probs - inner) * EHD ** (-0.5)).astype(low)
    next(second, None)
    grad_values = dot(probs.astype(low).T, grad_rows[...]).astype(low)
    grad_keys = dot(grad_scores.T, head_rows[...]).astype(low)
    grad_queries = head_pick(dot(grad_scores, qkv[1]), masks).astype(low)
    if KV_AT == 1:
        for _ in second:
            pass
        project_kv()

    def store(j, left, right):
        for upper in range(2):
            block = dot(left[640 * upper:640 * (upper + 1)], right)
            for k in range(8):
                for other in range(2):
                    at = 80 * k + 40 * other
                    grads[upper, other, j, k] = block[at:at + 40].astype(low)

    store(3, spread[...].T, sides)
    next(reduce)
    normed_t = normed[...].T
    for j, right in enumerate((grad_queries, grad_keys, grad_values)):
        store(j, normed_t, right)
        next(reduce)
        next(second, None)
    next(reduce)
    next(reduce)
    if KV_AT == 2:
        for _ in second:
            pass
        project_kv()

    for offset in range(1, 4):
        query_copy(queries, query_send, query_recv, offset).wait()
    text_rows = queries.shape[1]
    stacked = jnp.concatenate(
        [queries[g, :, half * HD:(half + 1) * HD] for g in range(4) for half in range(2)], axis=0)
    square = (text_rows, text_rows)
    diagonal = (lax.broadcasted_iota(jnp.int32, square, 0) == lax.broadcasted_iota(jnp.int32, square, 1))
    images = jnp.sum(jnp.where(diagonal, mask_ids[...].astype(jnp.float32).reshape(1, text_rows), 0.0),
                     axis=1, keepdims=True)
    images = jnp.concatenate([images] * 8, axis=0)
    tile_of = lax.broadcasted_iota(jnp.int32, (1, rows), 1).astype(jnp.float32)
    top = jnp.full((8 * text_rows, 1), NEG, jnp.float32)
    for i, (step, turn) in enumerate(NEAREST):
        if i == REDUCE_AT:
            next(reduce)
        next(exchange)
        counts = arrived[turn, step, pl.ds(rows, 16), pl.ds(0, 128)][0:1].astype(jnp.float32)
        number = image_at(step, turn).astype(jnp.float32)
        allowed = jnp.logical_and(tile_of < counts * float(PATCH), number < images)
        piece = dot(stacked, arrived[turn, step, pl.ds(0, rows), pl.ds(0, HD)], ((1,), (1,)))
        piece = jnp.where(allowed, piece * HD ** (-0.5), NEG)
        scores[:, i * 128:(i + 1) * 128] = piece
        top = jnp.maximum(top, jnp.max(piece, axis=-1, keepdims=True))
    total = jnp.zeros((8 * text_rows, 1), jnp.float32)
    context = jnp.zeros((8 * text_rows, HD), jnp.float32)
    for i, (step, turn) in enumerate(NEAREST):
        piece = jnp.exp(scores[:, i * 128:(i + 1) * 128] - top)
        total = total + jnp.sum(piece, axis=-1, keepdims=True)
        context = context + dot(piece.astype(low), arrived[turn, step, pl.ds(0, rows), pl.ds(HD, HD)])
    context = context / total
    total = jnp.where(top > 0.5 * NEG, total, 0.0)
    for _ in exchange:
        pass
    scores[:, 0:128] = context
    lane = lax.broadcasted_iota(jnp.int32, (1, 128), 1)
    scores[:, 128:256] = jnp.where(lane < 4, top, total)

    def own_rows(group):
        return pl.ds(pl.multiple_of(group * 2 * text_rows, 256), 2 * text_rows)

    def merge_copy(offset, out, into, send_sem, recv_sem):
        peer = device(x, y, z + (offset // 2) * (1 - 2 * side), lax.rem(core + offset, 2))
        return remote(out.at[offset - 1], into.at[offset - 1], send_sem.at[offset - 1],
                      recv_sem.at[offset - 1], peer)

    def context_copy(offset):
        return merge_copy(offset, part_out, part_in, part_send, part_recv)

    def stat_copy(offset):
        return merge_copy(offset, stat_out, stat_in, stat_send, stat_recv)

    for offset in (2, 3, 1):
        group = 2 * lax.rem(side + offset // 2, 2) + lax.rem(core + offset, 2)
        part_out[offset - 1] = scores[own_rows(group), 0:128].astype(low)
        context_copy(offset).start()
        stat_out[offset - 1] = scores[own_rows(group), 128:256].T[0:8]
        stat_copy(offset).start()
    if REDUCE_AT == 8:
        next(reduce)
    group = 2 * side + core
    parts = [scores[own_rows(group), 0:128]]
    tops = [scores[own_rows(group), 128:129]]
    totals = [scores[own_rows(group), 132:133]]
    for offset in range(1, 4):
        context_copy(offset).wait_recv()
        stat_copy(offset).wait_recv()
        stats = jnp.concatenate([stat_in[offset - 1]] * 16, axis=0).T
        parts.append(part_in[offset - 1].astype(jnp.float32))
        tops.append(stats[:, 0:1])
        totals.append(stats[:, 4:5])
    top = jnp.maximum(jnp.maximum(tops[0], tops[1]), jnp.maximum(tops[2], tops[3]))
    seen = jnp.zeros((2 * text_rows, 1), jnp.float32)
    context = jnp.zeros((2 * text_rows, HD), jnp.float32)
    for k in range(4):
        share = totals[k] * jnp.exp(tops[k] - top)
        seen = seen + share
        context = context + share * parts[k]
    context = (context / jnp.where(seen > 0.0, seen, 1.0)).astype(low)
    context = jnp.concatenate([context[:text_rows], context[text_rows:]], axis=1)
    pltpu.make_async_copy(weights, weights, load_sem.at[1]).wait()

    def project(half):
        for k in range(16):
            block = 2 * k + half
            partial[block] = dot(context, weights[block]).astype(low)

    project(1 - core)
    next(attend)
    project(core)
    next(attend)
    next(reduce)
    next(attend)
    next(reduce)
    next(attend)
    next(reduce)
    for _ in attend:
        pass
    for _ in reduce:
        pass
    for offset in range(1, 4):
        context_copy(offset).wait_send()
        stat_copy(offset).wait_send()
    rows_live = jnp.logical_and(
        seen[:text_rows] > 0.0,
        lax.broadcasted_iota(jnp.int32, (text_rows, 1), 0) < length_ref[0])
    gate = jnp.tanh(jnp.full((1, 256), gate_ref[0], jnp.float32))
    load_text.wait()
    result_out[...] = (text_in[...].astype(jnp.float32)
                       + gate * jnp.where(rows_live, attended[...], 0.0)).astype(low)


def step_peers():
    x, y, z, core = place()
    peers = reduce_peers()
    for step in range(1, 8):
        peers.append(device(x, lax.rem(y + 2, 4), lax.rem(z + step, 8), core))
    peers.append(device(x, y, z + 1 - 2 * lax.rem(z, 2), 1 - core))
    return peers


def whole_step(*operands):
    dma = pltpu.SemaphoreType.DMA
    vmem = pl.BlockSpec(memory_space=pltpu.VMEM)
    smem = pl.BlockSpec(memory_space=pltpu.SMEM)
    low = jnp.bfloat16
    rows = operands[3].shape[0]
    text = operands[13].shape[0]
    return pl.pallas_call(
        step_kernel,
        out_shape=(jax.ShapeDtypeStruct((4, 40, 640), low),
                   jax.ShapeDtypeStruct((text, 256), low)),
        in_specs=[smem] * 3 + [vmem] * 10 + [pl.BlockSpec(memory_space=pl.ANY)] * 3,
        out_specs=[vmem] * 2,
        scratch_shapes=[
            pltpu.VMEM((4, 40, 640), low), pltpu.VMEM((4, 2, 8, 80, 640), low),
            pltpu.VMEM((4, 2, 8, 80, 512), low), pltpu.VMEM((2, 40, 640), low),
            pltpu.VMEM((2, 40, 512), low), pltpu.VMEM((32, text, 256), low),
            pltpu.VMEM((32, 256, 256), low), pltpu.VMEM((KVH, rows + 16, 256), low),
            pltpu.VMEM((4, text, 256), low), pltpu.VMEM((rows, 1280), low),
            pltpu.VMEM((3, rows, 640), low), pltpu.VMEM((EH * rows, rows), jnp.float32),
            pltpu.VMEM((2 * rows, 1280), low), pltpu.VMEM((2, 4, rows + 16, 256), low),
            pltpu.VMEM((8 * text, 8 * 128), jnp.float32), pltpu.VMEM((2, 2, 4, 8, 40, 640), low),
            pltpu.VMEM((EH * rows, 640), low), pltpu.VMEM((EH * rows, 640), low),
            pltpu.VMEM((text, 256), jnp.float32), pltpu.VMEM((text, 256), low),
            pltpu.VMEM((3, 2 * text, HD), low), pltpu.VMEM((3, 2 * text, HD), low),
            pltpu.VMEM((3, 8, 2 * text), jnp.float32), pltpu.VMEM((3, 8, 2 * text), jnp.float32),
            dma((3,)), dma((3,)), dma((3,)), dma((3,)), dma((3,)), dma((3,)), dma((3,)),
        ] + gather_scratch() + exchange_scratch() + reduce_scratch() + attended_scratch(),
        compiler_params=pltpu.CompilerParams(
            collective_id=0, has_side_effects=True, vmem_limit_bytes=63 * 2**20),
        name="whole_step",
    )(*operands)


def result_kernel(sums, result, qkv_out, out_out, result_out):
    for j in range(3):
        qkv_out[:, j * 640:(j + 1) * 640] = sums[j].astype(jnp.float32)
    last = sums[3].astype(jnp.float32)
    out_out[:, 0:640] = last[0:20]
    out_out[:, 640:1280] = last[20:40]
    result_out[...] = result[...]


def write_results(sums, result):
    vmem = pl.BlockSpec(memory_space=pltpu.VMEM)
    return pl.pallas_call(
        result_kernel,
        out_shape=(jax.ShapeDtypeStruct((40, 1920), jnp.float32),
                   jax.ShapeDtypeStruct((20, 1280), jnp.float32),
                   jax.ShapeDtypeStruct(result.shape, result.dtype)),
        in_specs=[vmem] * 2,
        out_specs=[vmem] * 3,
        name="write_results",
    )(sums, result)


def per_device(
    patches,
    cotangent,
    tile_counts,
    ln_gain,
    qkv_weight,
    out_weight,
    text_states,
    mask_ids,
    text_lengths,
    gate_value,
    query_weight,
    kv_weight,
    output_weight,
):
    head_mask, pick, half_mask = tables()
    sums, result = whole_step(
        tile_counts, text_lengths, gate_value, patches, cotangent, ln_gain, qkv_weight, out_weight,
        kv_weight, mask_ids, head_mask, pick, half_mask, text_states,
        query_weight.reshape(32, 256, 256), output_weight)
    return write_results(sums, result)


def solution(mesh):
    placed = (
        P(("dp", "fsdp"), None),
        P(("dp", "fsdp"), None),
        P(("dp", "fsdp")),
        P(),
        P("fsdp", None),
        P("fsdp", None),
        P("dp", None),
        P("dp"),
        P("dp"),
        P(),
        P(None, "fsdp"),
        P("fsdp", None),
        P("fsdp", None),
    )
    return jax.shard_map(
        per_device,
        mesh=mesh,
        in_specs=placed,
        out_specs=(P("fsdp", None), P("fsdp", None), P("dp", "fsdp")),
        check_vma=False,
    )
```
